32 devices in a mesh: space: 16 (over z, y, core), orb: 2 (over x).
Axes of the slice: x: 2, y: 2, z: 4, core: 2. Of those that a mesh axis runs over, the one named last changes fastest.
Arguments:
- hamiltonian: bfloat16 [128, 7, 256, 256], P('space'), may hold values from -0.125 to 0.125
- orbitals: bfloat16 [256, 32768], P('orb', 'space'), may hold values from -6 to 6
- adjacency: int32 [128, 6], P('space'), may hold values from 0 to 127, as said below
Outputs:
- basis: float32 [256, 32768], P('orb', 'space')
- factor: float32 [256, 256], replicated
The draws below stay inside these ranges and needn't reach their ends.
Inputs may be any that keep to these rules, and one draw needn't show every extreme that they name: `adjacency`: with elements in blocks of 8 (block b holds elements b * 8 to b * 8 + 7), face 0 of an element in block b lies in block b - 1 and face 1 in block b + 1 (both modulo the number of blocks), faces 2 to 5 in block b; for each face, the elements of a block name every element of the target block exactly once.
All inputs are finite; a program needn't handle non-finite values.
Results may differ from the reference program's by a relative error of at most 0.0041.
Values may be sent and summed in bfloat16 or wider, within the bound.
No kernel may reach another device: no remote copies, remote signals or barrier semaphores. Data moves between devices by JAX's collectives and lax.ppermute only.
A program may use at most 64 MiB of HBM per device.

```python
import jax
import jax.numpy as jnp
from jax import lax

NB = 256
NORB = 256
ELEM_DEV = 8
ELEMENTS = 128
ROWS = 32768


def draw_adjacency(key, part):
    groups = ELEMENTS // ELEM_DEV
    keys = jax.random.split(jax.random.fold_in(key, 17), groups * 6)
    perms = jax.vmap(lambda k: jax.random.permutation(k, ELEM_DEV))(keys).reshape(groups, 6, ELEM_DEV)
    owner = jnp.arange(groups, dtype=jnp.int32)[:, None]
    offset = jnp.array([-1, 1, 0, 0, 0, 0], dtype=jnp.int32)
    target = (owner + offset[None, :]) % groups
    ident = target[:, :, None] * ELEM_DEV + perms.astype(jnp.int32)
    return ident.transpose(0, 2, 1).reshape(ELEMENTS, 6).astype(jnp.int32)


def shard_levels(stream_key, extent, pieces, least, high):
    level = 1.0
    for position, parts in pieces:
        draws = jax.random.uniform(jax.random.fold_in(jax.random.fold_in(stream_key, 6), position), (parts,), jnp.float32, least / len(pieces), high / len(pieces))
        level = level * jnp.repeat(jnp.exp(draws), extent[position] // parts).reshape((-1,) + (1,) * (len(extent) - 1 - position))
    return level


def bell_draw(rng, extent, width, most, pieces=(), kind=jnp.bfloat16):
    entries = width * jax.random.normal(rng, extent, jnp.float32)
    if pieces:
        entries = entries * shard_levels(rng, extent, pieces, -0.22, 0.18)
    return jnp.clip(entries, -most, most).astype(kind)


def setup_inputs(seed: int = 0) -> dict:
    arg_keys = jax.random.split(jax.random.key(seed), 4)
    return {
        "hamiltonian": bell_draw(arg_keys[0], (ELEMENTS, 7, NB, NB), (7 * NB) ** -0.5, 0.125, ((0, 16),)),
        "orbitals": bell_draw(arg_keys[1], (NORB, ROWS), 1.0, 6.0, ((0, 2), (1, 16))),
        "adjacency": draw_adjacency(jax.random.fold_in(arg_keys[3], 71), 0),
    }


centre = 0.25
radius = 0.75

def apply_ham(hamiltonian, adjacency, vec):
    blocks = vec.reshape(NORB, ELEMENTS, NB).astype(jnp.float32)
    result = jnp.einsum('oej,eij->oei', blocks, hamiltonian[:, 0].astype(jnp.float32))
    for face in range(6):
        near = jnp.take(blocks, adjacency[:, face], axis=1)
        result = result + jnp.einsum('oej,eij->oei', near, hamiltonian[:, face + 1].astype(jnp.float32))
    return result.reshape(NORB, ROWS)

def reference(hamiltonian, orbitals, adjacency):
    level_zero = orbitals.astype(jnp.float32)
    level_one = ((apply_ham(hamiltonian, adjacency, orbitals) - centre * level_zero) / radius).astype(jnp.bfloat16)
    one_wide = level_one.astype(jnp.float32)
    level_two = (2.0 * (apply_ham(hamiltonian, adjacency, level_one) - centre * one_wide) / radius - level_zero).astype(jnp.bfloat16)
    two_wide = level_two.astype(jnp.float32)
    filtered = 2.0 * (apply_ham(hamiltonian, adjacency, level_two) - centre * two_wide) / radius - one_wide
    gram = jnp.dot(filtered, filtered.T, precision=lax.Precision.HIGHEST)
    lower = jnp.linalg.cholesky(gram)
    basis = lax.linalg.triangular_solve(lower, filtered, left_side=True, lower=True)
    return (basis, lower.T)
```

```python
import functools

import jax
import jax.numpy as jnp
from jax import lax
from jax.experimental import pallas as pl
from jax.experimental.pallas import tpu as pltpu
from jax.sharding import PartitionSpec as P

centre = 0.25
radius = 0.75
SUB = 8


def vmem(count):
    return [pl.BlockSpec(memory_space=pltpu.VMEM)] * count


def dot_nt(a, b):
    return lax.dot_general(a, b, (((1,), (1,)), ((), ())), preferred_element_type=jnp.float32)


def dot_full(a, b, dims=((1,), (0,))):
    return lax.dot_general(
        a, b, (dims, ((), ())), precision=lax.Precision.HIGHEST, preferred_element_type=jnp.float32
    )


def split(a):
    high = a.astype(jnp.bfloat16)
    return high, (a - high.astype(jnp.float32)).astype(jnp.bfloat16)


def own_kernel(loc_ref, vec_ref, ham_ref, out_ref, buf, sems):
    count, _, width, _ = ham_ref.shape
    copies = []
    for e in range(count):
        copies.append(
            (
                pltpu.make_async_copy(ham_ref.at[e, 0:1], buf.at[e, 0:1], sems.at[e, 0]),
                pltpu.make_async_copy(ham_ref.at[e, 3:7], buf.at[e, 1:5], sems.at[e, 1]),
            )
        )
        for copy in copies[-1]:
            copy.start()
    for e in range(count):
        for copy in copies[e]:
            copy.wait()
        total = dot_nt(vec_ref[:, e * width : (e + 1) * width], buf[e, 0])
        for face in range(2, 6):
            start = pl.multiple_of(loc_ref[e, face] * width, width)
            total += dot_nt(vec_ref[:, pl.ds(start, width)], buf[e, face - 1])
        out_ref[:, e * width : (e + 1) * width] = total


def own_part(vec, hamiltonian, loc):
    count, _, width, _ = hamiltonian.shape
    owned = vec.shape[0]
    return pl.pallas_call(
        own_kernel,
        out_shape=jax.ShapeDtypeStruct(vec.shape, jnp.float32),
        in_specs=[pl.BlockSpec(memory_space=pltpu.SMEM)]
        + vmem(1)
        + [pl.BlockSpec(memory_space=pl.ANY)],
        out_specs=pl.BlockSpec(memory_space=pltpu.VMEM),
        scratch_shapes=[
            pltpu.VMEM((count, 5, width, width), jnp.bfloat16),
            pltpu.SemaphoreType.DMA((count, 2)),
        ],
        compiler_params=pltpu.CompilerParams(vmem_limit_bytes=24 << 20),
        cost_estimate=pl.CostEstimate(
            flops=2 * owned * count * width * width * 5,
            bytes_accessed=count * 5 * width * width * 2,
            transcendentals=0,
        ),
    )(loc, vec, hamiltonian)


def halo_kernel(level, loc_ref, low_ref, high_ref, acc_ref, vec_ref, prior_ref, ham_ref, *rest):
    outs, (buf, sems) = rest[:-2], rest[-2:]
    count, _, width, _ = ham_ref.shape
    copies = []
    for e in range(count):
        copies.append(pltpu.make_async_copy(ham_ref.at[e, 1:3], buf.at[e], sems.at[e]))
        copies[-1].start()
    for e in range(count):
        copies[e].wait()
        here = slice(e * width, (e + 1) * width)
        total = acc_ref[:, here]
        for face, ref in enumerate((low_ref, high_ref)):
            start = pl.multiple_of(loc_ref[e, face] * width, width)
            total += dot_nt(ref[:, pl.ds(start, width)], buf[e, face])
        shifted = (total - centre * vec_ref[:, here].astype(jnp.float32)) * (1.0 / radius)
        if level > 1:
            shifted = 2.0 * shifted - prior_ref[:, here].astype(jnp.float32)
        for out in outs:
            out[:, here] = shifted.astype(out.dtype)


def halo_part(level, low, high, acc, vec, prior, hamiltonian, loc):
    count, _, width, _ = hamiltonian.shape
    owned = vec.shape[0]
    kinds = [jnp.bfloat16] if level < 3 else [jnp.float32, jnp.bfloat16]
    out = pl.pallas_call(
        functools.partial(halo_kernel, level),
        out_shape=[jax.ShapeDtypeStruct(vec.shape, kind) for kind in kinds],
        in_specs=[pl.BlockSpec(memory_space=pltpu.SMEM)]
        + vmem(5)
        + [pl.BlockSpec(memory_space=pl.ANY)],
        out_specs=vmem(len(kinds)),
        scratch_shapes=[
            pltpu.VMEM((count, 2, width, width), jnp.bfloat16),
            pltpu.SemaphoreType.DMA((count,)),
        ],
        compiler_params=pltpu.CompilerParams(vmem_limit_bytes=24 << 20),
        cost_estimate=pl.CostEstimate(
            flops=2 * owned * count * width * width * 2,
            bytes_accessed=count * 2 * width * width * 2,
            transcendentals=0,
        ),
    )(loc, low, high, acc, vec, prior, hamiltonian)
    return out


def gram_kernel(place_ref, own_ref, other_ref, out_ref):
    def fill(first, second):
        out_ref[0] = dot_nt(first[...], first[...])
        out_ref[1] = dot_nt(first[...], second[...])
        out_ref[2] = dot_nt(second[...], second[...])

    @pl.when(place_ref[0] == 0)
    def _():
        fill(own_ref, other_ref)

    @pl.when(place_ref[0] != 0)
    def _():
        fill(other_ref, own_ref)


def factor_block(rows, right):
    strips = len(rows)
    shape = rows[0].shape
    sub = lax.broadcasted_iota(jnp.int32, shape, 0)
    upper, inverse = [], []
    for k in range(strips):
        strip, beside = rows[k], right[k]
        lanes = [jnp.broadcast_to(strip[:, k * SUB + j : k * SUB + j + 1], shape) for j in range(SUB)]
        entry = [
            [jnp.broadcast_to(lanes[j][i : i + 1, :], shape) if j <= i else None for j in range(SUB)]
            for i in range(SUB)
        ]
        low = [[None] * SUB for _ in range(SUB)]
        root = []
        for j in range(SUB):
            root.append(lax.rsqrt(entry[j][j]))
            for i in range(j + 1, SUB):
                low[i][j] = entry[i][j] * root[j]
            for i in range(j + 1, SUB):
                for t in range(j + 1, i + 1):
                    entry[i][t] = entry[i][t] - low[i][j] * low[t][j]
        inv = [[None] * SUB for _ in range(SUB)]
        for i in range(SUB):
            inv[i][i] = root[i]
            for j in range(i):
                total = low[i][j] * inv[j][j]
                for t in range(j + 1, i):
                    total = total + low[i][t] * inv[t][j]
                inv[i][j] = -root[i] * total

        def solve(source):
            wide = [jnp.broadcast_to(source[i : i + 1, :], shape) for i in range(SUB)]
            solved = []
            for i in range(SUB):
                total = inv[i][0] * wide[0]
                for j in range(1, i + 1):
                    total = total + inv[i][j] * wide[j]
                solved.append(total)
            back = []
            for i in range(SUB):
                total = inv[i][i] * solved[i]
                for j in range(i + 1, SUB):
                    total = total + inv[j][i] * solved[j]
                back.append(total)
            packed = solved[0]
            for i in range(1, SUB):
                packed = jnp.where(sub == i, solved[i], packed)
            return packed, back

        row_packed, row_back = solve(strip)
        inv_packed, inv_back = solve(beside)
        upper.append(row_packed)
        inverse.append(inv_packed)
        for r in range(k + 1, strips):
            for i in range(SUB):
                column = jnp.broadcast_to(rows[r][:, k * SUB + i : k * SUB + i + 1], shape)
                rows_r = row_back[i] * column
                right_r = inv_back[i] * column
                total = rows_r if i == 0 else total + rows_r
                beyond = right_r if i == 0 else beyond + right_r
            rows[r] = rows[r] - total
            right[r] = right[r] - beyond
    return upper, inverse


def factor_kernel(gram_ref, upper_ref, inv_ref, work, right):
    half = gram_ref.shape[1]
    strips = half // SUB
    row = lax.broadcasted_iota(jnp.int32, (half, half), 0)
    col = lax.broadcasted_iota(jnp.int32, (half, half), 1)

    def one(at):
        rows = [work[SUB * s : SUB * (s + 1), :] for s in range(strips)]
        eye = (row == col).astype(jnp.float32)
        beside = [eye[SUB * s : SUB * (s + 1), :] for s in range(strips)]
        upper, inverse = factor_block(rows, beside)
        for s in range(strips):
            work[SUB * s : SUB * (s + 1), :] = upper[s]
            right[SUB * s : SUB * (s + 1), :] = inverse[s]
        here = pl.ds(pl.multiple_of(at * half, half), half)
        upper_ref[here, here] = jnp.where(col >= row, work[...], 0.0)
        inv_ref[here, here] = jnp.where(col <= row, right[...], 0.0)

    work[...] = gram_ref[0]
    zero = jnp.zeros((half, half), jnp.float32)

    def body(at, carry):
        one(at)

        @pl.when(at == 0)
        def _():
            across = dot_full(inv_ref[0:half, 0:half], gram_ref[1])
            upper_ref[0:half, half:] = across
            work[...] = gram_ref[2] - dot_full(across, across, ((0,), (0,)))

        return carry

    lax.fori_loop(0, 2, body, 0)
    upper_ref[half:, 0:half] = zero
    inv_ref[0:half, half:] = zero
    between = dot_full(upper_ref[0:half, half:], inv_ref[0:half, 0:half], ((0,), (0,)))
    inv_ref[half:, 0:half] = -dot_full(inv_ref[half:, half:], between)


def factorize(gram):
    half = gram.shape[1]
    return pl.pallas_call(
        factor_kernel,
        out_shape=[jax.ShapeDtypeStruct((2 * half, 2 * half), jnp.float32)] * 2,
        in_specs=vmem(1),
        out_specs=vmem(2),
        scratch_shapes=[pltpu.VMEM((half, half), jnp.float32)] * 2,
        compiler_params=pltpu.CompilerParams(vmem_limit_bytes=24 << 20),
    )(gram)


def basis_kernel(place_ref, inv_ref, own_ref, other_ref, out_ref):
    half = own_ref.shape[0]
    place = place_ref[0]
    rows = pl.ds(pl.multiple_of(place * half, half), half)
    away = pl.ds(pl.multiple_of((1 - place) * half, half), half)
    near_high, near_low = split(inv_ref[rows, rows])
    far_high, far_low = split(inv_ref[rows, away])
    total = own_ref.shape[1]
    step = 512 if total % 512 == 0 else total
    for at in range(0, total, step):
        high, low = split(own_ref[:, at : at + step])
        other = other_ref[:, at : at + step]
        out_ref[:, at : at + step] = (
            jnp.dot(near_high, high, preferred_element_type=jnp.float32)
            + jnp.dot(near_high, low, preferred_element_type=jnp.float32)
            + jnp.dot(near_low, high, preferred_element_type=jnp.float32)
            + jnp.dot(far_high, other, preferred_element_type=jnp.float32)
            + jnp.dot(far_low, other, preferred_element_type=jnp.float32)
        )


def shards(hamiltonian, orbitals, adjacency):
    count = hamiltonian.shape[0]
    owned = orbitals.shape[0]
    blocks = lax.axis_size("space")
    groups = lax.axis_size("orb")
    half = owned * groups // 2
    loc = adjacency % count
    forward = [(i, (i + 1) % blocks) for i in range(blocks)]
    backward = [(target, source) for source, target in forward]

    def apply_level(level, vec, prior):
        low = lax.ppermute(vec, "space", forward)
        high = lax.ppermute(vec, "space", backward)
        acc = own_part(vec, hamiltonian, loc)
        return halo_part(level, low, high, acc, vec, prior, hamiltonian, loc)

    (level_one,) = apply_level(1, orbitals, orbitals)
    (level_two,) = apply_level(2, level_one, orbitals)
    filtered, narrow = apply_level(3, level_two, level_one)

    place = lax.axis_index("orb").astype(jnp.int32).reshape(1)
    if groups == 2:
        other = lax.ppermute(narrow, "orb", [(0, 1), (1, 0)])
        gram = pl.pallas_call(
            gram_kernel,
            out_shape=jax.ShapeDtypeStruct((3, half, half), jnp.float32),
            in_specs=[pl.BlockSpec(memory_space=pltpu.SMEM)] + vmem(2),
            out_specs=pl.BlockSpec(memory_space=pltpu.VMEM),
            compiler_params=pltpu.CompilerParams(vmem_limit_bytes=24 << 20),
        )(place, narrow, other)
    else:
        columns = lax.all_gather(narrow, "orb", axis=0, tiled=True)
        whole = dot_nt(columns, columns)
        gram = jnp.stack([whole[:half, :half], whole[:half, half:], whole[half:, half:]])
    step = 1
    while step < blocks:
        gram = gram + lax.ppermute(gram, "space", [(i, i ^ step) for i in range(blocks)])
        step *= 2
    upper, inverse = factorize(gram)
    if groups == 2:
        basis = pl.pallas_call(
            basis_kernel,
            out_shape=jax.ShapeDtypeStruct(filtered.shape, jnp.float32),
            in_specs=[pl.BlockSpec(memory_space=pltpu.SMEM)] + vmem(3),
            out_specs=pl.BlockSpec(memory_space=pltpu.VMEM),
            compiler_params=pltpu.CompilerParams(vmem_limit_bytes=24 << 20),
        )(place, inverse, filtered, other)
    else:
        mine = lax.dynamic_slice_in_dim(inverse, place[0] * owned, owned, 0)
        near = lax.dynamic_slice_in_dim(mine, place[0] * owned, owned, 1)
        rest = filtered - narrow.astype(jnp.float32)
        basis = dot_full(mine, columns.astype(jnp.float32)) + dot_full(near, rest)
    return (basis, upper)


def solution(mesh):
    in_specs = (P("space", None, None, None), P("orb", "space"), P("space", None))
    out_specs = (P("orb", "space"), P())
    return jax.shard_map(shards, mesh=mesh, in_specs=in_specs, out_specs=out_specs, check_vma=False)
```

```python
import functools

import jax
import jax.numpy as jnp
from jax import lax
from jax.experimental import pallas as pl
from jax.experimental.pallas import tpu as pltpu
from jax.sharding import PartitionSpec as P

centre = 0.25
radius = 0.75
SUB = 8


def vmem(count):
    return [pl.BlockSpec(memory_space=pltpu.VMEM)] * count


def dot_nt(a, b):
    return lax.dot_general(a, b, (((1,), (1,)), ((), ())), preferred_element_type=jnp.float32)


def dot_full(a, b, dims=((1,), (0,))):
    return lax.dot_general(
        a, b, (dims, ((), ())), precision=lax.Precision.HIGHEST, preferred_element_type=jnp.float32
    )


def split(a):
    high = a.astype(jnp.bfloat16)
    return high, (a - high.astype(jnp.float32)).astype(jnp.bfloat16)


def turn_kernel(loc_ref, vec_ref, ham_ref, turned_ref, *outs):
    count, faces, width, _ = ham_ref.shape
    rows = outs[0].shape[0]
    for e in range(count):
        here = slice(e * width, (e + 1) * width)
        total = None
        for face in range(faces):
            turned = ham_ref[e, face].T
            turned_ref[e, face] = turned
            if face == 1 or face == 2:
                continue
            at = here if face == 0 else pl.ds(pl.multiple_of(loc_ref[e, face - 1] * width, width), width)
            part = jnp.dot(vec_ref[:, at], turned, preferred_element_type=jnp.float32)
            total = part if total is None else total + part
        for piece, out in enumerate(outs):
            out[:, here] = total[piece * rows : (piece + 1) * rows]


def turn_part(vec, hamiltonian, loc, chunks):
    count, faces, width, _ = hamiltonian.shape
    owned = vec.shape[0]
    share = jax.ShapeDtypeStruct((owned // chunks, vec.shape[1]), jnp.float32)
    return pl.pallas_call(
        turn_kernel,
        out_shape=[jax.ShapeDtypeStruct(hamiltonian.shape, hamiltonian.dtype)] + [share] * chunks,
        in_specs=[pl.BlockSpec(memory_space=pltpu.SMEM)] + vmem(2),
        out_specs=vmem(1 + chunks),
        compiler_params=pltpu.CompilerParams(vmem_limit_bytes=32 << 20),
        cost_estimate=pl.CostEstimate(
            flops=2 * owned * count * width * width * 5,
            bytes_accessed=count * faces * width * width * 4,
            transcendentals=0,
        ),
    )(loc, vec, hamiltonian)


def own_kernel(loc_ref, vec_ref, turned_ref, out_ref):
    count, _, width, _ = turned_ref.shape
    for e in range(count):
        here = slice(e * width, (e + 1) * width)
        total = jnp.dot(vec_ref[:, here], turned_ref[e, 0], preferred_element_type=jnp.float32)
        for face in range(2, 6):
            at = pl.ds(pl.multiple_of(loc_ref[e, face] * width, width), width)
            total += jnp.dot(
                vec_ref[:, at], turned_ref[e, face + 1], preferred_element_type=jnp.float32
            )
        out_ref[:, here] = total


def own_part(vec, turned, loc):
    count, _, width, _ = turned.shape
    owned = vec.shape[0]
    return pl.pallas_call(
        own_kernel,
        out_shape=jax.ShapeDtypeStruct(vec.shape, jnp.float32),
        in_specs=[pl.BlockSpec(memory_space=pltpu.SMEM)] + vmem(2),
        out_specs=pl.BlockSpec(memory_space=pltpu.VMEM),
        compiler_params=pltpu.CompilerParams(vmem_limit_bytes=24 << 20),
        cost_estimate=pl.CostEstimate(
            flops=2 * owned * count * width * width * 5,
            bytes_accessed=count * 5 * width * width * 2,
            transcendentals=0,
        ),
    )(loc, vec, turned)


def halo_kernel(level, loc_ref, low_ref, high_ref, acc_ref, vec_ref, prior_ref, turned_ref, *outs):
    count, _, width, _ = turned_ref.shape
    for e in range(count):
        here = slice(e * width, (e + 1) * width)
        total = acc_ref[:, here]
        for face, ref in enumerate((low_ref, high_ref)):
            at = pl.ds(pl.multiple_of(loc_ref[e, face] * width, width), width)
            total += jnp.dot(
                ref[:, at], turned_ref[e, face + 1], preferred_element_type=jnp.float32
            )
        shifted = (total - centre * vec_ref[:, here].astype(jnp.float32)) * (1.0 / radius)
        if level > 1:
            shifted = 2.0 * shifted - prior_ref[:, here].astype(jnp.float32)
        for out in outs:
            out[:, here] = shifted.astype(out.dtype)


def halo_part(level, low, high, acc, vec, prior, turned, loc):
    count, _, width, _ = turned.shape
    owned = vec.shape[0]
    kinds = [jnp.bfloat16] if level < 3 else [jnp.float32, jnp.bfloat16]
    return pl.pallas_call(
        functools.partial(halo_kernel, level),
        out_shape=[jax.ShapeDtypeStruct(vec.shape, kind) for kind in kinds],
        in_specs=[pl.BlockSpec(memory_space=pltpu.SMEM)] + vmem(6),
        out_specs=vmem(len(kinds)),
        compiler_params=pltpu.CompilerParams(vmem_limit_bytes=24 << 20),
        cost_estimate=pl.CostEstimate(
            flops=2 * owned * count * width * width * 2,
            bytes_accessed=count * 2 * width * width * 2,
            transcendentals=0,
        ),
    )(loc, low, high, acc, vec, prior, turned)


def gram_kernel(chunks, place_ref, *refs):
    own_refs, other_refs, out_ref, columns = refs[:chunks], refs[chunks:-2], refs[-2], refs[-1]
    share = own_refs[0].shape[0]
    half = share * chunks

    def fill(first, second):
        for piece in range(chunks):
            columns[piece * share : (piece + 1) * share, :] = first[piece][...]
            columns[half + piece * share : half + (piece + 1) * share, :] = second[piece][...]

    @pl.when(place_ref[0] == 0)
    def _():
        fill(own_refs, other_refs)

    @pl.when(place_ref[0] != 0)
    def _():
        fill(other_refs, own_refs)

    out_ref[0] = dot_nt(columns[:half, :], columns[:half, :])
    out_ref[1] = dot_nt(columns[:half, :], columns[half:, :])
    out_ref[2] = dot_nt(columns[half:, :], columns[half:, :])


def factor_block(rows, right):
    strips = len(rows)
    shape = rows[0].shape
    sub = lax.broadcasted_iota(jnp.int32, shape, 0)
    upper, inverse = [], []
    for k in range(strips):
        strip, beside = rows[k], right[k]
        lanes = [jnp.broadcast_to(strip[:, k * SUB + j : k * SUB + j + 1], shape) for j in range(SUB)]
        entry = [
            [jnp.broadcast_to(lanes[j][i : i + 1, :], shape) if j <= i else None for j in range(SUB)]
            for i in range(SUB)
        ]
        low = [[None] * SUB for _ in range(SUB)]
        root = []
        for j in range(SUB):
            root.append(lax.rsqrt(entry[j][j]))
            for i in range(j + 1, SUB):
                low[i][j] = entry[i][j] * root[j]
            for i in range(j + 1, SUB):
                for t in range(j + 1, i + 1):
                    entry[i][t] = entry[i][t] - low[i][j] * low[t][j]
        inv = [[None] * SUB for _ in range(SUB)]
        for i in range(SUB):
            inv[i][i] = root[i]
            for j in range(i):
                total = low[i][j] * inv[j][j]
                for t in range(j + 1, i):
                    total = total + low[i][t] * inv[t][j]
                inv[i][j] = -root[i] * total

        def solve(source):
            wide = [jnp.broadcast_to(source[i : i + 1, :], shape) for i in range(SUB)]
            solved = []
            for i in range(SUB):
                total = inv[i][0] * wide[0]
                for j in range(1, i + 1):
                    total = total + inv[i][j] * wide[j]
                solved.append(total)
            back = []
            for i in range(SUB):
                total = inv[i][i] * solved[i]
                for j in range(i + 1, SUB):
                    total = total + inv[j][i] * solved[j]
                back.append(total)
            packed = solved[0]
            for i in range(1, SUB):
                packed = jnp.where(sub == i, solved[i], packed)
            return packed, back

        row_packed, row_back = solve(strip)
        inv_packed, inv_back = solve(beside)
        upper.append(row_packed)
        inverse.append(inv_packed)
        for r in range(k + 1, strips):
            for i in range(SUB):
                column = jnp.broadcast_to(rows[r][:, k * SUB + i : k * SUB + i + 1], shape)
                rows_r = row_back[i] * column
                right_r = inv_back[i] * column
                total = rows_r if i == 0 else total + rows_r
                beyond = right_r if i == 0 else beyond + right_r
            rows[r] = rows[r] - total
            right[r] = right[r] - beyond
    return upper, inverse


def factor_kernel(gram_ref, upper_ref, inv_ref, work, right):
    half = gram_ref.shape[1]
    strips = half // SUB
    row = lax.broadcasted_iota(jnp.int32, (half, half), 0)
    col = lax.broadcasted_iota(jnp.int32, (half, half), 1)

    def one(at):
        rows = [work[SUB * s : SUB * (s + 1), :] for s in range(strips)]
        eye = (row == col).astype(jnp.float32)
        beside = [eye[SUB * s : SUB * (s + 1), :] for s in range(strips)]
        upper, inverse = factor_block(rows, beside)
        for s in range(strips):
            work[SUB * s : SUB * (s + 1), :] = upper[s]
            right[SUB * s : SUB * (s + 1), :] = inverse[s]
        here = pl.ds(pl.multiple_of(at * half, half), half)
        upper_ref[here, here] = jnp.where(col >= row, work[...], 0.0)
        inv_ref[here, here] = jnp.where(col <= row, right[...], 0.0)

    work[...] = gram_ref[0]
    zero = jnp.zeros((half, half), jnp.float32)

    def body(at, carry):
        one(at)

        @pl.when(at == 0)
        def _():
            across = dot_full(inv_ref[0:half, 0:half], gram_ref[1])
            upper_ref[0:half, half:] = across
            work[...] = gram_ref[2] - dot_full(across, across, ((0,), (0,)))

        return carry

    lax.fori_loop(0, 2, body, 0)
    upper_ref[half:, 0:half] = zero
    inv_ref[0:half, half:] = zero
    between = dot_full(upper_ref[0:half, half:], inv_ref[0:half, 0:half], ((0,), (0,)))
    inv_ref[half:, 0:half] = -dot_full(inv_ref[half:, half:], between)


def factorize(gram):
    half = gram.shape[1]
    return pl.pallas_call(
        factor_kernel,
        out_shape=[jax.ShapeDtypeStruct((2 * half, 2 * half), jnp.float32)] * 2,
        in_specs=vmem(1),
        out_specs=vmem(2),
        scratch_shapes=[pltpu.VMEM((half, half), jnp.float32)] * 2,
        compiler_params=pltpu.CompilerParams(vmem_limit_bytes=24 << 20),
    )(gram)


def basis_kernel(chunks, place_ref, inv_ref, *refs):
    own_refs, other_refs, out_ref = refs[:chunks], refs[chunks:-1], refs[-1]
    half, total = out_ref.shape
    place = place_ref[0]
    rows = pl.ds(pl.multiple_of(place * half, half), half)
    away = pl.ds(pl.multiple_of((1 - place) * half, half), half)
    near_high, near_low = split(inv_ref[rows, rows])
    far_high, far_low = split(inv_ref[rows, away])
    step = 512 if total % 512 == 0 else total
    for at in range(0, total, step):
        here = slice(at, at + step)
        high, low = split(jnp.concatenate([ref[:, here] for ref in own_refs], axis=0))
        other = jnp.concatenate([ref[:, here] for ref in other_refs], axis=0)
        out_ref[:, here] = (
            jnp.dot(near_high, high, preferred_element_type=jnp.float32)
            + jnp.dot(near_high, low, preferred_element_type=jnp.float32)
            + jnp.dot(near_low, high, preferred_element_type=jnp.float32)
            + jnp.dot(far_high, other, preferred_element_type=jnp.float32)
            + jnp.dot(far_low, other, preferred_element_type=jnp.float32)
        )


def shards(hamiltonian, orbitals, adjacency):
    count = hamiltonian.shape[0]
    owned = orbitals.shape[0]
    blocks = lax.axis_size("space")
    groups = lax.axis_size("orb")
    half = owned * groups // 2
    chunks = 2
    share = owned // chunks
    loc = adjacency % count
    forward = [(i, (i + 1) % blocks) for i in range(blocks)]
    backward = [(target, source) for source, target in forward]
    smem = [pl.BlockSpec(memory_space=pltpu.SMEM)]

    def halo(vec):
        return lax.ppermute(vec, "space", forward), lax.ppermute(vec, "space", backward)

    zero = [orbitals[piece * share : (piece + 1) * share] for piece in range(chunks)]
    sides = [halo(vec) for vec in zero]
    turned, *accs = turn_part(orbitals, hamiltonian, loc, chunks)
    one, two, filtered, narrow = [], [], [], []
    for piece in range(chunks):
        one += halo_part(1, *sides[piece], accs[piece], zero[piece], zero[piece], turned, loc)
    for piece in range(chunks):
        side = halo(one[piece])
        acc = own_part(one[piece], turned, loc)
        two += halo_part(2, *side, acc, one[piece], zero[piece], turned, loc)
    for piece in range(chunks):
        side = halo(two[piece])
        acc = own_part(two[piece], turned, loc)
        wide, short = halo_part(3, *side, acc, two[piece], one[piece], turned, loc)
        filtered.append(wide)
        narrow.append(short)

    place = lax.axis_index("orb").astype(jnp.int32).reshape(1)
    if groups == 2:
        other = [lax.ppermute(piece, "orb", [(0, 1), (1, 0)]) for piece in narrow]
        gram = pl.pallas_call(
            functools.partial(gram_kernel, chunks),
            out_shape=jax.ShapeDtypeStruct((3, half, half), jnp.float32),
            in_specs=smem + vmem(2 * chunks),
            out_specs=pl.BlockSpec(memory_space=pltpu.VMEM),
            scratch_shapes=[pltpu.VMEM((2 * half, orbitals.shape[1]), jnp.bfloat16)],
            compiler_params=pltpu.CompilerParams(vmem_limit_bytes=24 << 20),
        )(place, *narrow, *other)
    else:
        columns = lax.all_gather(jnp.concatenate(narrow), "orb", axis=0, tiled=True)
        whole = dot_nt(columns, columns)
        gram = jnp.stack([whole[:half, :half], whole[:half, half:], whole[half:, half:]])
    step = 1
    while step < blocks:
        gram = gram + lax.ppermute(gram, "space", [(i, i ^ step) for i in range(blocks)])
        step *= 2
    upper, inverse = factorize(gram)
    if groups == 2:
        basis = pl.pallas_call(
            functools.partial(basis_kernel, chunks),
            out_shape=jax.ShapeDtypeStruct(orbitals.shape, jnp.float32),
            in_specs=smem + vmem(1 + 2 * chunks),
            out_specs=pl.BlockSpec(memory_space=pltpu.VMEM),
            compiler_params=pltpu.CompilerParams(vmem_limit_bytes=24 << 20),
        )(place, inverse, *filtered, *other)
    else:
        mine = lax.dynamic_slice_in_dim(inverse, place[0] * owned, owned, 0)
        near = lax.dynamic_slice_in_dim(mine, place[0] * owned, owned, 1)
        rest = jnp.concatenate(filtered) - jnp.concatenate(narrow).astype(jnp.float32)
        basis = dot_full(mine, columns.astype(jnp.float32)) + dot_full(near, rest)
    return (basis, upper)


def solution(mesh):
    in_specs = (P("space", None, None, None), P("orb", "space"), P("space", None))
    out_specs = (P("orb", "space"), P())
    return jax.shard_map(shards, mesh=mesh, in_specs=in_specs, out_specs=out_specs, check_vma=False)
```

```python
import functools

import jax
import jax.numpy as jnp
from jax import lax
from jax.experimental import pallas as pl
from jax.experimental.pallas import tpu as pltpu
from jax.sharding import PartitionSpec as P

centre = 0.25
radius = 0.75
SUB = 8


def vmem(count):
    return [pl.BlockSpec(memory_space=pltpu.VMEM)] * count


def dot_nt(a, b):
    return lax.dot_general(a, b, (((1,), (1,)), ((), ())), preferred_element_type=jnp.float32)


def dot_full(a, b, dims=((1,), (0,))):
    return lax.dot_general(
        a, b, (dims, ((), ())), precision=lax.Precision.HIGHEST, preferred_element_type=jnp.float32
    )


def split(a):
    high = a.astype(jnp.bfloat16)
    return high, (a - high.astype(jnp.float32)).astype(jnp.bfloat16)


def turn_kernel(loc_ref, vec_ref, ham_ref, turned_ref, out_ref):
    count, faces, width, _ = ham_ref.shape
    for e in range(count):
        here = slice(e * width, (e + 1) * width)
        total = None
        for face in range(faces):
            turned = ham_ref[e, face].T
            turned_ref[e, face] = turned
            if face == 1 or face == 2:
                continue
            at = here if face == 0 else pl.ds(pl.multiple_of(loc_ref[e, face - 1] * width, width), width)
            part = jnp.dot(vec_ref[:, at], turned, preferred_element_type=jnp.float32)
            total = part if total is None else total + part
        out_ref[:, here] = total


def turn_part(vec, hamiltonian, loc):
    count, faces, width, _ = hamiltonian.shape
    owned = vec.shape[0]
    return pl.pallas_call(
        turn_kernel,
        out_shape=[
            jax.ShapeDtypeStruct(hamiltonian.shape, hamiltonian.dtype),
            jax.ShapeDtypeStruct(vec.shape, jnp.float32),
        ],
        in_specs=[pl.BlockSpec(memory_space=pltpu.SMEM)] + vmem(2),
        out_specs=vmem(2),
        compiler_params=pltpu.CompilerParams(vmem_limit_bytes=32 << 20),
        cost_estimate=pl.CostEstimate(
            flops=2 * owned * count * width * width * 5,
            bytes_accessed=count * faces * width * width * 4,
            transcendentals=0,
        ),
    )(loc, vec, hamiltonian)


def own_kernel(loc_ref, vec_ref, turned_ref, out_ref):
    count, _, width, _ = turned_ref.shape
    for e in range(count):
        here = slice(e * width, (e + 1) * width)
        total = jnp.dot(vec_ref[:, here], turned_ref[e, 0], preferred_element_type=jnp.float32)
        for face in range(2, 6):
            at = pl.ds(pl.multiple_of(loc_ref[e, face] * width, width), width)
            total += jnp.dot(
                vec_ref[:, at], turned_ref[e, face + 1], preferred_element_type=jnp.float32
            )
        out_ref[:, here] = total


def own_part(vec, turned, loc):
    count, _, width, _ = turned.shape
    owned = vec.shape[0]
    return pl.pallas_call(
        own_kernel,
        out_shape=jax.ShapeDtypeStruct(vec.shape, jnp.float32),
        in_specs=[pl.BlockSpec(memory_space=pltpu.SMEM)] + vmem(2),
        out_specs=pl.BlockSpec(memory_space=pltpu.VMEM),
        compiler_params=pltpu.CompilerParams(vmem_limit_bytes=24 << 20),
        cost_estimate=pl.CostEstimate(
            flops=2 * owned * count * width * width * 5,
            bytes_accessed=count * 5 * width * width * 2,
            transcendentals=0,
        ),
    )(loc, vec, turned)


def halo_kernel(level, loc_ref, low_ref, high_ref, acc_ref, vec_ref, prior_ref, turned_ref, *outs):
    count, _, width, _ = turned_ref.shape
    for e in range(count):
        here = slice(e * width, (e + 1) * width)
        total = acc_ref[:, here]
        for face, ref in enumerate((low_ref, high_ref)):
            at = pl.ds(pl.multiple_of(loc_ref[e, face] * width, width), width)
            total += jnp.dot(
                ref[:, at], turned_ref[e, face + 1], preferred_element_type=jnp.float32
            )
        shifted = (total - centre * vec_ref[:, here].astype(jnp.float32)) * (1.0 / radius)
        if level > 1:
            shifted = 2.0 * shifted - prior_ref[:, here].astype(jnp.float32)
        for out in outs:
            out[:, here] = shifted.astype(out.dtype)


def halo_part(level, low, high, acc, vec, prior, turned, loc):
    count, _, width, _ = turned.shape
    owned = vec.shape[0]
    kinds = [jnp.bfloat16] if level < 3 else [jnp.float32, jnp.bfloat16]
    return pl.pallas_call(
        functools.partial(halo_kernel, level),
        out_shape=[jax.ShapeDtypeStruct(vec.shape, kind) for kind in kinds],
        in_specs=[pl.BlockSpec(memory_space=pltpu.SMEM)] + vmem(6),
        out_specs=vmem(len(kinds)),
        compiler_params=pltpu.CompilerParams(vmem_limit_bytes=24 << 20),
        cost_estimate=pl.CostEstimate(
            flops=2 * owned * count * width * width * 2,
            bytes_accessed=count * 2 * width * width * 2,
            transcendentals=0,
        ),
    )(loc, low, high, acc, vec, prior, turned)


def own_gram_kernel(own_ref, high_ref, out_ref):
    high = high_ref[...]
    low = (own_ref[...] - high.astype(jnp.float32)).astype(jnp.bfloat16)
    mixed = dot_nt(high, low)
    out_ref[...] = dot_nt(high, high) + (mixed + mixed.T)


def cross_gram_kernel(place_ref, own_ref, other_ref, out_ref):
    @pl.when(place_ref[0] == 0)
    def _():
        out_ref[...] = dot_nt(own_ref[...], other_ref[...])

    @pl.when(place_ref[0] != 0)
    def _():
        out_ref[...] = dot_nt(other_ref[...], own_ref[...])


def factor_block(rows, right):
    strips = len(rows)
    shape = rows[0].shape
    sub = lax.broadcasted_iota(jnp.int32, shape, 0)
    upper, inverse = [], []
    for k in range(strips):
        strip, beside = rows[k], right[k]
        lanes = [jnp.broadcast_to(strip[:, k * SUB + j : k * SUB + j + 1], shape) for j in range(SUB)]
        entry = [
            [jnp.broadcast_to(lanes[j][i : i + 1, :], shape) if j <= i else None for j in range(SUB)]
            for i in range(SUB)
        ]
        low = [[None] * SUB for _ in range(SUB)]
        root = []
        for j in range(SUB):
            root.append(lax.rsqrt(entry[j][j]))
            for i in range(j + 1, SUB):
                low[i][j] = entry[i][j] * root[j]
            for i in range(j + 1, SUB):
                for t in range(j + 1, i + 1):
                    entry[i][t] = entry[i][t] - low[i][j] * low[t][j]
        inv = [[None] * SUB for _ in range(SUB)]
        for i in range(SUB):
            inv[i][i] = root[i]
            for j in range(i):
                total = low[i][j] * inv[j][j]
                for t in range(j + 1, i):
                    total = total + low[i][t] * inv[t][j]
                inv[i][j] = -root[i] * total

        def solve(source):
            wide = [jnp.broadcast_to(source[i : i + 1, :], shape) for i in range(SUB)]
            solved = []
            for i in range(SUB):
                total = inv[i][0] * wide[0]
                for j in range(1, i + 1):
                    total = total + inv[i][j] * wide[j]
                solved.append(total)
            back = []
            for i in range(SUB):
                total = inv[i][i] * solved[i]
                for j in range(i + 1, SUB):
                    total = total + inv[j][i] * solved[j]
                back.append(total)
            packed = solved[0]
            for i in range(1, SUB):
                packed = jnp.where(sub == i, solved[i], packed)
            return packed, back

        row_packed, row_back = solve(strip)
        inv_packed, inv_back = solve(beside)
        upper.append(row_packed)
        inverse.append(inv_packed)
        for r in range(k + 1, strips):
            for i in range(SUB):
                column = jnp.broadcast_to(rows[r][:, k * SUB + i : k * SUB + i + 1], shape)
                rows_r = row_back[i] * column
                right_r = inv_back[i] * column
                total = rows_r if i == 0 else total + rows_r
                beyond = right_r if i == 0 else beyond + right_r
            rows[r] = rows[r] - total
            right[r] = right[r] - beyond
    return upper, inverse


def factor_into(work, right, upper_ref, inv_ref):
    half = work.shape[0]
    strips = half // SUB
    row = lax.broadcasted_iota(jnp.int32, (half, half), 0)
    col = lax.broadcasted_iota(jnp.int32, (half, half), 1)
    rows = [work[SUB * s : SUB * (s + 1), :] for s in range(strips)]
    eye = (row == col).astype(jnp.float32)
    beside = [eye[SUB * s : SUB * (s + 1), :] for s in range(strips)]
    upper, inverse = factor_block(rows, beside)
    for s in range(strips):
        work[SUB * s : SUB * (s + 1), :] = upper[s]
        right[SUB * s : SUB * (s + 1), :] = inverse[s]
    upper_ref[...] = jnp.where(col >= row, work[...], 0.0)
    inv_ref[...] = jnp.where(col <= row, right[...], 0.0)


def first_kernel(place_ref, own_ref, other_ref, upper_ref, inv_ref, work, right):
    @pl.when(place_ref[0] == 0)
    def _():
        work[...] = own_ref[...]

    @pl.when(place_ref[0] != 0)
    def _():
        work[...] = other_ref[...]

    factor_into(work, right, upper_ref, inv_ref)


def second_kernel(place_ref, own_ref, other_ref, cross_ref, first_ref, first_inv_ref, upper_ref, inv_ref, work, right):
    half = own_ref.shape[0]
    across = dot_full(first_inv_ref[...], cross_ref[...])
    update = dot_full(across, across, ((0,), (0,)))

    @pl.when(place_ref[0] == 0)
    def _():
        work[...] = other_ref[...] - update

    @pl.when(place_ref[0] != 0)
    def _():
        work[...] = own_ref[...] - update

    zero = jnp.zeros((half, half), jnp.float32)
    upper_ref[0:half, 0:half] = first_ref[...]
    upper_ref[0:half, half:] = across
    upper_ref[half:, 0:half] = zero
    inv_ref[0:half, 0:half] = first_inv_ref[...]
    inv_ref[0:half, half:] = zero
    between = dot_full(across, first_inv_ref[...], ((0,), (0,)))
    factor_into(work, right, upper_ref.at[half:, half:], inv_ref.at[half:, half:])
    inv_ref[half:, 0:half] = -dot_full(inv_ref[half:, half:], between)


def factorize(place, own, other, cross):
    half = own.shape[0]
    smem = [pl.BlockSpec(memory_space=pltpu.SMEM)]
    tile = jax.ShapeDtypeStruct((half, half), jnp.float32)
    scratch = [pltpu.VMEM((half, half), jnp.float32)] * 2
    params = pltpu.CompilerParams(vmem_limit_bytes=24 << 20)
    first, first_inv = pl.pallas_call(
        first_kernel,
        out_shape=[tile] * 2,
        in_specs=smem + vmem(2),
        out_specs=vmem(2),
        scratch_shapes=scratch,
        compiler_params=params,
        cost_estimate=pl.CostEstimate(flops=2 * half**3, bytes_accessed=1 << 24, transcendentals=half),
    )(place, own, other)
    return pl.pallas_call(
        second_kernel,
        out_shape=[jax.ShapeDtypeStruct((2 * half, 2 * half), jnp.float32)] * 2,
        in_specs=smem + vmem(5),
        out_specs=vmem(2),
        scratch_shapes=scratch,
        compiler_params=params,
    )(place, own, other, cross, first, first_inv)


def basis_kernel(place_ref, inv_ref, own_ref, other_ref, out_ref):
    half, total = out_ref.shape
    place = place_ref[0]
    rows = pl.ds(pl.multiple_of(place * half, half), half)
    away = pl.ds(pl.multiple_of((1 - place) * half, half), half)
    near_high, near_low = split(inv_ref[rows, rows])
    far_high, far_low = split(inv_ref[rows, away])
    step = 512 if total % 512 == 0 else total
    for at in range(0, total, step):
        here = slice(at, at + step)
        high, low = split(own_ref[:, here])
        other = other_ref[:, here]
        out_ref[:, here] = (
            jnp.dot(near_high, high, preferred_element_type=jnp.float32)
            + jnp.dot(near_high, low, preferred_element_type=jnp.float32)
            + jnp.dot(near_low, high, preferred_element_type=jnp.float32)
            + jnp.dot(far_high, other, preferred_element_type=jnp.float32)
            + jnp.dot(far_low, other, preferred_element_type=jnp.float32)
        )


def shards(hamiltonian, orbitals, adjacency):
    count = hamiltonian.shape[0]
    owned = orbitals.shape[0]
    blocks = lax.axis_size("space")
    groups = lax.axis_size("orb")
    half = owned * groups // 2
    loc = adjacency % count
    forward = [(i, (i + 1) % blocks) for i in range(blocks)]
    backward = [(target, source) for source, target in forward]
    smem = [pl.BlockSpec(memory_space=pltpu.SMEM)]

    def halo(vec):
        return lax.ppermute(vec, "space", forward), lax.ppermute(vec, "space", backward)

    side = halo(orbitals)
    turned, acc = turn_part(orbitals, hamiltonian, loc)
    (one,) = halo_part(1, *side, acc, orbitals, orbitals, turned, loc)
    side = halo(one)
    (two,) = halo_part(2, *side, own_part(one, turned, loc), one, orbitals, turned, loc)
    side = halo(two)
    filtered, narrow = halo_part(3, *side, own_part(two, turned, loc), two, one, turned, loc)

    def summed(part):
        step = 1
        while step < blocks:
            part = part + lax.ppermute(part, "space", [(i, i ^ step) for i in range(blocks)])
            step *= 2
        return part

    place = lax.axis_index("orb").astype(jnp.int32).reshape(1)
    if groups == 2:
        swap = [(0, 1), (1, 0)]
        other = lax.ppermute(narrow, "orb", swap)
        tile = jax.ShapeDtypeStruct((half, half), jnp.float32)
        params = pltpu.CompilerParams(vmem_limit_bytes=24 << 20)
        near = pl.pallas_call(
            own_gram_kernel,
            out_shape=tile,
            in_specs=vmem(2),
            out_specs=pl.BlockSpec(memory_space=pltpu.VMEM),
            compiler_params=params,
        )(filtered, narrow)
        near = summed(near)
        far = lax.ppermute(near, "orb", swap)
        cross = pl.pallas_call(
            cross_gram_kernel,
            out_shape=tile,
            in_specs=smem + vmem(2),
            out_specs=pl.BlockSpec(memory_space=pltpu.VMEM),
            compiler_params=params,
        )(place, narrow, other)
        upper, inverse = factorize(place, near, far, summed(cross))
    else:
        columns = lax.all_gather(narrow, "orb", axis=0, tiled=True)
        whole = summed(dot_nt(columns, columns))
        upper, inverse = factorize(
            jnp.zeros_like(place), whole[:half, :half], whole[half:, half:], whole[:half, half:]
        )
    if groups == 2:
        basis = pl.pallas_call(
            basis_kernel,
            out_shape=jax.ShapeDtypeStruct(orbitals.shape, jnp.float32),
            in_specs=smem + vmem(3),
            out_specs=pl.BlockSpec(memory_space=pltpu.VMEM),
            compiler_params=pltpu.CompilerParams(vmem_limit_bytes=24 << 20),
        )(place, inverse, filtered, other)
    else:
        mine = lax.dynamic_slice_in_dim(inverse, place[0] * owned, owned, 0)
        near = lax.dynamic_slice_in_dim(mine, place[0] * owned, owned, 1)
        rest = filtered - narrow.astype(jnp.float32)
        basis = dot_full(mine, columns.astype(jnp.float32)) + dot_full(near, rest)
    return (basis, upper)


def solution(mesh):
    in_specs = (P("space", None, None, None), P("orb", "space"), P("space", None))
    out_specs = (P("orb", "space"), P())
    return jax.shard_map(shards, mesh=mesh, in_specs=in_specs, out_specs=out_specs, check_vma=False)
```

```python
import functools

import jax
import jax.numpy as jnp
from jax import lax
from jax.experimental import pallas as pl
from jax.experimental.pallas import tpu as pltpu
from jax.sharding import PartitionSpec as P

centre = 0.25
radius = 0.75
SUB = 8


def vmem(count):
    return [pl.BlockSpec(memory_space=pltpu.VMEM)] * count


def dot_nt(a, b):
    return lax.dot_general(a, b, (((1,), (1,)), ((), ())), preferred_element_type=jnp.float32)


def dot_full(a, b, dims=((1,), (0,))):
    return lax.dot_general(
        a, b, (dims, ((), ())), precision=lax.Precision.HIGHEST, preferred_element_type=jnp.float32
    )


def split(a):
    high = a.astype(jnp.bfloat16)
    return high, (a - high.astype(jnp.float32)).astype(jnp.bfloat16)


def turn_kernel(loc_ref, vec_ref, ham_ref, turned_ref, out_ref):
    count, faces, width, _ = ham_ref.shape
    for e in range(count):
        here = slice(e * width, (e + 1) * width)
        total = None
        for face in range(faces):
            turned = ham_ref[e, face].T
            turned_ref[e, face] = turned
            if face == 1 or face == 2:
                continue
            at = here if face == 0 else pl.ds(pl.multiple_of(loc_ref[e, face - 1] * width, width), width)
            part = jnp.dot(vec_ref[:, at], turned, preferred_element_type=jnp.float32)
            total = part if total is None else total + part
        out_ref[:, here] = total


def turn_part(vec, hamiltonian, loc):
    count, faces, width, _ = hamiltonian.shape
    owned = vec.shape[0]
    return pl.pallas_call(
        turn_kernel,
        out_shape=[
            jax.ShapeDtypeStruct(hamiltonian.shape, hamiltonian.dtype),
            jax.ShapeDtypeStruct(vec.shape, jnp.float32),
        ],
        in_specs=[pl.BlockSpec(memory_space=pltpu.SMEM)] + vmem(2),
        out_specs=vmem(2),
        compiler_params=pltpu.CompilerParams(vmem_limit_bytes=32 << 20),
        cost_estimate=pl.CostEstimate(
            flops=2 * owned * count * width * width * 5,
            bytes_accessed=count * faces * width * width * 4,
            transcendentals=0,
        ),
    )(loc, vec, hamiltonian)


def own_kernel(loc_ref, vec_ref, turned_ref, out_ref):
    count, _, width, _ = turned_ref.shape
    for e in range(count):
        here = slice(e * width, (e + 1) * width)
        total = jnp.dot(vec_ref[:, here], turned_ref[e, 0], preferred_element_type=jnp.float32)
        for face in range(2, 6):
            at = pl.ds(pl.multiple_of(loc_ref[e, face] * width, width), width)
            total += jnp.dot(
                vec_ref[:, at], turned_ref[e, face + 1], preferred_element_type=jnp.float32
            )
        out_ref[:, here] = total


def own_part(vec, turned, loc):
    count, _, width, _ = turned.shape
    owned = vec.shape[0]
    return pl.pallas_call(
        own_kernel,
        out_shape=jax.ShapeDtypeStruct(vec.shape, jnp.float32),
        in_specs=[pl.BlockSpec(memory_space=pltpu.SMEM)] + vmem(2),
        out_specs=pl.BlockSpec(memory_space=pltpu.VMEM),
        compiler_params=pltpu.CompilerParams(vmem_limit_bytes=24 << 20),
        cost_estimate=pl.CostEstimate(
            flops=2 * owned * count * width * width * 5,
            bytes_accessed=count * 5 * width * width * 2,
            transcendentals=0,
        ),
    )(loc, vec, turned)


def halo_kernel(level, loc_ref, low_ref, high_ref, acc_ref, vec_ref, prior_ref, turned_ref, *outs):
    count, _, width, _ = turned_ref.shape
    for e in range(count):
        here = slice(e * width, (e + 1) * width)
        total = acc_ref[:, here]
        for face, ref in enumerate((low_ref, high_ref)):
            at = pl.ds(pl.multiple_of(loc_ref[e, face] * width, width), width)
            total += jnp.dot(
                ref[:, at], turned_ref[e, face + 1], preferred_element_type=jnp.float32
            )
        shifted = (total - centre * vec_ref[:, here].astype(jnp.float32)) * (1.0 / radius)
        if level > 1:
            shifted = 2.0 * shifted - prior_ref[:, here].astype(jnp.float32)
        for out in outs:
            out[:, here] = shifted.astype(out.dtype)


def halo_part(level, low, high, acc, vec, prior, turned, loc):
    count, _, width, _ = turned.shape
    owned = vec.shape[0]
    kinds = [jnp.bfloat16] if level < 3 else [jnp.float32, jnp.bfloat16]
    return pl.pallas_call(
        functools.partial(halo_kernel, level),
        out_shape=[jax.ShapeDtypeStruct(vec.shape, kind) for kind in kinds],
        in_specs=[pl.BlockSpec(memory_space=pltpu.SMEM)] + vmem(6),
        out_specs=vmem(len(kinds)),
        compiler_params=pltpu.CompilerParams(vmem_limit_bytes=24 << 20),
        cost_estimate=pl.CostEstimate(
            flops=2 * owned * count * width * width * 2,
            bytes_accessed=count * 2 * width * width * 2,
            transcendentals=0,
        ),
    )(loc, low, high, acc, vec, prior, turned)


def own_gram_kernel(own_ref, high_ref, out_ref):
    high = high_ref[...]
    low = (own_ref[...] - high.astype(jnp.float32)).astype(jnp.bfloat16)
    mixed = dot_nt(high, low)
    out_ref[...] = dot_nt(high, high) + (mixed + mixed.T)


def cross_gram_kernel(place_ref, own_ref, other_ref, out_ref):
    @pl.when(place_ref[0] == 0)
    def _():
        out_ref[...] = dot_nt(own_ref[...], other_ref[...])

    @pl.when(place_ref[0] != 0)
    def _():
        out_ref[...] = dot_nt(other_ref[...], own_ref[...])


def factor_block(rows, right):
    strips = len(rows)
    shape = rows[0].shape
    sub = lax.broadcasted_iota(jnp.int32, shape, 0)
    upper, inverse = [], []
    for k in range(strips):
        strip, beside = rows[k], right[k]
        lanes = [jnp.broadcast_to(strip[:, k * SUB + j : k * SUB + j + 1], shape) for j in range(SUB)]
        entry = [
            [jnp.broadcast_to(lanes[j][i : i + 1, :], shape) if j <= i else None for j in range(SUB)]
            for i in range(SUB)
        ]
        low = [[None] * SUB for _ in range(SUB)]
        root = []
        for j in range(SUB):
            root.append(lax.rsqrt(entry[j][j]))
            for i in range(j + 1, SUB):
                low[i][j] = entry[i][j] * root[j]
            for i in range(j + 1, SUB):
                for t in range(j + 1, i + 1):
                    entry[i][t] = entry[i][t] - low[i][j] * low[t][j]
        inv = [[None] * SUB for _ in range(SUB)]
        for i in range(SUB):
            inv[i][i] = root[i]
            for j in range(i):
                total = low[i][j] * inv[j][j]
                for t in range(j + 1, i):
                    total = total + low[i][t] * inv[t][j]
                inv[i][j] = -root[i] * total

        def solve(source):
            wide = [jnp.broadcast_to(source[i : i + 1, :], shape) for i in range(SUB)]
            solved = []
            for i in range(SUB):
                total = inv[i][0] * wide[0]
                for j in range(1, i + 1):
                    total = total + inv[i][j] * wide[j]
                solved.append(total)
            back = []
            for i in range(SUB):
                total = inv[i][i] * solved[i]
                for j in range(i + 1, SUB):
                    total = total + inv[j][i] * solved[j]
                back.append(total)
            packed = solved[0]
            for i in range(1, SUB):
                packed = jnp.where(sub == i, solved[i], packed)
            return packed, back

        row_packed, row_back = solve(strip)
        inv_packed, inv_back = solve(beside)
        upper.append(row_packed)
        inverse.append(inv_packed)
        for r in range(k + 1, strips):
            for i in range(SUB):
                column = jnp.broadcast_to(rows[r][:, k * SUB + i : k * SUB + i + 1], shape)
                rows_r = row_back[i] * column
                right_r = inv_back[i] * column
                total = rows_r if i == 0 else total + rows_r
                beyond = right_r if i == 0 else beyond + right_r
            rows[r] = rows[r] - total
            right[r] = right[r] - beyond
    return upper, inverse


def factor_into(work, right, upper_ref, inv_ref):
    half = work.shape[0]
    strips = half // SUB
    row = lax.broadcasted_iota(jnp.int32, (half, half), 0)
    col = lax.broadcasted_iota(jnp.int32, (half, half), 1)
    rows = [work[SUB * s : SUB * (s + 1), :] for s in range(strips)]
    eye = (row == col).astype(jnp.float32)
    beside = [eye[SUB * s : SUB * (s + 1), :] for s in range(strips)]
    upper, inverse = factor_block(rows, beside)
    for s in range(strips):
        work[SUB * s : SUB * (s + 1), :] = upper[s]
        right[SUB * s : SUB * (s + 1), :] = inverse[s]
    upper_ref[...] = jnp.where(col >= row, work[...], 0.0)
    inv_ref[...] = jnp.where(col <= row, right[...], 0.0)


def first_kernel(place_ref, own_ref, other_ref, upper_ref, inv_ref, work, right):
    @pl.when(place_ref[0] == 0)
    def _():
        work[...] = own_ref[...]

    @pl.when(place_ref[0] != 0)
    def _():
        work[...] = other_ref[...]

    factor_into(work, right, upper_ref, inv_ref)


def second_kernel(place_ref, own_ref, other_ref, cross_ref, first_ref, first_inv_ref, upper_ref, inv_ref, work, right):
    half = own_ref.shape[0]
    across = dot_full(first_inv_ref[...], cross_ref[...])
    update = dot_full(across, across, ((0,), (0,)))

    @pl.when(place_ref[0] == 0)
    def _():
        work[...] = other_ref[...] - update

    @pl.when(place_ref[0] != 0)
    def _():
        work[...] = own_ref[...] - update

    zero = jnp.zeros((half, half), jnp.float32)
    upper_ref[0:half, 0:half] = first_ref[...]
    upper_ref[0:half, half:] = across
    upper_ref[half:, 0:half] = zero
    inv_ref[0:half, 0:half] = first_inv_ref[...]
    inv_ref[0:half, half:] = zero
    between = dot_full(across, first_inv_ref[...], ((0,), (0,)))
    factor_into(work, right, upper_ref.at[half:, half:], inv_ref.at[half:, half:])
    inv_ref[half:, 0:half] = -dot_full(inv_ref[half:, half:], between)


def factorize(place, own, other, cross):
    half = own.shape[0]
    smem = [pl.BlockSpec(memory_space=pltpu.SMEM)]
    tile = jax.ShapeDtypeStruct((half, half), jnp.float32)
    scratch = [pltpu.VMEM((half, half), jnp.float32)] * 2
    params = pltpu.CompilerParams(vmem_limit_bytes=24 << 20)
    first, first_inv = pl.pallas_call(
        first_kernel,
        out_shape=[tile] * 2,
        in_specs=smem + vmem(2),
        out_specs=vmem(2),
        scratch_shapes=scratch,
        compiler_params=params,
        cost_estimate=pl.CostEstimate(flops=2 * half**3, bytes_accessed=1 << 24, transcendentals=half),
    )(place, own, other)
    return pl.pallas_call(
        second_kernel,
        out_shape=[jax.ShapeDtypeStruct((2 * half, 2 * half), jnp.float32)] * 2,
        in_specs=smem + vmem(5),
        out_specs=vmem(2),
        scratch_shapes=scratch,
        compiler_params=params,
    )(place, own, other, cross, first, first_inv)


def basis_kernel(place_ref, inv_ref, own_ref, other_ref, out_ref):
    half, total = out_ref.shape
    place = place_ref[0]
    rows = pl.ds(pl.multiple_of(place * half, half), half)
    away = pl.ds(pl.multiple_of((1 - place) * half, half), half)
    near_high, near_low = split(inv_ref[rows, rows])
    far_high, far_low = split(inv_ref[rows, away])
    step = 512 if total % 512 == 0 else total
    for at in range(0, total, step):
        here = slice(at, at + step)
        high, low = split(own_ref[:, here])
        other = other_ref[:, here]
        out_ref[:, here] = (
            jnp.dot(near_high, high, preferred_element_type=jnp.float32)
            + jnp.dot(near_high, low, preferred_element_type=jnp.float32)
            + jnp.dot(near_low, high, preferred_element_type=jnp.float32)
            + jnp.dot(far_high, other, preferred_element_type=jnp.float32)
            + jnp.dot(far_low, other, preferred_element_type=jnp.float32)
        )


def shards(hamiltonian, orbitals, adjacency):
    count = hamiltonian.shape[0]
    owned = orbitals.shape[0]
    blocks = lax.axis_size("space")
    groups = lax.axis_size("orb")
    half = owned * groups // 2
    loc = adjacency % count
    forward = [(i, (i + 1) % blocks) for i in range(blocks)]
    backward = [(target, source) for source, target in forward]
    smem = [pl.BlockSpec(memory_space=pltpu.SMEM)]

    def halo(vec):
        return lax.ppermute(vec, "space", forward), lax.ppermute(vec, "space", backward)

    side = halo(orbitals)
    turned, acc = turn_part(orbitals, hamiltonian, loc)
    (one,) = halo_part(1, *side, acc, orbitals, orbitals, turned, loc)
    side = halo(one)
    (two,) = halo_part(2, *side, own_part(one, turned, loc), one, orbitals, turned, loc)
    side = halo(two)
    filtered, narrow = halo_part(3, *side, own_part(two, turned, loc), two, one, turned, loc)

    def summed(part):
        pieces = part.reshape(blocks, part.shape[0] // blocks, part.shape[1])
        owned_sum = jnp.sum(lax.all_to_all(pieces, "space", 0, 0), axis=0)
        spread = jnp.broadcast_to(owned_sum, pieces.shape)
        return lax.all_to_all(spread, "space", 0, 0).reshape(part.shape)

    place = lax.axis_index("orb").astype(jnp.int32).reshape(1)
    if groups == 2:
        swap = [(0, 1), (1, 0)]
        other = lax.ppermute(narrow, "orb", swap)
        tile = jax.ShapeDtypeStruct((half, half), jnp.float32)
        params = pltpu.CompilerParams(vmem_limit_bytes=24 << 20)
        near = pl.pallas_call(
            own_gram_kernel,
            out_shape=tile,
            in_specs=vmem(2),
            out_specs=pl.BlockSpec(memory_space=pltpu.VMEM),
            compiler_params=params,
        )(filtered, narrow)
        near = summed(near)
        far = lax.ppermute(near, "orb", swap)
        cross = pl.pallas_call(
            cross_gram_kernel,
            out_shape=tile,
            in_specs=smem + vmem(2),
            out_specs=pl.BlockSpec(memory_space=pltpu.VMEM),
            compiler_params=params,
        )(place, narrow, other)
        upper, inverse = factorize(place, near, far, summed(cross))
    else:
        columns = lax.all_gather(narrow, "orb", axis=0, tiled=True)
        whole = summed(dot_nt(columns, columns))
        upper, inverse = factorize(
            jnp.zeros_like(place), whole[:half, :half], whole[half:, half:], whole[:half, half:]
        )
    if groups == 2:
        basis = pl.pallas_call(
            basis_kernel,
            out_shape=jax.ShapeDtypeStruct(orbitals.shape, jnp.float32),
            in_specs=smem + vmem(3),
            out_specs=pl.BlockSpec(memory_space=pltpu.VMEM),
            compiler_params=pltpu.CompilerParams(vmem_limit_bytes=24 << 20),
        )(place, inverse, filtered, other)
    else:
        mine = lax.dynamic_slice_in_dim(inverse, place[0] * owned, owned, 0)
        near = lax.dynamic_slice_in_dim(mine, place[0] * owned, owned, 1)
        rest = filtered - narrow.astype(jnp.float32)
        basis = dot_full(mine, columns.astype(jnp.float32)) + dot_full(near, rest)
    return (basis, upper)


def solution(mesh):
    in_specs = (P("space", None, None, None), P("orb", "space"), P("space", None))
    out_specs = (P("orb", "space"), P())
    return jax.shard_map(shards, mesh=mesh, in_specs=in_specs, out_specs=out_specs, check_vma=False)
```

```python
import functools

import jax
import jax.numpy as jnp
from jax import lax
from jax.experimental import pallas as pl
from jax.experimental.pallas import tpu as pltpu
from jax.sharding import PartitionSpec as P

centre = 0.25
radius = 0.75
SUB = 8


def vmem(count):
    return [pl.BlockSpec(memory_space=pltpu.VMEM)] * count


def dot_nt(a, b):
    return lax.dot_general(a, b, (((1,), (1,)), ((), ())), preferred_element_type=jnp.float32)


def dot_full(a, b, dims=((1,), (0,))):
    return lax.dot_general(
        a, b, (dims, ((), ())), precision=lax.Precision.HIGHEST, preferred_element_type=jnp.float32
    )


def split(a):
    high = a.astype(jnp.bfloat16)
    return high, (a - high.astype(jnp.float32)).astype(jnp.bfloat16)


def turn_kernel(loc_ref, odd_ref, vec_ref, near_ref, ham_ref, turned_ref, out_ref):
    count, faces, width, _ = ham_ref.shape
    odd = odd_ref[0]
    for e in range(count):
        here = slice(e * width, (e + 1) * width)
        total = None
        for face in range(faces):
            source = 2 - odd if face == 1 else 1 + odd if face == 2 else face
            turned = ham_ref[e, source].T
            turned_ref[e, face] = turned
            if face == 2:
                continue
            at = here if face == 0 else pl.ds(pl.multiple_of(loc_ref[e, face - 1] * width, width), width)
            vec = near_ref if face == 1 else vec_ref
            part = jnp.dot(vec[:, at], turned, preferred_element_type=jnp.float32)
            total = part if total is None else total + part
        out_ref[:, here] = total


def turn_part(vec, near, hamiltonian, loc, odd):
    count, faces, width, _ = hamiltonian.shape
    owned = vec.shape[0]
    return pl.pallas_call(
        turn_kernel,
        out_shape=[
            jax.ShapeDtypeStruct(hamiltonian.shape, hamiltonian.dtype),
            jax.ShapeDtypeStruct(vec.shape, jnp.float32),
        ],
        in_specs=[pl.BlockSpec(memory_space=pltpu.SMEM)] * 2 + vmem(3),
        out_specs=vmem(2),
        compiler_params=pltpu.CompilerParams(vmem_limit_bytes=32 << 20),
        cost_estimate=pl.CostEstimate(
            flops=2 * owned * count * width * width * 5,
            bytes_accessed=count * faces * width * width * 4,
            transcendentals=0,
        ),
    )(loc, odd, vec, near, hamiltonian)


def own_kernel(loc_ref, vec_ref, near_ref, turned_ref, out_ref):
    count, _, width, _ = turned_ref.shape
    for e in range(count):
        here = slice(e * width, (e + 1) * width)
        total = jnp.dot(vec_ref[:, here], turned_ref[e, 0], preferred_element_type=jnp.float32)
        for face in (2, 3, 4, 5, 0):
            ref = near_ref if face == 0 else vec_ref
            at = pl.ds(pl.multiple_of(loc_ref[e, face] * width, width), width)
            total += jnp.dot(
                ref[:, at], turned_ref[e, face + 1], preferred_element_type=jnp.float32
            )
        out_ref[:, here] = total


def own_part(vec, near, turned, loc):
    count, _, width, _ = turned.shape
    owned = vec.shape[0]
    return pl.pallas_call(
        own_kernel,
        out_shape=jax.ShapeDtypeStruct(vec.shape, jnp.float32),
        in_specs=[pl.BlockSpec(memory_space=pltpu.SMEM)] + vmem(3),
        out_specs=pl.BlockSpec(memory_space=pltpu.VMEM),
        compiler_params=pltpu.CompilerParams(vmem_limit_bytes=24 << 20),
        cost_estimate=pl.CostEstimate(
            flops=2 * owned * count * width * width * 6,
            bytes_accessed=count * 6 * width * width * 2,
            transcendentals=0,
        ),
    )(loc, vec, near, turned)


def halo_kernel(level, loc_ref, far_ref, acc_ref, vec_ref, prior_ref, turned_ref, *outs):
    count, _, width, _ = turned_ref.shape
    for e in range(count):
        here = slice(e * width, (e + 1) * width)
        at = pl.ds(pl.multiple_of(loc_ref[e, 1] * width, width), width)
        total = acc_ref[:, here] + jnp.dot(
            far_ref[:, at], turned_ref[e, 2], preferred_element_type=jnp.float32
        )
        shifted = (total - centre * vec_ref[:, here].astype(jnp.float32)) * (1.0 / radius)
        if level > 1:
            shifted = 2.0 * shifted - prior_ref[:, here].astype(jnp.float32)
        for out in outs:
            out[:, here] = shifted.astype(out.dtype)


def halo_part(level, far, acc, vec, prior, turned, loc):
    count, _, width, _ = turned.shape
    owned = vec.shape[0]
    kinds = [jnp.bfloat16] if level < 3 else [jnp.float32, jnp.bfloat16]
    return pl.pallas_call(
        functools.partial(halo_kernel, level),
        out_shape=[jax.ShapeDtypeStruct(vec.shape, kind) for kind in kinds],
        in_specs=[pl.BlockSpec(memory_space=pltpu.SMEM)] + vmem(5),
        out_specs=vmem(len(kinds)),
        compiler_params=pltpu.CompilerParams(vmem_limit_bytes=24 << 20),
        cost_estimate=pl.CostEstimate(
            flops=2 * owned * count * width * width,
            bytes_accessed=count * width * width * 2,
            transcendentals=0,
        ),
    )(loc, far, acc, vec, prior, turned)


def own_gram_kernel(own_ref, high_ref, out_ref):
    high = high_ref[...]
    low = (own_ref[...] - high.astype(jnp.float32)).astype(jnp.bfloat16)
    mixed = dot_nt(high, low)
    out_ref[...] = dot_nt(high, high) + (mixed + mixed.T)


def cross_gram_kernel(place_ref, own_ref, other_ref, out_ref):
    @pl.when(place_ref[0] == 0)
    def _():
        out_ref[...] = dot_nt(own_ref[...], other_ref[...])

    @pl.when(place_ref[0] != 0)
    def _():
        out_ref[...] = dot_nt(other_ref[...], own_ref[...])


def factor_block(rows, right):
    strips = len(rows)
    shape = rows[0].shape
    sub = lax.broadcasted_iota(jnp.int32, shape, 0)
    upper, inverse = [], []
    for k in range(strips):
        strip, beside = rows[k], right[k]
        lanes = [jnp.broadcast_to(strip[:, k * SUB + j : k * SUB + j + 1], shape) for j in range(SUB)]
        entry = [
            [jnp.broadcast_to(lanes[j][i : i + 1, :], shape) if j <= i else None for j in range(SUB)]
            for i in range(SUB)
        ]
        low = [[None] * SUB for _ in range(SUB)]
        root = []
        for j in range(SUB):
            root.append(lax.rsqrt(entry[j][j]))
            for i in range(j + 1, SUB):
                low[i][j] = entry[i][j] * root[j]
            for i in range(j + 1, SUB):
                for t in range(j + 1, i + 1):
                    entry[i][t] = entry[i][t] - low[i][j] * low[t][j]
        inv = [[None] * SUB for _ in range(SUB)]
        for i in range(SUB):
            inv[i][i] = root[i]
            for j in range(i):
                total = low[i][j] * inv[j][j]
                for t in range(j + 1, i):
                    total = total + low[i][t] * inv[t][j]
                inv[i][j] = -root[i] * total

        def solve(source):
            wide = [jnp.broadcast_to(source[i : i + 1, :], shape) for i in range(SUB)]
            solved = []
            for i in range(SUB):
                total = inv[i][0] * wide[0]
                for j in range(1, i + 1):
                    total = total + inv[i][j] * wide[j]
                solved.append(total)
            back = []
            for i in range(SUB):
                total = inv[i][i] * solved[i]
                for j in range(i + 1, SUB):
                    total = total + inv[j][i] * solved[j]
                back.append(total)
            packed = solved[0]
            for i in range(1, SUB):
                packed = jnp.where(sub == i, solved[i], packed)
            return packed, back

        row_packed, row_back = solve(strip)
        inv_packed, inv_back = solve(beside)
        upper.append(row_packed)
        inverse.append(inv_packed)
        for r in range(k + 1, strips):
            for i in range(SUB):
                column = jnp.broadcast_to(rows[r][:, k * SUB + i : k * SUB + i + 1], shape)
                rows_r = row_back[i] * column
                right_r = inv_back[i] * column
                total = rows_r if i == 0 else total + rows_r
                beyond = right_r if i == 0 else beyond + right_r
            rows[r] = rows[r] - total
            right[r] = right[r] - beyond
    return upper, inverse


def factor_into(work, right, upper_ref, inv_ref):
    half = work.shape[0]
    strips = half // SUB
    row = lax.broadcasted_iota(jnp.int32, (half, half), 0)
    col = lax.broadcasted_iota(jnp.int32, (half, half), 1)
    rows = [work[SUB * s : SUB * (s + 1), :] for s in range(strips)]
    eye = (row == col).astype(jnp.float32)
    beside = [eye[SUB * s : SUB * (s + 1), :] for s in range(strips)]
    upper, inverse = factor_block(rows, beside)
    for s in range(strips):
        work[SUB * s : SUB * (s + 1), :] = upper[s]
        right[SUB * s : SUB * (s + 1), :] = inverse[s]
    upper_ref[...] = jnp.where(col >= row, work[...], 0.0)
    inv_ref[...] = jnp.where(col <= row, right[...], 0.0)


def first_kernel(place_ref, own_ref, other_ref, upper_ref, inv_ref, work, right):
    @pl.when(place_ref[0] == 0)
    def _():
        work[...] = own_ref[...]

    @pl.when(place_ref[0] != 0)
    def _():
        work[...] = other_ref[...]

    factor_into(work, right, upper_ref, inv_ref)


def second_kernel(place_ref, own_ref, other_ref, cross_ref, first_ref, first_inv_ref, upper_ref, inv_ref, work, right):
    half = own_ref.shape[0]
    across = dot_full(first_inv_ref[...], cross_ref[...])
    update = dot_full(across, across, ((0,), (0,)))

    @pl.when(place_ref[0] == 0)
    def _():
        work[...] = other_ref[...] - update

    @pl.when(place_ref[0] != 0)
    def _():
        work[...] = own_ref[...] - update

    zero = jnp.zeros((half, half), jnp.float32)
    upper_ref[0:half, 0:half] = first_ref[...]
    upper_ref[0:half, half:] = across
    upper_ref[half:, 0:half] = zero
    inv_ref[0:half, 0:half] = first_inv_ref[...]
    inv_ref[0:half, half:] = zero
    between = dot_full(across, first_inv_ref[...], ((0,), (0,)))
    factor_into(work, right, upper_ref.at[half:, half:], inv_ref.at[half:, half:])
    inv_ref[half:, 0:half] = -dot_full(inv_ref[half:, half:], between)


def factorize(place, own, other, cross):
    half = own.shape[0]
    smem = [pl.BlockSpec(memory_space=pltpu.SMEM)]
    tile = jax.ShapeDtypeStruct((half, half), jnp.float32)
    scratch = [pltpu.VMEM((half, half), jnp.float32)] * 2
    params = pltpu.CompilerParams(vmem_limit_bytes=24 << 20)
    first, first_inv = pl.pallas_call(
        first_kernel,
        out_shape=[tile] * 2,
        in_specs=smem + vmem(2),
        out_specs=vmem(2),
        scratch_shapes=scratch,
        compiler_params=params,
        cost_estimate=pl.CostEstimate(flops=2 * half**3, bytes_accessed=1 << 24, transcendentals=half),
    )(place, own, other)
    return pl.pallas_call(
        second_kernel,
        out_shape=[jax.ShapeDtypeStruct((2 * half, 2 * half), jnp.float32)] * 2,
        in_specs=smem + vmem(5),
        out_specs=vmem(2),
        scratch_shapes=scratch,
        compiler_params=params,
    )(place, own, other, cross, first, first_inv)


def basis_kernel(place_ref, inv_ref, own_ref, other_ref, out_ref):
    half, total = out_ref.shape
    place = place_ref[0]
    rows = pl.ds(pl.multiple_of(place * half, half), half)
    away = pl.ds(pl.multiple_of((1 - place) * half, half), half)
    near_high, near_low = split(inv_ref[rows, rows])
    far_high, far_low = split(inv_ref[rows, away])
    step = 512 if total % 512 == 0 else total
    for at in range(0, total, step):
        here = slice(at, at + step)
        high, low = split(own_ref[:, here])
        other = other_ref[:, here]
        out_ref[:, here] = (
            jnp.dot(near_high, high, preferred_element_type=jnp.float32)
            + jnp.dot(near_high, low, preferred_element_type=jnp.float32)
            + jnp.dot(near_low, high, preferred_element_type=jnp.float32)
            + jnp.dot(far_high, other, preferred_element_type=jnp.float32)
            + jnp.dot(far_low, other, preferred_element_type=jnp.float32)
        )


def shards(hamiltonian, orbitals, adjacency):
    count = hamiltonian.shape[0]
    owned = orbitals.shape[0]
    blocks = lax.axis_size("space")
    groups = lax.axis_size("orb")
    half = owned * groups // 2
    odd = lax.axis_index("space").astype(jnp.int32).reshape(1) % 2
    loc = adjacency % count
    swapped = jnp.concatenate([loc[:, 1:2], loc[:, 0:1], loc[:, 2:]], axis=1)
    loc = jnp.where(odd[0] == 1, loc, swapped)
    near_pairs = [(i, i ^ 1) for i in range(blocks)]
    far_pairs = [(i, (i + 1 if i % 2 else i - 1) % blocks) for i in range(blocks)]
    smem = [pl.BlockSpec(memory_space=pltpu.SMEM)]

    def halo(vec):
        far = lax.ppermute(vec, "space", far_pairs)
        return far, lax.ppermute(vec, "space", near_pairs)

    far, near = halo(orbitals)
    turned, acc = turn_part(orbitals, near, hamiltonian, loc, odd)
    (one,) = halo_part(1, far, acc, orbitals, orbitals, turned, loc)
    far, near = halo(one)
    (two,) = halo_part(2, far, own_part(one, near, turned, loc), one, orbitals, turned, loc)
    far, near = halo(two)
    filtered, narrow = halo_part(3, far, own_part(two, near, turned, loc), two, one, turned, loc)

    def summed(part):
        step = 1
        while step < blocks:
            part = part + lax.ppermute(part, "space", [(i, i ^ step) for i in range(blocks)])
            step *= 2
        return part

    place = lax.axis_index("orb").astype(jnp.int32).reshape(1)
    if groups == 2:
        swap = [(0, 1), (1, 0)]
        other = lax.ppermute(narrow, "orb", swap)
        tile = jax.ShapeDtypeStruct((half, half), jnp.float32)
        params = pltpu.CompilerParams(vmem_limit_bytes=24 << 20)
        near = pl.pallas_call(
            own_gram_kernel,
            out_shape=tile,
            in_specs=vmem(2),
            out_specs=pl.BlockSpec(memory_space=pltpu.VMEM),
            compiler_params=params,
        )(filtered, narrow)
        near = summed(near)
        far = lax.ppermute(near, "orb", swap)
        cross = pl.pallas_call(
            cross_gram_kernel,
            out_shape=tile,
            in_specs=smem + vmem(2),
            out_specs=pl.BlockSpec(memory_space=pltpu.VMEM),
            compiler_params=params,
        )(place, narrow, other)
        upper, inverse = factorize(place, near, far, summed(cross))
    else:
        columns = lax.all_gather(narrow, "orb", axis=0, tiled=True)
        whole = summed(dot_nt(columns, columns))
        upper, inverse = factorize(
            jnp.zeros_like(place), whole[:half, :half], whole[half:, half:], whole[:half, half:]
        )
    if groups == 2:
        basis = pl.pallas_call(
            basis_kernel,
            out_shape=jax.ShapeDtypeStruct(orbitals.shape, jnp.float32),
            in_specs=smem + vmem(3),
            out_specs=pl.BlockSpec(memory_space=pltpu.VMEM),
            compiler_params=pltpu.CompilerParams(vmem_limit_bytes=24 << 20),
        )(place, inverse, filtered, other)
    else:
        mine = lax.dynamic_slice_in_dim(inverse, place[0] * owned, owned, 0)
        near = lax.dynamic_slice_in_dim(mine, place[0] * owned, owned, 1)
        rest = filtered - narrow.astype(jnp.float32)
        basis = dot_full(mine, columns.astype(jnp.float32)) + dot_full(near, rest)
    return (basis, upper)


def solution(mesh):
    in_specs = (P("space", None, None, None), P("orb", "space"), P("space", None))
    out_specs = (P("orb", "space"), P())
    return jax.shard_map(shards, mesh=mesh, in_specs=in_specs, out_specs=out_specs, check_vma=False)
```

```python
import functools

import jax
import jax.numpy as jnp
from jax import lax
from jax.experimental import pallas as pl
from jax.experimental.pallas import tpu as pltpu
from jax.sharding import PartitionSpec as P

centre = 0.25
radius = 0.75
SUB = 8


def vmem(count):
    return [pl.BlockSpec(memory_space=pltpu.VMEM)] * count


def dot_nt(a, b):
    return lax.dot_general(a, b, (((1,), (1,)), ((), ())), preferred_element_type=jnp.float32)


def dot_full(a, b, dims=((1,), (0,))):
    return lax.dot_general(
        a, b, (dims, ((), ())), precision=lax.Precision.HIGHEST, preferred_element_type=jnp.float32
    )


def split(a):
    high = a.astype(jnp.bfloat16)
    return high, (a - high.astype(jnp.float32)).astype(jnp.bfloat16)


def turn_kernel(loc_ref, odd_ref, vec_ref, ham_ref, turned_ref, out_ref):
    count, faces, width, _ = ham_ref.shape
    odd = odd_ref[0]
    for e in range(count):
        here = slice(e * width, (e + 1) * width)
        total = None
        for face in range(faces):
            source = 2 - odd if face == 1 else 1 + odd if face == 2 else face
            turned = ham_ref[e, source].T
            turned_ref[e, face] = turned
            if face == 1 or face == 2:
                continue
            at = here if face == 0 else pl.ds(pl.multiple_of(loc_ref[e, face - 1] * width, width), width)
            part = jnp.dot(vec_ref[:, at], turned, preferred_element_type=jnp.float32)
            total = part if total is None else total + part
        out_ref[:, here] = total


def turn_part(vec, hamiltonian, loc, odd):
    count, faces, width, _ = hamiltonian.shape
    owned = vec.shape[0]
    return pl.pallas_call(
        turn_kernel,
        out_shape=[
            jax.ShapeDtypeStruct(hamiltonian.shape, hamiltonian.dtype),
            jax.ShapeDtypeStruct(vec.shape, jnp.float32),
        ],
        in_specs=[pl.BlockSpec(memory_space=pltpu.SMEM)] * 2 + vmem(2),
        out_specs=vmem(2),
        compiler_params=pltpu.CompilerParams(vmem_limit_bytes=32 << 20),
        cost_estimate=pl.CostEstimate(
            flops=2 * owned * count * width * width * 5,
            bytes_accessed=count * faces * width * width * 4,
            transcendentals=0,
        ),
    )(loc, odd, vec, hamiltonian)


def own_kernel(loc_ref, vec_ref, turned_ref, out_ref):
    count, _, width, _ = turned_ref.shape
    for e in range(count):
        here = slice(e * width, (e + 1) * width)
        total = jnp.dot(vec_ref[:, here], turned_ref[e, 0], preferred_element_type=jnp.float32)
        for face in range(2, 6):
            at = pl.ds(pl.multiple_of(loc_ref[e, face] * width, width), width)
            total += jnp.dot(
                vec_ref[:, at], turned_ref[e, face + 1], preferred_element_type=jnp.float32
            )
        out_ref[:, here] = total


def own_part(vec, turned, loc):
    count, _, width, _ = turned.shape
    owned = vec.shape[0]
    return pl.pallas_call(
        own_kernel,
        out_shape=jax.ShapeDtypeStruct(vec.shape, jnp.float32),
        in_specs=[pl.BlockSpec(memory_space=pltpu.SMEM)] + vmem(2),
        out_specs=pl.BlockSpec(memory_space=pltpu.VMEM),
        compiler_params=pltpu.CompilerParams(vmem_limit_bytes=24 << 20),
        cost_estimate=pl.CostEstimate(
            flops=2 * owned * count * width * width * 5,
            bytes_accessed=count * 5 * width * width * 2,
            transcendentals=0,
        ),
    )(loc, vec, turned)


def halo_kernel(level, loc_ref, near_ref, far_ref, acc_ref, vec_ref, prior_ref, turned_ref, *outs):
    count, _, width, _ = turned_ref.shape
    for e in range(count):
        here = slice(e * width, (e + 1) * width)
        total = acc_ref[:, here]
        for face, ref in enumerate((near_ref, far_ref)):
            at = pl.ds(pl.multiple_of(loc_ref[e, face] * width, width), width)
            total += jnp.dot(
                ref[:, at], turned_ref[e, face + 1], preferred_element_type=jnp.float32
            )
        shifted = (total - centre * vec_ref[:, here].astype(jnp.float32)) * (1.0 / radius)
        if level > 1:
            shifted = 2.0 * shifted - prior_ref[:, here].astype(jnp.float32)
        for out in outs:
            out[:, here] = shifted.astype(out.dtype)


def halo_part(level, near, far, acc, vec, prior, turned, loc):
    count, _, width, _ = turned.shape
    owned = vec.shape[0]
    kinds = [jnp.bfloat16] if level < 3 else [jnp.float32, jnp.bfloat16]
    return pl.pallas_call(
        functools.partial(halo_kernel, level),
        out_shape=[jax.ShapeDtypeStruct(vec.shape, kind) for kind in kinds],
        in_specs=[pl.BlockSpec(memory_space=pltpu.SMEM)] + vmem(6),
        out_specs=vmem(len(kinds)),
        compiler_params=pltpu.CompilerParams(vmem_limit_bytes=24 << 20),
        cost_estimate=pl.CostEstimate(
            flops=2 * owned * count * width * width * 2,
            bytes_accessed=count * 2 * width * width * 2,
            transcendentals=0,
        ),
    )(loc, near, far, acc, vec, prior, turned)


def own_gram_kernel(own_ref, high_ref, out_ref):
    high = high_ref[...]
    low = (own_ref[...] - high.astype(jnp.float32)).astype(jnp.bfloat16)
    mixed = dot_nt(high, low)
    out_ref[...] = dot_nt(high, high) + (mixed + mixed.T)


def cross_gram_kernel(place_ref, own_ref, other_ref, out_ref):
    @pl.when(place_ref[0] == 0)
    def _():
        out_ref[...] = dot_nt(own_ref[...], other_ref[...])

    @pl.when(place_ref[0] != 0)
    def _():
        out_ref[...] = dot_nt(other_ref[...], own_ref[...])


def factor_block(rows, right):
    strips = len(rows)
    shape = rows[0].shape
    sub = lax.broadcasted_iota(jnp.int32, shape, 0)
    upper, inverse = [], []
    for k in range(strips):
        strip, beside = rows[k], right[k]
        lanes = [jnp.broadcast_to(strip[:, k * SUB + j : k * SUB + j + 1], shape) for j in range(SUB)]
        entry = [
            [jnp.broadcast_to(lanes[j][i : i + 1, :], shape) if j <= i else None for j in range(SUB)]
            for i in range(SUB)
        ]
        low = [[None] * SUB for _ in range(SUB)]
        root = []
        for j in range(SUB):
            root.append(lax.rsqrt(entry[j][j]))
            for i in range(j + 1, SUB):
                low[i][j] = entry[i][j] * root[j]
            for i in range(j + 1, SUB):
                for t in range(j + 1, i + 1):
                    entry[i][t] = entry[i][t] - low[i][j] * low[t][j]
        inv = [[None] * SUB for _ in range(SUB)]
        for i in range(SUB):
            inv[i][i] = root[i]
            for j in range(i):
                total = low[i][j] * inv[j][j]
                for t in range(j + 1, i):
                    total = total + low[i][t] * inv[t][j]
                inv[i][j] = -root[i] * total

        def solve(source):
            wide = [jnp.broadcast_to(source[i : i + 1, :], shape) for i in range(SUB)]
            solved = []
            for i in range(SUB):
                total = inv[i][0] * wide[0]
                for j in range(1, i + 1):
                    total = total + inv[i][j] * wide[j]
                solved.append(total)
            back = []
            for i in range(SUB):
                total = inv[i][i] * solved[i]
                for j in range(i + 1, SUB):
                    total = total + inv[j][i] * solved[j]
                back.append(total)
            packed = solved[0]
            for i in range(1, SUB):
                packed = jnp.where(sub == i, solved[i], packed)
            return packed, back

        row_packed, row_back = solve(strip)
        inv_packed, inv_back = solve(beside)
        upper.append(row_packed)
        inverse.append(inv_packed)
        for r in range(k + 1, strips):
            for i in range(SUB):
                column = jnp.broadcast_to(rows[r][:, k * SUB + i : k * SUB + i + 1], shape)
                rows_r = row_back[i] * column
                right_r = inv_back[i] * column
                total = rows_r if i == 0 else total + rows_r
                beyond = right_r if i == 0 else beyond + right_r
            rows[r] = rows[r] - total
            right[r] = right[r] - beyond
    return upper, inverse


def factor_into(work, right, upper_ref, inv_ref):
    half = work.shape[0]
    strips = half // SUB
    row = lax.broadcasted_iota(jnp.int32, (half, half), 0)
    col = lax.broadcasted_iota(jnp.int32, (half, half), 1)
    rows = [work[SUB * s : SUB * (s + 1), :] for s in range(strips)]
    eye = (row == col).astype(jnp.float32)
    beside = [eye[SUB * s : SUB * (s + 1), :] for s in range(strips)]
    upper, inverse = factor_block(rows, beside)
    for s in range(strips):
        work[SUB * s : SUB * (s + 1), :] = upper[s]
        right[SUB * s : SUB * (s + 1), :] = inverse[s]
    upper_ref[...] = jnp.where(col >= row, work[...], 0.0)
    inv_ref[...] = jnp.where(col <= row, right[...], 0.0)


def first_kernel(place_ref, own_ref, other_ref, upper_ref, inv_ref, work, right):
    @pl.when(place_ref[0] == 0)
    def _():
        work[...] = own_ref[...]

    @pl.when(place_ref[0] != 0)
    def _():
        work[...] = other_ref[...]

    factor_into(work, right, upper_ref, inv_ref)


def second_kernel(place_ref, own_ref, other_ref, cross_ref, first_ref, first_inv_ref, upper_ref, inv_ref, work, right):
    half = own_ref.shape[0]
    across = dot_full(first_inv_ref[...], cross_ref[...])
    update = dot_full(across, across, ((0,), (0,)))

    @pl.when(place_ref[0] == 0)
    def _():
        work[...] = other_ref[...] - update

    @pl.when(place_ref[0] != 0)
    def _():
        work[...] = own_ref[...] - update

    zero = jnp.zeros((half, half), jnp.float32)
    upper_ref[0:half, 0:half] = first_ref[...]
    upper_ref[0:half, half:] = across
    upper_ref[half:, 0:half] = zero
    inv_ref[0:half, 0:half] = first_inv_ref[...]
    inv_ref[0:half, half:] = zero
    between = dot_full(across, first_inv_ref[...], ((0,), (0,)))
    factor_into(work, right, upper_ref.at[half:, half:], inv_ref.at[half:, half:])
    inv_ref[half:, 0:half] = -dot_full(inv_ref[half:, half:], between)


def factorize(place, own, other, cross):
    half = own.shape[0]
    smem = [pl.BlockSpec(memory_space=pltpu.SMEM)]
    tile = jax.ShapeDtypeStruct((half, half), jnp.float32)
    scratch = [pltpu.VMEM((half, half), jnp.float32)] * 2
    params = pltpu.CompilerParams(vmem_limit_bytes=24 << 20)
    first, first_inv = pl.pallas_call(
        first_kernel,
        out_shape=[tile] * 2,
        in_specs=smem + vmem(2),
        out_specs=vmem(2),
        scratch_shapes=scratch,
        compiler_params=params,
        cost_estimate=pl.CostEstimate(flops=2 * half**3, bytes_accessed=1 << 24, transcendentals=half),
    )(place, own, other)
    return pl.pallas_call(
        second_kernel,
        out_shape=[jax.ShapeDtypeStruct((2 * half, 2 * half), jnp.float32)] * 2,
        in_specs=smem + vmem(5),
        out_specs=vmem(2),
        scratch_shapes=scratch,
        compiler_params=params,
    )(place, own, other, cross, first, first_inv)


def basis_kernel(place_ref, inv_ref, own_ref, other_ref, out_ref):
    half, total = out_ref.shape
    place = place_ref[0]
    rows = pl.ds(pl.multiple_of(place * half, half), half)
    away = pl.ds(pl.multiple_of((1 - place) * half, half), half)
    near_high, near_low = split(inv_ref[rows, rows])
    far_high, far_low = split(inv_ref[rows, away])
    step = 512 if total % 512 == 0 else total
    for at in range(0, total, step):
        here = slice(at, at + step)
        high, low = split(own_ref[:, here])
        other = other_ref[:, here]
        out_ref[:, here] = (
            jnp.dot(near_high, high, preferred_element_type=jnp.float32)
            + jnp.dot(near_high, low, preferred_element_type=jnp.float32)
            + jnp.dot(near_low, high, preferred_element_type=jnp.float32)
            + jnp.dot(far_high, other, preferred_element_type=jnp.float32)
            + jnp.dot(far_low, other, preferred_element_type=jnp.float32)
        )


def shards(hamiltonian, orbitals, adjacency):
    count = hamiltonian.shape[0]
    owned = orbitals.shape[0]
    blocks = lax.axis_size("space")
    groups = lax.axis_size("orb")
    half = owned * groups // 2
    odd = lax.axis_index("space").astype(jnp.int32).reshape(1) % 2
    loc = adjacency % count
    swapped = jnp.concatenate([loc[:, 1:2], loc[:, 0:1], loc[:, 2:]], axis=1)
    loc = jnp.where(odd[0] == 1, loc, swapped)
    near_pairs = [(i, i ^ 1) for i in range(blocks)]
    far_pairs = [(i, (i + 1 if i % 2 else i - 1) % blocks) for i in range(blocks)]
    smem = [pl.BlockSpec(memory_space=pltpu.SMEM)]

    def halo(vec):
        far = lax.ppermute(vec, "space", far_pairs)
        return lax.ppermute(vec, "space", near_pairs), far

    side = halo(orbitals)
    turned, acc = turn_part(orbitals, hamiltonian, loc, odd)
    (one,) = halo_part(1, *side, acc, orbitals, orbitals, turned, loc)
    side = halo(one)
    (two,) = halo_part(2, *side, own_part(one, turned, loc), one, orbitals, turned, loc)
    side = halo(two)
    filtered, narrow = halo_part(3, *side, own_part(two, turned, loc), two, one, turned, loc)

    def summed(part):
        step = 1
        while step < blocks:
            part = part + lax.ppermute(part, "space", [(i, i ^ step) for i in range(blocks)])
            step *= 2
        return part

    place = lax.axis_index("orb").astype(jnp.int32).reshape(1)
    if groups == 2:
        swap = [(0, 1), (1, 0)]
        other = lax.ppermute(narrow, "orb", swap)
        tile = jax.ShapeDtypeStruct((half, half), jnp.float32)
        params = pltpu.CompilerParams(vmem_limit_bytes=24 << 20)
        near = pl.pallas_call(
            own_gram_kernel,
            out_shape=tile,
            in_specs=vmem(2),
            out_specs=pl.BlockSpec(memory_space=pltpu.VMEM),
            compiler_params=params,
        )(filtered, narrow)
        near = summed(near)
        far = lax.ppermute(near, "orb", swap)
        cross = pl.pallas_call(
            cross_gram_kernel,
            out_shape=tile,
            in_specs=smem + vmem(2),
            out_specs=pl.BlockSpec(memory_space=pltpu.VMEM),
            compiler_params=params,
        )(place, narrow, other)
        upper, inverse = factorize(place, near, far, summed(cross))
    else:
        columns = lax.all_gather(narrow, "orb", axis=0, tiled=True)
        whole = summed(dot_nt(columns, columns))
        upper, inverse = factorize(
            jnp.zeros_like(place), whole[:half, :half], whole[half:, half:], whole[:half, half:]
        )
    if groups == 2:
        basis = pl.pallas_call(
            basis_kernel,
            out_shape=jax.ShapeDtypeStruct(orbitals.shape, jnp.float32),
            in_specs=smem + vmem(3),
            out_specs=pl.BlockSpec(memory_space=pltpu.VMEM),
            compiler_params=pltpu.CompilerParams(vmem_limit_bytes=24 << 20),
        )(place, inverse, filtered, other)
    else:
        mine = lax.dynamic_slice_in_dim(inverse, place[0] * owned, owned, 0)
        near = lax.dynamic_slice_in_dim(mine, place[0] * owned, owned, 1)
        rest = filtered - narrow.astype(jnp.float32)
        basis = dot_full(mine, columns.astype(jnp.float32)) + dot_full(near, rest)
    return (basis, upper)


def solution(mesh):
    in_specs = (P("space", None, None, None), P("orb", "space"), P("space", None))
    out_specs = (P("orb", "space"), P())
    return jax.shard_map(shards, mesh=mesh, in_specs=in_specs, out_specs=out_specs, check_vma=False)
```

```python
import functools

import jax
import jax.numpy as jnp
from jax import lax
from jax.experimental import pallas as pl
from jax.experimental.pallas import tpu as pltpu
from jax.sharding import PartitionSpec as P

centre = 0.25
radius = 0.75
SUB = 8


def vmem(count):
    return [pl.BlockSpec(memory_space=pltpu.VMEM)] * count


def dot_nt(a, b):
    return lax.dot_general(a, b, (((1,), (1,)), ((), ())), preferred_element_type=jnp.float32)


def dot_full(a, b, dims=((1,), (0,))):
    return lax.dot_general(
        a, b, (dims, ((), ())), precision=lax.Precision.HIGHEST, preferred_element_type=jnp.float32
    )


def split(a):
    high = a.astype(jnp.bfloat16)
    return high, (a - high.astype(jnp.float32)).astype(jnp.bfloat16)


def turn_kernel(loc_ref, odd_ref, vec_ref, ham_ref, turned_ref, *outs):
    count, faces, width, _ = ham_ref.shape
    share = outs[0].shape[0]
    odd = odd_ref[0]
    for e in range(count):
        here = slice(e * width, (e + 1) * width)
        total = None
        for face in range(faces):
            source = 2 - odd if face == 1 else 1 + odd if face == 2 else face
            turned = ham_ref[e, source].T
            turned_ref[e, face] = turned
            if face == 1 or face == 2:
                continue
            at = here if face == 0 else pl.ds(pl.multiple_of(loc_ref[e, face - 1] * width, width), width)
            part = jnp.dot(vec_ref[:, at], turned, preferred_element_type=jnp.float32)
            total = part if total is None else total + part
        for piece, out in enumerate(outs):
            out[:, here] = total[piece * share : (piece + 1) * share]


def turn_part(vec, hamiltonian, loc, odd, chunks):
    count, faces, width, _ = hamiltonian.shape
    owned = vec.shape[0]
    return pl.pallas_call(
        turn_kernel,
        out_shape=[
            jax.ShapeDtypeStruct(hamiltonian.shape, hamiltonian.dtype),
            *[jax.ShapeDtypeStruct((owned // chunks, vec.shape[1]), jnp.float32)] * chunks,
        ],
        in_specs=[pl.BlockSpec(memory_space=pltpu.SMEM)] * 2 + vmem(2),
        out_specs=vmem(1 + chunks),
        compiler_params=pltpu.CompilerParams(vmem_limit_bytes=32 << 20),
        cost_estimate=pl.CostEstimate(
            flops=2 * owned * count * width * width * 5,
            bytes_accessed=count * faces * width * width * 4,
            transcendentals=0,
        ),
    )(loc, odd, vec, hamiltonian)


def own_kernel(loc_ref, vec_ref, turned_ref, out_ref):
    count, _, width, _ = turned_ref.shape
    for e in range(count):
        here = slice(e * width, (e + 1) * width)
        total = jnp.dot(vec_ref[:, here], turned_ref[e, 0], preferred_element_type=jnp.float32)
        for face in range(2, 6):
            at = pl.ds(pl.multiple_of(loc_ref[e, face] * width, width), width)
            total += jnp.dot(
                vec_ref[:, at], turned_ref[e, face + 1], preferred_element_type=jnp.float32
            )
        out_ref[:, here] = total


def own_part(vec, turned, loc):
    count, _, width, _ = turned.shape
    owned = vec.shape[0]
    return pl.pallas_call(
        own_kernel,
        out_shape=jax.ShapeDtypeStruct(vec.shape, jnp.float32),
        in_specs=[pl.BlockSpec(memory_space=pltpu.SMEM)] + vmem(2),
        out_specs=pl.BlockSpec(memory_space=pltpu.VMEM),
        compiler_params=pltpu.CompilerParams(vmem_limit_bytes=24 << 20),
        cost_estimate=pl.CostEstimate(
            flops=2 * owned * count * width * width * 5,
            bytes_accessed=count * 5 * width * width * 2,
            transcendentals=0,
        ),
    )(loc, vec, turned)


def halo_kernel(level, loc_ref, near_ref, far_ref, acc_ref, vec_ref, prior_ref, turned_ref, *outs):
    count, _, width, _ = turned_ref.shape
    for e in range(count):
        here = slice(e * width, (e + 1) * width)
        total = acc_ref[:, here]
        for face, ref in enumerate((near_ref, far_ref)):
            at = pl.ds(pl.multiple_of(loc_ref[e, face] * width, width), width)
            total += jnp.dot(
                ref[:, at], turned_ref[e, face + 1], preferred_element_type=jnp.float32
            )
        shifted = (total - centre * vec_ref[:, here].astype(jnp.float32)) * (1.0 / radius)
        if level > 1:
            shifted = 2.0 * shifted - prior_ref[:, here].astype(jnp.float32)
        for out in outs:
            out[:, here] = shifted.astype(out.dtype)


def halo_part(level, near, far, acc, vec, prior, turned, loc):
    count, _, width, _ = turned.shape
    owned = vec.shape[0]
    kinds = [jnp.bfloat16] if level < 3 else [jnp.float32, jnp.bfloat16]
    return pl.pallas_call(
        functools.partial(halo_kernel, level),
        out_shape=[jax.ShapeDtypeStruct(vec.shape, kind) for kind in kinds],
        in_specs=[pl.BlockSpec(memory_space=pltpu.SMEM)] + vmem(6),
        out_specs=vmem(len(kinds)),
        compiler_params=pltpu.CompilerParams(vmem_limit_bytes=24 << 20),
        cost_estimate=pl.CostEstimate(
            flops=2 * owned * count * width * width * 2,
            bytes_accessed=count * 2 * width * width * 2,
            transcendentals=0,
        ),
    )(loc, near, far, acc, vec, prior, turned)


def stacked(refs, here=slice(None)):
    return jnp.concatenate([ref[:, here] for ref in refs], axis=0)


def own_gram_kernel(chunks, *refs):
    own_refs, high_refs, out_ref = refs[:chunks], refs[chunks:-1], refs[-1]
    high = stacked(high_refs)
    low = (stacked(own_refs) - high.astype(jnp.float32)).astype(jnp.bfloat16)
    mixed = dot_nt(high, low)
    out_ref[...] = dot_nt(high, high) + (mixed + mixed.T)


def cross_gram_kernel(chunks, place_ref, *refs):
    own_refs, other_refs, out_ref = refs[:chunks], refs[chunks:-1], refs[-1]

    @pl.when(place_ref[0] == 0)
    def _():
        out_ref[...] = dot_nt(stacked(own_refs), stacked(other_refs))

    @pl.when(place_ref[0] != 0)
    def _():
        out_ref[...] = dot_nt(stacked(other_refs), stacked(own_refs))


def factor_block(rows, right):
    strips = len(rows)
    shape = rows[0].shape
    sub = lax.broadcasted_iota(jnp.int32, shape, 0)
    upper, inverse = [], []
    for k in range(strips):
        strip, beside = rows[k], right[k]
        lanes = [jnp.broadcast_to(strip[:, k * SUB + j : k * SUB + j + 1], shape) for j in range(SUB)]
        entry = [
            [jnp.broadcast_to(lanes[j][i : i + 1, :], shape) if j <= i else None for j in range(SUB)]
            for i in range(SUB)
        ]
        low = [[None] * SUB for _ in range(SUB)]
        root = []
        for j in range(SUB):
            root.append(lax.rsqrt(entry[j][j]))
            for i in range(j + 1, SUB):
                low[i][j] = entry[i][j] * root[j]
            for i in range(j + 1, SUB):
                for t in range(j + 1, i + 1):
                    entry[i][t] = entry[i][t] - low[i][j] * low[t][j]
        inv = [[None] * SUB for _ in range(SUB)]
        for i in range(SUB):
            inv[i][i] = root[i]
            for j in range(i):
                total = low[i][j] * inv[j][j]
                for t in range(j + 1, i):
                    total = total + low[i][t] * inv[t][j]
                inv[i][j] = -root[i] * total

        def solve(source):
            wide = [jnp.broadcast_to(source[i : i + 1, :], shape) for i in range(SUB)]
            solved = []
            for i in range(SUB):
                total = inv[i][0] * wide[0]
                for j in range(1, i + 1):
                    total = total + inv[i][j] * wide[j]
                solved.append(total)
            back = []
            for i in range(SUB):
                total = inv[i][i] * solved[i]
                for j in range(i + 1, SUB):
                    total = total + inv[j][i] * solved[j]
                back.append(total)
            packed = solved[0]
            for i in range(1, SUB):
                packed = jnp.where(sub == i, solved[i], packed)
            return packed, back

        row_packed, row_back = solve(strip)
        inv_packed, inv_back = solve(beside)
        upper.append(row_packed)
        inverse.append(inv_packed)
        for r in range(k + 1, strips):
            for i in range(SUB):
                column = jnp.broadcast_to(rows[r][:, k * SUB + i : k * SUB + i + 1], shape)
                rows_r = row_back[i] * column
                right_r = inv_back[i] * column
                total = rows_r if i == 0 else total + rows_r
                beyond = right_r if i == 0 else beyond + right_r
            rows[r] = rows[r] - total
            right[r] = right[r] - beyond
    return upper, inverse


def factor_into(work, right, upper_ref, inv_ref):
    half = work.shape[0]
    strips = half // SUB
    row = lax.broadcasted_iota(jnp.int32, (half, half), 0)
    col = lax.broadcasted_iota(jnp.int32, (half, half), 1)
    rows = [work[SUB * s : SUB * (s + 1), :] for s in range(strips)]
    eye = (row == col).astype(jnp.float32)
    beside = [eye[SUB * s : SUB * (s + 1), :] for s in range(strips)]
    upper, inverse = factor_block(rows, beside)
    for s in range(strips):
        work[SUB * s : SUB * (s + 1), :] = upper[s]
        right[SUB * s : SUB * (s + 1), :] = inverse[s]
    upper_ref[...] = jnp.where(col >= row, work[...], 0.0)
    inv_ref[...] = jnp.where(col <= row, right[...], 0.0)


def first_kernel(place_ref, own_ref, other_ref, upper_ref, inv_ref, work, right):
    @pl.when(place_ref[0] == 0)
    def _():
        work[...] = own_ref[...]

    @pl.when(place_ref[0] != 0)
    def _():
        work[...] = other_ref[...]

    factor_into(work, right, upper_ref, inv_ref)


def second_kernel(place_ref, own_ref, other_ref, cross_ref, first_ref, first_inv_ref, upper_ref, inv_ref, work, right):
    half = own_ref.shape[0]
    across = dot_full(first_inv_ref[...], cross_ref[...])
    update = dot_full(across, across, ((0,), (0,)))

    @pl.when(place_ref[0] == 0)
    def _():
        work[...] = other_ref[...] - update

    @pl.when(place_ref[0] != 0)
    def _():
        work[...] = own_ref[...] - update

    zero = jnp.zeros((half, half), jnp.float32)
    upper_ref[0:half, 0:half] = first_ref[...]
    upper_ref[0:half, half:] = across
    upper_ref[half:, 0:half] = zero
    inv_ref[0:half, 0:half] = first_inv_ref[...]
    inv_ref[0:half, half:] = zero
    between = dot_full(across, first_inv_ref[...], ((0,), (0,)))
    factor_into(work, right, upper_ref.at[half:, half:], inv_ref.at[half:, half:])
    inv_ref[half:, 0:half] = -dot_full(inv_ref[half:, half:], between)


def factorize(place, own, other, cross):
    half = own.shape[0]
    smem = [pl.BlockSpec(memory_space=pltpu.SMEM)]
    tile = jax.ShapeDtypeStruct((half, half), jnp.float32)
    scratch = [pltpu.VMEM((half, half), jnp.float32)] * 2
    params = pltpu.CompilerParams(vmem_limit_bytes=24 << 20)
    first, first_inv = pl.pallas_call(
        first_kernel,
        out_shape=[tile] * 2,
        in_specs=smem + vmem(2),
        out_specs=vmem(2),
        scratch_shapes=scratch,
        compiler_params=params,
        cost_estimate=pl.CostEstimate(flops=2 * half**3, bytes_accessed=1 << 24, transcendentals=half),
    )(place, own, other)
    return pl.pallas_call(
        second_kernel,
        out_shape=[jax.ShapeDtypeStruct((2 * half, 2 * half), jnp.float32)] * 2,
        in_specs=smem + vmem(5),
        out_specs=vmem(2),
        scratch_shapes=scratch,
        compiler_params=params,
    )(place, own, other, cross, first, first_inv)


def basis_kernel(chunks, place_ref, inv_ref, *refs):
    own_refs, other_refs, out_ref = refs[:chunks], refs[chunks:-1], refs[-1]
    half, total = out_ref.shape
    place = place_ref[0]
    rows = pl.ds(pl.multiple_of(place * half, half), half)
    away = pl.ds(pl.multiple_of((1 - place) * half, half), half)
    near_high, near_low = split(inv_ref[rows, rows])
    far_high, far_low = split(inv_ref[rows, away])
    step = 512 if total % 512 == 0 else total
    for at in range(0, total, step):
        here = slice(at, at + step)
        high, low = split(stacked(own_refs, here))
        other = stacked(other_refs, here)
        out_ref[:, here] = (
            jnp.dot(near_high, high, preferred_element_type=jnp.float32)
            + jnp.dot(near_high, low, preferred_element_type=jnp.float32)
            + jnp.dot(near_low, high, preferred_element_type=jnp.float32)
            + jnp.dot(far_high, other, preferred_element_type=jnp.float32)
            + jnp.dot(far_low, other, preferred_element_type=jnp.float32)
        )


def shards(hamiltonian, orbitals, adjacency):
    count = hamiltonian.shape[0]
    owned = orbitals.shape[0]
    blocks = lax.axis_size("space")
    groups = lax.axis_size("orb")
    half = owned * groups // 2
    chunks = 2
    share = owned // chunks
    odd = lax.axis_index("space").astype(jnp.int32).reshape(1) % 2
    loc = adjacency % count
    swapped = jnp.concatenate([loc[:, 1:2], loc[:, 0:1], loc[:, 2:]], axis=1)
    loc = jnp.where(odd[0] == 1, loc, swapped)
    near_pairs = [(i, i ^ 1) for i in range(blocks)]
    far_pairs = [(i, (i + 1 if i % 2 else i - 1) % blocks) for i in range(blocks)]
    smem = [pl.BlockSpec(memory_space=pltpu.SMEM)]

    def level(number, vec, prior, turned):
        far = lax.ppermute(vec, "space", far_pairs)
        near = lax.ppermute(vec, "space", near_pairs)
        acc = own_part(vec, turned, loc)
        return halo_part(number, near, far, acc, vec, prior, turned, loc)

    zero = [orbitals[piece * share : (piece + 1) * share] for piece in range(chunks)]
    far = [lax.ppermute(vec, "space", far_pairs) for vec in zero]
    near = [lax.ppermute(vec, "space", near_pairs) for vec in zero]
    turned, *accs = turn_part(orbitals, hamiltonian, loc, odd, chunks)
    one, two, filtered, narrow = [], [], [], []
    for piece in range(chunks):
        base = zero[piece]
        one += halo_part(1, near[piece], far[piece], accs[piece], base, base, turned, loc)
    for piece in range(chunks):
        two += level(2, one[piece], zero[piece], turned)
    for piece in range(chunks):
        wide, short = level(3, two[piece], one[piece], turned)
        filtered.append(wide)
        narrow.append(short)

    def summed(part):
        step = 1
        while step < blocks:
            part = part + lax.ppermute(part, "space", [(i, i ^ step) for i in range(blocks)])
            step *= 2
        return part

    place = lax.axis_index("orb").astype(jnp.int32).reshape(1)
    if groups == 2:
        swap = [(0, 1), (1, 0)]
        other = [lax.ppermute(piece, "orb", swap) for piece in narrow]
        tile = jax.ShapeDtypeStruct((half, half), jnp.float32)
        params = pltpu.CompilerParams(vmem_limit_bytes=24 << 20)
        near = pl.pallas_call(
            functools.partial(own_gram_kernel, chunks),
            out_shape=tile,
            in_specs=vmem(2 * chunks),
            out_specs=pl.BlockSpec(memory_space=pltpu.VMEM),
            compiler_params=params,
        )(*filtered, *narrow)
        near = summed(near)
        far = lax.ppermute(near, "orb", swap)
        cross = pl.pallas_call(
            functools.partial(cross_gram_kernel, chunks),
            out_shape=tile,
            in_specs=smem + vmem(2 * chunks),
            out_specs=pl.BlockSpec(memory_space=pltpu.VMEM),
            compiler_params=params,
        )(place, *narrow, *other)
        upper, inverse = factorize(place, near, far, summed(cross))
    else:
        columns = lax.all_gather(jnp.concatenate(narrow), "orb", axis=0, tiled=True)
        whole = summed(dot_nt(columns, columns))
        upper, inverse = factorize(
            jnp.zeros_like(place), whole[:half, :half], whole[half:, half:], whole[:half, half:]
        )
    if groups == 2:
        basis = pl.pallas_call(
            functools.partial(basis_kernel, chunks),
            out_shape=jax.ShapeDtypeStruct(orbitals.shape, jnp.float32),
            in_specs=smem + vmem(1 + 2 * chunks),
            out_specs=pl.BlockSpec(memory_space=pltpu.VMEM),
            compiler_params=pltpu.CompilerParams(vmem_limit_bytes=24 << 20),
        )(place, inverse, *filtered, *other)
    else:
        mine = lax.dynamic_slice_in_dim(inverse, place[0] * owned, owned, 0)
        near = lax.dynamic_slice_in_dim(mine, place[0] * owned, owned, 1)
        rest = jnp.concatenate(filtered) - jnp.concatenate(narrow).astype(jnp.float32)
        basis = dot_full(mine, columns.astype(jnp.float32)) + dot_full(near, rest)
    return (basis, upper)


def solution(mesh):
    in_specs = (P("space", None, None, None), P("orb", "space"), P("space", None))
    out_specs = (P("orb", "space"), P())
    return jax.shard_map(shards, mesh=mesh, in_specs=in_specs, out_specs=out_specs, check_vma=False)
```

```python
import functools

import jax
import jax.numpy as jnp
from jax import lax
from jax.experimental import pallas as pl
from jax.experimental.pallas import tpu as pltpu
from jax.sharding import PartitionSpec as P

centre = 0.25
radius = 0.75
SUB = 8


def vmem(count):
    return [pl.BlockSpec(memory_space=pltpu.VMEM)] * count


def dot_nt(a, b):
    return lax.dot_general(a, b, (((1,), (1,)), ((), ())), preferred_element_type=jnp.float32)


def dot_full(a, b, dims=((1,), (0,))):
    return lax.dot_general(
        a, b, (dims, ((), ())), precision=lax.Precision.HIGHEST, preferred_element_type=jnp.float32
    )


def split(a):
    high = a.astype(jnp.bfloat16)
    return high, (a - high.astype(jnp.float32)).astype(jnp.bfloat16)


def turn_kernel(loc_ref, odd_ref, vec_ref, ham_ref, turned_ref, out_ref):
    count, faces, width, _ = ham_ref.shape
    odd = odd_ref[0]
    for e in range(count):
        here = slice(e * width, (e + 1) * width)
        total = None
        for face in range(faces):
            source = 2 - odd if face == 1 else 1 + odd if face == 2 else face
            turned = ham_ref[e, source].T
            turned_ref[e, face] = turned
            if face == 1 or face == 2:
                continue
            at = here if face == 0 else pl.ds(pl.multiple_of(loc_ref[e, face - 1] * width, width), width)
            part = jnp.dot(vec_ref[:, at], turned, preferred_element_type=jnp.float32)
            total = part if total is None else total + part
        out_ref[:, here] = total


def turn_part(vec, hamiltonian, loc, odd):
    count, faces, width, _ = hamiltonian.shape
    owned = vec.shape[0]
    return pl.pallas_call(
        turn_kernel,
        out_shape=[
            jax.ShapeDtypeStruct(hamiltonian.shape, hamiltonian.dtype),
            jax.ShapeDtypeStruct(vec.shape, jnp.float32),
        ],
        in_specs=[pl.BlockSpec(memory_space=pltpu.SMEM)] * 2 + vmem(2),
        out_specs=vmem(2),
        compiler_params=pltpu.CompilerParams(vmem_limit_bytes=32 << 20),
        cost_estimate=pl.CostEstimate(
            flops=2 * owned * count * width * width * 5,
            bytes_accessed=count * faces * width * width * 4,
            transcendentals=0,
        ),
    )(loc, odd, vec, hamiltonian)


def own_kernel(loc_ref, vec_ref, turned_ref, out_ref):
    count, _, width, _ = turned_ref.shape
    for e in range(count):
        here = slice(e * width, (e + 1) * width)
        total = jnp.dot(vec_ref[:, here], turned_ref[e, 0], preferred_element_type=jnp.float32)
        for face in range(2, 6):
            at = pl.ds(pl.multiple_of(loc_ref[e, face] * width, width), width)
            total += jnp.dot(
                vec_ref[:, at], turned_ref[e, face + 1], preferred_element_type=jnp.float32
            )
        out_ref[:, here] = total


def own_part(vec, turned, loc):
    count, _, width, _ = turned.shape
    owned = vec.shape[0]
    return pl.pallas_call(
        own_kernel,
        out_shape=jax.ShapeDtypeStruct(vec.shape, jnp.float32),
        in_specs=[pl.BlockSpec(memory_space=pltpu.SMEM)] + vmem(2),
        out_specs=pl.BlockSpec(memory_space=pltpu.VMEM),
        compiler_params=pltpu.CompilerParams(vmem_limit_bytes=24 << 20),
        cost_estimate=pl.CostEstimate(
            flops=2 * owned * count * width * width * 5,
            bytes_accessed=count * 5 * width * width * 2,
            transcendentals=0,
        ),
    )(loc, vec, turned)


def halo_kernel(level, loc_ref, near_ref, far_ref, acc_ref, vec_ref, prior_ref, turned_ref, *outs):
    count, _, width, _ = turned_ref.shape
    for e in range(count):
        here = slice(e * width, (e + 1) * width)
        total = acc_ref[:, here]
        for face, ref in enumerate((near_ref, far_ref)):
            at = pl.ds(pl.multiple_of(loc_ref[e, face] * width, width), width)
            total += jnp.dot(
                ref[:, at], turned_ref[e, face + 1], preferred_element_type=jnp.float32
            )
        shifted = (total - centre * vec_ref[:, here].astype(jnp.float32)) * (1.0 / radius)
        if level > 1:
            shifted = 2.0 * shifted - prior_ref[:, here].astype(jnp.float32)
        for out in outs:
            out[:, here] = shifted.astype(out.dtype)


def halo_part(level, near, far, acc, vec, prior, turned, loc):
    count, _, width, _ = turned.shape
    owned = vec.shape[0]
    kinds = [jnp.bfloat16] if level < 3 else [jnp.float32, jnp.bfloat16]
    return pl.pallas_call(
        functools.partial(halo_kernel, level),
        out_shape=[jax.ShapeDtypeStruct(vec.shape, kind) for kind in kinds],
        in_specs=[pl.BlockSpec(memory_space=pltpu.SMEM)] + vmem(6),
        out_specs=vmem(len(kinds)),
        compiler_params=pltpu.CompilerParams(vmem_limit_bytes=24 << 20),
        cost_estimate=pl.CostEstimate(
            flops=2 * owned * count * width * width * 2,
            bytes_accessed=count * 2 * width * width * 2,
            transcendentals=0,
        ),
    )(loc, near, far, acc, vec, prior, turned)


def own_gram_kernel(own_ref, high_ref, out_ref):
    high = high_ref[...]
    low = (own_ref[...] - high.astype(jnp.float32)).astype(jnp.bfloat16)
    mixed = dot_nt(high, low)
    out_ref[...] = dot_nt(high, high) + (mixed + mixed.T)


def cross_gram_kernel(place_ref, own_ref, other_ref, after_ref, out_ref):
    del after_ref

    @pl.when(place_ref[0] == 0)
    def _():
        out_ref[...] = dot_nt(own_ref[...], other_ref[...])

    @pl.when(place_ref[0] != 0)
    def _():
        out_ref[...] = dot_nt(other_ref[...], own_ref[...])


def factor_block(rows, right):
    strips = len(rows)
    shape = rows[0].shape
    sub = lax.broadcasted_iota(jnp.int32, shape, 0)
    upper, inverse = [], []
    for k in range(strips):
        strip, beside = rows[k], right[k]
        lanes = [jnp.broadcast_to(strip[:, k * SUB + j : k * SUB + j + 1], shape) for j in range(SUB)]
        entry = [
            [jnp.broadcast_to(lanes[j][i : i + 1, :], shape) if j <= i else None for j in range(SUB)]
            for i in range(SUB)
        ]
        low = [[None] * SUB for _ in range(SUB)]
        root = []
        for j in range(SUB):
            root.append(lax.rsqrt(entry[j][j]))
            for i in range(j + 1, SUB):
                low[i][j] = entry[i][j] * root[j]
            for i in range(j + 1, SUB):
                for t in range(j + 1, i + 1):
                    entry[i][t] = entry[i][t] - low[i][j] * low[t][j]
        inv = [[None] * SUB for _ in range(SUB)]
        for i in range(SUB):
            inv[i][i] = root[i]
            for j in range(i):
                total = low[i][j] * inv[j][j]
                for t in range(j + 1, i):
                    total = total + low[i][t] * inv[t][j]
                inv[i][j] = -root[i] * total

        def solve(source):
            wide = [jnp.broadcast_to(source[i : i + 1, :], shape) for i in range(SUB)]
            solved = []
            for i in range(SUB):
                total = inv[i][0] * wide[0]
                for j in range(1, i + 1):
                    total = total + inv[i][j] * wide[j]
                solved.append(total)
            back = []
            for i in range(SUB):
                total = inv[i][i] * solved[i]
                for j in range(i + 1, SUB):
                    total = total + inv[j][i] * solved[j]
                back.append(total)
            packed = solved[0]
            for i in range(1, SUB):
                packed = jnp.where(sub == i, solved[i], packed)
            return packed, back

        row_packed, row_back = solve(strip)
        inv_packed, inv_back = solve(beside)
        upper.append(row_packed)
        inverse.append(inv_packed)
        for r in range(k + 1, strips):
            for i in range(SUB):
                column = jnp.broadcast_to(rows[r][:, k * SUB + i : k * SUB + i + 1], shape)
                rows_r = row_back[i] * column
                right_r = inv_back[i] * column
                total = rows_r if i == 0 else total + rows_r
                beyond = right_r if i == 0 else beyond + right_r
            rows[r] = rows[r] - total
            right[r] = right[r] - beyond
    return upper, inverse


def factor_into(work, right, upper_ref, inv_ref):
    half = work.shape[0]
    strips = half // SUB
    row = lax.broadcasted_iota(jnp.int32, (half, half), 0)
    col = lax.broadcasted_iota(jnp.int32, (half, half), 1)
    rows = [work[SUB * s : SUB * (s + 1), :] for s in range(strips)]
    eye = (row == col).astype(jnp.float32)
    beside = [eye[SUB * s : SUB * (s + 1), :] for s in range(strips)]
    upper, inverse = factor_block(rows, beside)
    for s in range(strips):
        work[SUB * s : SUB * (s + 1), :] = upper[s]
        right[SUB * s : SUB * (s + 1), :] = inverse[s]
    upper_ref[...] = jnp.where(col >= row, work[...], 0.0)
    inv_ref[...] = jnp.where(col <= row, right[...], 0.0)


def first_kernel(place_ref, own_ref, other_ref, after_ref, upper_ref, inv_ref, work, right):
    del after_ref

    @pl.when(place_ref[0] == 0)
    def _():
        work[...] = own_ref[...]

    @pl.when(place_ref[0] != 0)
    def _():
        work[...] = other_ref[...]

    factor_into(work, right, upper_ref, inv_ref)


def second_kernel(place_ref, own_ref, other_ref, cross_ref, first_ref, first_inv_ref, upper_ref, inv_ref, work, right):
    half = own_ref.shape[0]
    across = dot_full(first_inv_ref[...], cross_ref[...])
    update = dot_full(across, across, ((0,), (0,)))

    @pl.when(place_ref[0] == 0)
    def _():
        work[...] = other_ref[...] - update

    @pl.when(place_ref[0] != 0)
    def _():
        work[...] = own_ref[...] - update

    zero = jnp.zeros((half, half), jnp.float32)
    upper_ref[0:half, 0:half] = first_ref[...]
    upper_ref[0:half, half:] = across
    upper_ref[half:, 0:half] = zero
    inv_ref[0:half, 0:half] = first_inv_ref[...]
    inv_ref[0:half, half:] = zero
    between = dot_full(across, first_inv_ref[...], ((0,), (0,)))
    factor_into(work, right, upper_ref.at[half:, half:], inv_ref.at[half:, half:])
    inv_ref[half:, 0:half] = -dot_full(inv_ref[half:, half:], between)


def factorize(place, own, other, cross, after):
    half = own.shape[0]
    smem = [pl.BlockSpec(memory_space=pltpu.SMEM)]
    tile = jax.ShapeDtypeStruct((half, half), jnp.float32)
    scratch = [pltpu.VMEM((half, half), jnp.float32)] * 2
    params = pltpu.CompilerParams(vmem_limit_bytes=24 << 20)
    first, first_inv = pl.pallas_call(
        first_kernel,
        out_shape=[tile] * 2,
        in_specs=smem + vmem(2) + [pl.BlockSpec(memory_space=pl.ANY)],
        out_specs=vmem(2),
        scratch_shapes=scratch,
        compiler_params=params,
        cost_estimate=pl.CostEstimate(flops=2 * half**3, bytes_accessed=1 << 24, transcendentals=half),
    )(place, own, other, after)
    return pl.pallas_call(
        second_kernel,
        out_shape=[jax.ShapeDtypeStruct((2 * half, 2 * half), jnp.float32)] * 2,
        in_specs=smem + vmem(5),
        out_specs=vmem(2),
        scratch_shapes=scratch,
        compiler_params=params,
    )(place, own, other, cross, first, first_inv)


def basis_kernel(place_ref, inv_ref, own_ref, other_ref, out_ref):
    half, total = out_ref.shape
    place = place_ref[0]
    rows = pl.ds(pl.multiple_of(place * half, half), half)
    away = pl.ds(pl.multiple_of((1 - place) * half, half), half)
    near_high, near_low = split(inv_ref[rows, rows])
    far_high, far_low = split(inv_ref[rows, away])
    step = 512 if total % 512 == 0 else total
    for at in range(0, total, step):
        here = slice(at, at + step)
        high, low = split(own_ref[:, here])
        other = other_ref[:, here]
        out_ref[:, here] = (
            jnp.dot(near_high, high, preferred_element_type=jnp.float32)
            + jnp.dot(near_high, low, preferred_element_type=jnp.float32)
            + jnp.dot(near_low, high, preferred_element_type=jnp.float32)
            + jnp.dot(far_high, other, preferred_element_type=jnp.float32)
            + jnp.dot(far_low, other, preferred_element_type=jnp.float32)
        )


def shards(hamiltonian, orbitals, adjacency):
    count = hamiltonian.shape[0]
    owned = orbitals.shape[0]
    blocks = lax.axis_size("space")
    groups = lax.axis_size("orb")
    half = owned * groups // 2
    odd = lax.axis_index("space").astype(jnp.int32).reshape(1) % 2
    loc = adjacency % count
    swapped = jnp.concatenate([loc[:, 1:2], loc[:, 0:1], loc[:, 2:]], axis=1)
    loc = jnp.where(odd[0] == 1, loc, swapped)
    near_pairs = [(i, i ^ 1) for i in range(blocks)]
    far_pairs = [(i, (i + 1 if i % 2 else i - 1) % blocks) for i in range(blocks)]
    smem = [pl.BlockSpec(memory_space=pltpu.SMEM)]

    def halo(vec):
        far = lax.ppermute(vec, "space", far_pairs)
        return lax.ppermute(vec, "space", near_pairs), far

    side = halo(orbitals)
    turned, acc = turn_part(orbitals, hamiltonian, loc, odd)
    (one,) = halo_part(1, *side, acc, orbitals, orbitals, turned, loc)
    side = halo(one)
    (two,) = halo_part(2, *side, own_part(one, turned, loc), one, orbitals, turned, loc)
    side = halo(two)
    filtered, narrow = halo_part(3, *side, own_part(two, turned, loc), two, one, turned, loc)

    steps = [1 << i for i in range((blocks - 1).bit_length())]

    def summed(part, chosen):
        for step in chosen:
            part = part + lax.ppermute(part, "space", [(i, i ^ step) for i in range(blocks)])
        return part

    place = lax.axis_index("orb").astype(jnp.int32).reshape(1)
    if groups == 2:
        swap = [(0, 1), (1, 0)]
        other = lax.ppermute(narrow, "orb", swap)
        tile = jax.ShapeDtypeStruct((half, half), jnp.float32)
        params = pltpu.CompilerParams(vmem_limit_bytes=24 << 20)
        near = pl.pallas_call(
            own_gram_kernel,
            out_shape=tile,
            in_specs=vmem(2),
            out_specs=pl.BlockSpec(memory_space=pltpu.VMEM),
            compiler_params=params,
        )(filtered, narrow)
        near = summed(near, steps[:-1])
        cross = pl.pallas_call(
            cross_gram_kernel,
            out_shape=tile,
            in_specs=smem + vmem(2) + [pl.BlockSpec(memory_space=pl.ANY)],
            out_specs=pl.BlockSpec(memory_space=pltpu.VMEM),
            compiler_params=params,
        )(place, narrow, other, near)
        near = summed(near, steps[-1:])
        far = lax.ppermute(near, "orb", swap)
        cross = summed(cross, steps[:-1])
        upper, inverse = factorize(place, near, far, summed(cross, steps[-1:]), cross)
    else:
        columns = lax.all_gather(narrow, "orb", axis=0, tiled=True)
        whole = summed(dot_nt(columns, columns), steps)
        upper, inverse = factorize(
            jnp.zeros_like(place), whole[:half, :half], whole[half:, half:], whole[:half, half:], whole
        )
    if groups == 2:
        basis = pl.pallas_call(
            basis_kernel,
            out_shape=jax.ShapeDtypeStruct(orbitals.shape, jnp.float32),
            in_specs=smem + vmem(3),
            out_specs=pl.BlockSpec(memory_space=pltpu.VMEM),
            compiler_params=pltpu.CompilerParams(vmem_limit_bytes=24 << 20),
        )(place, inverse, filtered, other)
    else:
        mine = lax.dynamic_slice_in_dim(inverse, place[0] * owned, owned, 0)
        near = lax.dynamic_slice_in_dim(mine, place[0] * owned, owned, 1)
        rest = filtered - narrow.astype(jnp.float32)
        basis = dot_full(mine, columns.astype(jnp.float32)) + dot_full(near, rest)
    return (basis, upper)


def solution(mesh):
    in_specs = (P("space", None, None, None), P("orb", "space"), P("space", None))
    out_specs = (P("orb", "space"), P())
    return jax.shard_map(shards, mesh=mesh, in_specs=in_specs, out_specs=out_specs, check_vma=False)
```

```python
import functools

import jax
import jax.numpy as jnp
from jax import lax
from jax.experimental import pallas as pl
from jax.experimental.pallas import tpu as pltpu
from jax.sharding import PartitionSpec as P

centre = 0.25
radius = 0.75
SUB = 8


def vmem(count):
    return [pl.BlockSpec(memory_space=pltpu.VMEM)] * count


def dot_nt(a, b):
    return lax.dot_general(a, b, (((1,), (1,)), ((), ())), preferred_element_type=jnp.float32)


def dot_full(a, b, dims=((1,), (0,))):
    return lax.dot_general(
        a, b, (dims, ((), ())), precision=lax.Precision.HIGHEST, preferred_element_type=jnp.float32
    )


def split(a):
    high = a.astype(jnp.bfloat16)
    return high, (a - high.astype(jnp.float32)).astype(jnp.bfloat16)


def turn_kernel(loc_ref, odd_ref, vec_ref, ham_ref, turned_ref, out_ref):
    count, faces, width, _ = ham_ref.shape
    odd = odd_ref[0]
    for e in range(count):
        here = slice(e * width, (e + 1) * width)
        total = None
        for face in range(faces):
            source = 2 - odd if face == 1 else 1 + odd if face == 2 else face
            turned = ham_ref[e, source].T
            turned_ref[e, face] = turned
            if face == 1 or face == 2:
                continue
            at = here if face == 0 else pl.ds(pl.multiple_of(loc_ref[e, face - 1] * width, width), width)
            part = jnp.dot(vec_ref[:, at], turned, preferred_element_type=jnp.float32)
            total = part if total is None else total + part
        out_ref[:, here] = total


def turn_part(vec, hamiltonian, loc, odd):
    count, faces, width, _ = hamiltonian.shape
    owned = vec.shape[0]
    return pl.pallas_call(
        turn_kernel,
        out_shape=[
            jax.ShapeDtypeStruct(hamiltonian.shape, hamiltonian.dtype),
            jax.ShapeDtypeStruct(vec.shape, jnp.float32),
        ],
        in_specs=[pl.BlockSpec(memory_space=pltpu.SMEM)] * 2 + vmem(2),
        out_specs=vmem(2),
        compiler_params=pltpu.CompilerParams(vmem_limit_bytes=32 << 20),
        cost_estimate=pl.CostEstimate(
            flops=2 * owned * count * width * width * 5,
            bytes_accessed=count * faces * width * width * 4,
            transcendentals=0,
        ),
    )(loc, odd, vec, hamiltonian)


def own_kernel(loc_ref, vec_ref, turned_ref, out_ref):
    count, _, width, _ = turned_ref.shape
    for e in range(count):
        here = slice(e * width, (e + 1) * width)
        total = jnp.dot(vec_ref[:, here], turned_ref[e, 0], preferred_element_type=jnp.float32)
        for face in range(2, 6):
            at = pl.ds(pl.multiple_of(loc_ref[e, face] * width, width), width)
            total += jnp.dot(
                vec_ref[:, at], turned_ref[e, face + 1], preferred_element_type=jnp.float32
            )
        out_ref[:, here] = total


def own_part(vec, turned, loc):
    count, _, width, _ = turned.shape
    owned = vec.shape[0]
    return pl.pallas_call(
        own_kernel,
        out_shape=jax.ShapeDtypeStruct(vec.shape, jnp.float32),
        in_specs=[pl.BlockSpec(memory_space=pltpu.SMEM)] + vmem(2),
        out_specs=pl.BlockSpec(memory_space=pltpu.VMEM),
        compiler_params=pltpu.CompilerParams(vmem_limit_bytes=24 << 20),
        cost_estimate=pl.CostEstimate(
            flops=2 * owned * count * width * width * 5,
            bytes_accessed=count * 5 * width * width * 2,
            transcendentals=0,
        ),
    )(loc, vec, turned)


def halo_kernel(level, loc_ref, near_ref, far_ref, acc_ref, vec_ref, prior_ref, turned_ref, *outs):
    count, _, width, _ = turned_ref.shape
    for e in range(count):
        here = slice(e * width, (e + 1) * width)
        total = acc_ref[:, here]
        for face, ref in enumerate((near_ref, far_ref)):
            at = pl.ds(pl.multiple_of(loc_ref[e, face] * width, width), width)
            total += jnp.dot(
                ref[:, at], turned_ref[e, face + 1], preferred_element_type=jnp.float32
            )
        shifted = (total - centre * vec_ref[:, here].astype(jnp.float32)) * (1.0 / radius)
        if level > 1:
            shifted = 2.0 * shifted - prior_ref[:, here].astype(jnp.float32)
        for out in outs:
            out[:, here] = shifted.astype(out.dtype)


def halo_part(level, near, far, acc, vec, prior, turned, loc):
    count, _, width, _ = turned.shape
    owned = vec.shape[0]
    kinds = [jnp.bfloat16] if level < 3 else [jnp.float32, jnp.bfloat16]
    return pl.pallas_call(
        functools.partial(halo_kernel, level),
        out_shape=[jax.ShapeDtypeStruct(vec.shape, kind) for kind in kinds],
        in_specs=[pl.BlockSpec(memory_space=pltpu.SMEM)] + vmem(6),
        out_specs=vmem(len(kinds)),
        compiler_params=pltpu.CompilerParams(vmem_limit_bytes=24 << 20),
        cost_estimate=pl.CostEstimate(
            flops=2 * owned * count * width * width * 2,
            bytes_accessed=count * 2 * width * width * 2,
            transcendentals=0,
        ),
    )(loc, near, far, acc, vec, prior, turned)


def own_gram_kernel(own_ref, high_ref, out_ref):
    high = high_ref[...]
    low = (own_ref[...] - high.astype(jnp.float32)).astype(jnp.bfloat16)
    mixed = dot_nt(high, low)
    out_ref[...] = dot_nt(high, high) + (mixed + mixed.T)


def cross_gram_kernel(place_ref, own_ref, other_ref, out_ref):
    @pl.when(place_ref[0] == 0)
    def _():
        out_ref[...] = dot_nt(own_ref[...], other_ref[...])

    @pl.when(place_ref[0] != 0)
    def _():
        out_ref[...] = dot_nt(other_ref[...], own_ref[...])


def tree(terms):
    while len(terms) > 1:
        terms = [terms[i] + terms[i + 1] if i + 1 < len(terms) else terms[i] for i in range(0, len(terms), 2)]
    return terms[0]


def factor_block(rows, right):
    strips = len(rows)
    shape = rows[0].shape
    sub = lax.broadcasted_iota(jnp.int32, shape, 0)
    upper, inverse = [], []
    for k in range(strips):
        lanes = [
            jnp.broadcast_to(rows[k][:, k * SUB + j : k * SUB + j + 1], shape) for j in range(SUB)
        ]
        entry = [
            [jnp.broadcast_to(lanes[j][i : i + 1, :], shape) if j <= i else None for j in range(SUB)]
            for i in range(SUB)
        ]
        parts = [
            [jnp.broadcast_to(source[i : i + 1, :], shape) for i in range(SUB)]
            for source in (rows[k], right[k])
        ]
        pairs = []
        for p in range(0, SUB, 2):
            q = p + 1
            a, b, c = entry[p][p], entry[q][p], entry[q][q]
            det = a * c - b * b
            root = lax.rsqrt(det)
            over = root * root
            scaled = {}
            for i in range(q + 1, SUB):
                first = c * entry[i][p] - b * entry[i][q]
                second = a * entry[i][q] - b * entry[i][p]
                scaled[i] = (first * over, second * over)
                for t in range(q + 1, i + 1):
                    entry[i][t] = entry[i][t] - (first * entry[t][p] + second * entry[t][q]) * over
                for part in parts:
                    part[i] = part[i] - (scaled[i][0] * part[p] + scaled[i][1] * part[q])
            pairs.append((p, a, b, c, root, over, scaled))
        packed = [None, None]
        backs = []
        for at, part in enumerate(parts):
            back = [None] * SUB
            for p, a, b, c, root, over, scaled in reversed(pairs):
                q = p + 1
                one = (c * part[p] - b * part[q]) * over
                two = (a * part[q] - b * part[p]) * over
                if scaled:
                    one = one - tree([scaled[i][0] * back[i] for i in scaled])
                    two = two - tree([scaled[i][1] * back[i] for i in scaled])
                back[p], back[q] = one, two
            backs.append(back)
            for p, a, b, c, root, over, scaled in pairs:
                first_root = lax.rsqrt(a)
                high = part[p] * first_root
                low = (a * part[p + 1] - b * part[p]) * (first_root * root)
                packed[at] = high if packed[at] is None else jnp.where(sub == p, high, packed[at])
                packed[at] = jnp.where(sub == p + 1, low, packed[at])
        upper.append(packed[0])
        inverse.append(packed[1])
        for r in range(k + 1, strips):
            columns = [
                jnp.broadcast_to(rows[r][:, k * SUB + i : k * SUB + i + 1], shape) for i in range(SUB)
            ]
            rows[r] = rows[r] - tree([backs[0][i] * columns[i] for i in range(SUB)])
            right[r] = right[r] - tree([backs[1][i] * columns[i] for i in range(SUB)])
    return upper, inverse


def factor_into(work, right, upper_ref, inv_ref):
    half = work.shape[0]
    strips = half // SUB
    row = lax.broadcasted_iota(jnp.int32, (half, half), 0)
    col = lax.broadcasted_iota(jnp.int32, (half, half), 1)
    whole = work[...]
    diagonal = jnp.where(row == col, whole, 0.0)
    across = jnp.sum(diagonal, axis=0, keepdims=True)
    scale = lax.rsqrt(across)
    work[...] = whole * lax.rsqrt(jnp.sum(diagonal, axis=1, keepdims=True)) * scale
    rows = [work[SUB * s : SUB * (s + 1), :] for s in range(strips)]
    eye = (row == col).astype(jnp.float32)
    beside = [eye[SUB * s : SUB * (s + 1), :] for s in range(strips)]
    upper, inverse = factor_block(rows, beside)
    for s in range(strips):
        work[SUB * s : SUB * (s + 1), :] = upper[s]
        right[SUB * s : SUB * (s + 1), :] = inverse[s]
    upper_ref[...] = jnp.where(col >= row, work[...] * (across * scale), 0.0)
    inv_ref[...] = jnp.where(col <= row, right[...] * scale, 0.0)


def first_kernel(place_ref, own_ref, other_ref, upper_ref, inv_ref, work, right):
    @pl.when(place_ref[0] == 0)
    def _():
        work[...] = own_ref[...]

    @pl.when(place_ref[0] != 0)
    def _():
        work[...] = other_ref[...]

    factor_into(work, right, upper_ref, inv_ref)


def second_kernel(place_ref, own_ref, other_ref, cross_ref, first_ref, first_inv_ref, upper_ref, inv_ref, work, right):
    half = own_ref.shape[0]
    across = dot_full(first_inv_ref[...], cross_ref[...])
    update = dot_full(across, across, ((0,), (0,)))

    @pl.when(place_ref[0] == 0)
    def _():
        work[...] = other_ref[...] - update

    @pl.when(place_ref[0] != 0)
    def _():
        work[...] = own_ref[...] - update

    zero = jnp.zeros((half, half), jnp.float32)
    upper_ref[0:half, 0:half] = first_ref[...]
    upper_ref[0:half, half:] = across
    upper_ref[half:, 0:half] = zero
    inv_ref[0:half, 0:half] = first_inv_ref[...]
    inv_ref[0:half, half:] = zero
    between = dot_full(across, first_inv_ref[...], ((0,), (0,)))
    factor_into(work, right, upper_ref.at[half:, half:], inv_ref.at[half:, half:])
    inv_ref[half:, 0:half] = -dot_full(inv_ref[half:, half:], between)


def factorize(place, own, other, cross):
    half = own.shape[0]
    smem = [pl.BlockSpec(memory_space=pltpu.SMEM)]
    tile = jax.ShapeDtypeStruct((half, half), jnp.float32)
    scratch = [pltpu.VMEM((half, half), jnp.float32)] * 2
    params = pltpu.CompilerParams(vmem_limit_bytes=24 << 20)
    first, first_inv = pl.pallas_call(
        first_kernel,
        out_shape=[tile] * 2,
        in_specs=smem + vmem(2),
        out_specs=vmem(2),
        scratch_shapes=scratch,
        compiler_params=params,
        cost_estimate=pl.CostEstimate(flops=2 * half**3, bytes_accessed=1 << 24, transcendentals=half),
    )(place, own, other)
    return pl.pallas_call(
        second_kernel,
        out_shape=[jax.ShapeDtypeStruct((2 * half, 2 * half), jnp.float32)] * 2,
        in_specs=smem + vmem(5),
        out_specs=vmem(2),
        scratch_shapes=scratch,
        compiler_params=params,
    )(place, own, other, cross, first, first_inv)


def basis_kernel(place_ref, inv_ref, own_ref, other_ref, out_ref):
    half, total = out_ref.shape
    place = place_ref[0]
    rows = pl.ds(pl.multiple_of(place * half, half), half)
    away = pl.ds(pl.multiple_of((1 - place) * half, half), half)
    near_high, near_low = split(inv_ref[rows, rows])
    far_high, far_low = split(inv_ref[rows, away])
    both_high = jnp.concatenate([near_high, far_high], axis=1)
    both_low = jnp.concatenate([near_low, far_low], axis=1)
    step = 512 if total % 512 == 0 else total
    for at in range(0, total, step):
        here = slice(at, at + step)
        high, low = split(own_ref[:, here])
        both = jnp.concatenate([high, other_ref[:, here]], axis=0)
        out_ref[:, here] = (
            jnp.dot(both_high, both, preferred_element_type=jnp.float32)
            + jnp.dot(both_low, both, preferred_element_type=jnp.float32)
            + jnp.dot(near_high, low, preferred_element_type=jnp.float32)
        )


def shards(hamiltonian, orbitals, adjacency):
    count = hamiltonian.shape[0]
    owned = orbitals.shape[0]
    blocks = lax.axis_size("space")
    groups = lax.axis_size("orb")
    half = owned * groups // 2
    odd = lax.axis_index("space").astype(jnp.int32).reshape(1) % 2
    loc = adjacency % count
    swapped = jnp.concatenate([loc[:, 1:2], loc[:, 0:1], loc[:, 2:]], axis=1)
    loc = jnp.where(odd[0] == 1, loc, swapped)
    near_pairs = [(i, i ^ 1) for i in range(blocks)]
    far_pairs = [(i, (i + 1 if i % 2 else i - 1) % blocks) for i in range(blocks)]
    smem = [pl.BlockSpec(memory_space=pltpu.SMEM)]

    def halo(vec):
        far = lax.ppermute(vec, "space", far_pairs)
        return lax.ppermute(vec, "space", near_pairs), far

    side = halo(orbitals)
    turned, acc = turn_part(orbitals, hamiltonian, loc, odd)
    (one,) = halo_part(1, *side, acc, orbitals, orbitals, turned, loc)
    side = halo(one)
    (two,) = halo_part(2, *side, own_part(one, turned, loc), one, orbitals, turned, loc)
    side = halo(two)
    filtered, narrow = halo_part(3, *side, own_part(two, turned, loc), two, one, turned, loc)

    def summed(part):
        step = 1
        while step < blocks:
            part = part + lax.ppermute(part, "space", [(i, i ^ step) for i in range(blocks)])
            step *= 2
        return part

    place = lax.axis_index("orb").astype(jnp.int32).reshape(1)
    if groups == 2:
        swap = [(0, 1), (1, 0)]
        other = lax.ppermute(narrow, "orb", swap)
        tile = jax.ShapeDtypeStruct((half, half), jnp.float32)
        params = pltpu.CompilerParams(vmem_limit_bytes=24 << 20)
        near = pl.pallas_call(
            own_gram_kernel,
            out_shape=tile,
            in_specs=vmem(2),
            out_specs=pl.BlockSpec(memory_space=pltpu.VMEM),
            compiler_params=params,
        )(filtered, narrow)
        near = summed(near)
        far = lax.ppermute(near, "orb", swap)
        cross = pl.pallas_call(
            cross_gram_kernel,
            out_shape=tile,
            in_specs=smem + vmem(2),
            out_specs=pl.BlockSpec(memory_space=pltpu.VMEM),
            compiler_params=params,
        )(place, narrow, other)
        upper, inverse = factorize(place, near, far, summed(cross))
    else:
        columns = lax.all_gather(narrow, "orb", axis=0, tiled=True)
        whole = summed(dot_nt(columns, columns))
        upper, inverse = factorize(
            jnp.zeros_like(place), whole[:half, :half], whole[half:, half:], whole[:half, half:]
        )
    if groups == 2:
        basis = pl.pallas_call(
            basis_kernel,
            out_shape=jax.ShapeDtypeStruct(orbitals.shape, jnp.float32),
            in_specs=smem + vmem(3),
            out_specs=pl.BlockSpec(memory_space=pltpu.VMEM),
            compiler_params=pltpu.CompilerParams(vmem_limit_bytes=24 << 20),
        )(place, inverse, filtered, other)
    else:
        mine = lax.dynamic_slice_in_dim(inverse, place[0] * owned, owned, 0)
        near = lax.dynamic_slice_in_dim(mine, place[0] * owned, owned, 1)
        rest = filtered - narrow.astype(jnp.float32)
        basis = dot_full(mine, columns.astype(jnp.float32)) + dot_full(near, rest)
    return (basis, upper)


def solution(mesh):
    in_specs = (P("space", None, None, None), P("orb", "space"), P("space", None))
    out_specs = (P("orb", "space"), P())
    return jax.shard_map(shards, mesh=mesh, in_specs=in_specs, out_specs=out_specs, check_vma=False)
```

```python
import functools

import jax
import jax.numpy as jnp
from jax import lax
from jax.experimental import pallas as pl
from jax.experimental.pallas import tpu as pltpu
from jax.sharding import PartitionSpec as P

centre = 0.25
radius = 0.75
SUB = 8


def vmem(count):
    return [pl.BlockSpec(memory_space=pltpu.VMEM)] * count


def dot_nt(a, b):
    return lax.dot_general(a, b, (((1,), (1,)), ((), ())), preferred_element_type=jnp.float32)


def dot_full(a, b, dims=((1,), (0,))):
    return lax.dot_general(
        a, b, (dims, ((), ())), precision=lax.Precision.HIGHEST, preferred_element_type=jnp.float32
    )


def split(a):
    high = a.astype(jnp.bfloat16)
    return high, (a - high.astype(jnp.float32)).astype(jnp.bfloat16)


def turn_kernel(loc_ref, odd_ref, vec_ref, ham_ref, turned_ref, out_ref):
    count, faces, width, _ = ham_ref.shape
    odd = odd_ref[0]
    for e in range(count):
        here = slice(e * width, (e + 1) * width)
        total = None
        for face in range(faces):
            source = 2 - odd if face == 1 else 1 + odd if face == 2 else face
            turned = ham_ref[e, source].T
            turned_ref[e, face] = turned
            if face == 1 or face == 2:
                continue
            at = here if face == 0 else pl.ds(pl.multiple_of(loc_ref[e, face - 1] * width, width), width)
            part = jnp.dot(vec_ref[:, at], turned, preferred_element_type=jnp.float32)
            total = part if total is None else total + part
        out_ref[:, here] = total


def turn_part(vec, hamiltonian, loc, odd):
    count, faces, width, _ = hamiltonian.shape
    owned = vec.shape[0]
    return pl.pallas_call(
        turn_kernel,
        out_shape=[
            jax.ShapeDtypeStruct(hamiltonian.shape, hamiltonian.dtype),
            jax.ShapeDtypeStruct(vec.shape, jnp.float32),
        ],
        in_specs=[pl.BlockSpec(memory_space=pltpu.SMEM)] * 2 + vmem(2),
        out_specs=vmem(2),
        compiler_params=pltpu.CompilerParams(vmem_limit_bytes=32 << 20),
        cost_estimate=pl.CostEstimate(
            flops=2 * owned * count * width * width * 5,
            bytes_accessed=count * faces * width * width * 4,
            transcendentals=0,
        ),
    )(loc, odd, vec, hamiltonian)


def own_kernel(loc_ref, vec_ref, turned_ref, out_ref):
    count, _, width, _ = turned_ref.shape
    for e in range(count):
        here = slice(e * width, (e + 1) * width)
        total = jnp.dot(vec_ref[:, here], turned_ref[e, 0], preferred_element_type=jnp.float32)
        for face in range(2, 6):
            at = pl.ds(pl.multiple_of(loc_ref[e, face] * width, width), width)
            total += jnp.dot(
                vec_ref[:, at], turned_ref[e, face + 1], preferred_element_type=jnp.float32
            )
        out_ref[:, here] = total


def own_part(vec, turned, loc):
    count, _, width, _ = turned.shape
    owned = vec.shape[0]
    return pl.pallas_call(
        own_kernel,
        out_shape=jax.ShapeDtypeStruct(vec.shape, jnp.float32),
        in_specs=[pl.BlockSpec(memory_space=pltpu.SMEM)] + vmem(2),
        out_specs=pl.BlockSpec(memory_space=pltpu.VMEM),
        compiler_params=pltpu.CompilerParams(vmem_limit_bytes=24 << 20),
        cost_estimate=pl.CostEstimate(
            flops=2 * owned * count * width * width * 5,
            bytes_accessed=count * 5 * width * width * 2,
            transcendentals=0,
        ),
    )(loc, vec, turned)


def halo_kernel(level, loc_ref, near_ref, far_ref, acc_ref, vec_ref, prior_ref, turned_ref, *outs):
    count, _, width, _ = turned_ref.shape
    for e in range(count):
        here = slice(e * width, (e + 1) * width)
        total = acc_ref[:, here]
        for face, ref in enumerate((near_ref, far_ref)):
            at = pl.ds(pl.multiple_of(loc_ref[e, face] * width, width), width)
            total += jnp.dot(
                ref[:, at], turned_ref[e, face + 1], preferred_element_type=jnp.float32
            )
        shifted = (total - centre * vec_ref[:, here].astype(jnp.float32)) * (1.0 / radius)
        if level > 1:
            shifted = 2.0 * shifted - prior_ref[:, here].astype(jnp.float32)
        for out in outs:
            out[:, here] = shifted.astype(out.dtype)


def halo_part(level, near, far, acc, vec, prior, turned, loc):
    count, _, width, _ = turned.shape
    owned = vec.shape[0]
    kinds = [jnp.bfloat16] if level < 3 else [jnp.float32, jnp.bfloat16]
    return pl.pallas_call(
        functools.partial(halo_kernel, level),
        out_shape=[jax.ShapeDtypeStruct(vec.shape, kind) for kind in kinds],
        in_specs=[pl.BlockSpec(memory_space=pltpu.SMEM)] + vmem(6),
        out_specs=vmem(len(kinds)),
        compiler_params=pltpu.CompilerParams(vmem_limit_bytes=24 << 20),
        cost_estimate=pl.CostEstimate(
            flops=2 * owned * count * width * width * 2,
            bytes_accessed=count * 2 * width * width * 2,
            transcendentals=0,
        ),
    )(loc, near, far, acc, vec, prior, turned)


def own_gram_kernel(own_ref, high_ref, out_ref):
    high = high_ref[...]
    low = (own_ref[...] - high.astype(jnp.float32)).astype(jnp.bfloat16)
    mixed = dot_nt(high, low)
    out_ref[...] = dot_nt(high, high) + (mixed + mixed.T)


def cross_gram_kernel(place_ref, own_ref, other_ref, after_ref, out_ref):
    del after_ref

    @pl.when(place_ref[0] == 0)
    def _():
        out_ref[...] = dot_nt(own_ref[...], other_ref[...])

    @pl.when(place_ref[0] != 0)
    def _():
        out_ref[...] = dot_nt(other_ref[...], own_ref[...])


def tree(terms):
    while len(terms) > 1:
        terms = [terms[i] + terms[i + 1] if i + 1 < len(terms) else terms[i] for i in range(0, len(terms), 2)]
    return terms[0]


def factor_block(rows, right):
    strips = len(rows)
    shape = rows[0].shape
    sub = lax.broadcasted_iota(jnp.int32, shape, 0)
    upper, inverse = [], []
    for k in range(strips):
        lanes = [
            jnp.broadcast_to(rows[k][:, k * SUB + j : k * SUB + j + 1], shape) for j in range(SUB)
        ]
        entry = [
            [jnp.broadcast_to(lanes[j][i : i + 1, :], shape) if j <= i else None for j in range(SUB)]
            for i in range(SUB)
        ]
        parts = [
            [jnp.broadcast_to(source[i : i + 1, :], shape) for i in range(SUB)]
            for source in (rows[k], right[k])
        ]
        pairs = []
        for p in range(0, SUB, 2):
            q = p + 1
            a, b, c = entry[p][p], entry[q][p], entry[q][q]
            det = a * c - b * b
            root = lax.rsqrt(det)
            over = root * root
            scaled = {}
            for i in range(q + 1, SUB):
                first = c * entry[i][p] - b * entry[i][q]
                second = a * entry[i][q] - b * entry[i][p]
                scaled[i] = (first * over, second * over)
                for t in range(q + 1, i + 1):
                    entry[i][t] = entry[i][t] - (first * entry[t][p] + second * entry[t][q]) * over
                for part in parts:
                    part[i] = part[i] - (scaled[i][0] * part[p] + scaled[i][1] * part[q])
            pairs.append((p, a, b, c, root, over, scaled))
        packed = [None, None]
        backs = []
        for at, part in enumerate(parts):
            back = [None] * SUB
            for p, a, b, c, root, over, scaled in reversed(pairs):
                q = p + 1
                one = (c * part[p] - b * part[q]) * over
                two = (a * part[q] - b * part[p]) * over
                if scaled:
                    one = one - tree([scaled[i][0] * back[i] for i in scaled])
                    two = two - tree([scaled[i][1] * back[i] for i in scaled])
                back[p], back[q] = one, two
            backs.append(back)
            for p, a, b, c, root, over, scaled in pairs:
                first_root = lax.rsqrt(a)
                high = part[p] * first_root
                low = (a * part[p + 1] - b * part[p]) * (first_root * root)
                packed[at] = high if packed[at] is None else jnp.where(sub == p, high, packed[at])
                packed[at] = jnp.where(sub == p + 1, low, packed[at])
        upper.append(packed[0])
        inverse.append(packed[1])
        for r in range(k + 1, strips):
            columns = [
                jnp.broadcast_to(rows[r][:, k * SUB + i : k * SUB + i + 1], shape) for i in range(SUB)
            ]
            rows[r] = rows[r] - tree([backs[0][i] * columns[i] for i in range(SUB)])
            right[r] = right[r] - tree([backs[1][i] * columns[i] for i in range(SUB)])
    return upper, inverse


def factor_into(work, right, upper_ref, inv_ref):
    half = work.shape[0]
    strips = half // SUB
    row = lax.broadcasted_iota(jnp.int32, (half, half), 0)
    col = lax.broadcasted_iota(jnp.int32, (half, half), 1)
    whole = work[...]
    diagonal = jnp.where(row == col, whole, 0.0)
    across = jnp.sum(diagonal, axis=0, keepdims=True)
    scale = lax.rsqrt(across)
    work[...] = whole * lax.rsqrt(jnp.sum(diagonal, axis=1, keepdims=True)) * scale
    rows = [work[SUB * s : SUB * (s + 1), :] for s in range(strips)]
    eye = (row == col).astype(jnp.float32)
    beside = [eye[SUB * s : SUB * (s + 1), :] for s in range(strips)]
    upper, inverse = factor_block(rows, beside)
    for s in range(strips):
        work[SUB * s : SUB * (s + 1), :] = upper[s]
        right[SUB * s : SUB * (s + 1), :] = inverse[s]
    upper_ref[...] = jnp.where(col >= row, work[...] * (across * scale), 0.0)
    inv_ref[...] = jnp.where(col <= row, right[...] * scale, 0.0)


def first_kernel(place_ref, own_ref, other_ref, after_ref, upper_ref, inv_ref, work, right):
    del after_ref

    @pl.when(place_ref[0] == 0)
    def _():
        work[...] = own_ref[...]

    @pl.when(place_ref[0] != 0)
    def _():
        work[...] = other_ref[...]

    factor_into(work, right, upper_ref, inv_ref)


def second_kernel(place_ref, own_ref, other_ref, cross_ref, first_ref, first_inv_ref, upper_ref, inv_ref, work, right):
    half = own_ref.shape[0]
    across = dot_full(first_inv_ref[...], cross_ref[...])
    update = dot_full(across, across, ((0,), (0,)))

    @pl.when(place_ref[0] == 0)
    def _():
        work[...] = other_ref[...] - update

    @pl.when(place_ref[0] != 0)
    def _():
        work[...] = own_ref[...] - update

    zero = jnp.zeros((half, half), jnp.float32)
    upper_ref[0:half, 0:half] = first_ref[...]
    upper_ref[0:half, half:] = across
    upper_ref[half:, 0:half] = zero
    inv_ref[0:half, 0:half] = first_inv_ref[...]
    inv_ref[0:half, half:] = zero
    between = dot_full(across, first_inv_ref[...], ((0,), (0,)))
    factor_into(work, right, upper_ref.at[half:, half:], inv_ref.at[half:, half:])
    inv_ref[half:, 0:half] = -dot_full(inv_ref[half:, half:], between)


def factorize(place, own, other, cross, after):
    half = own.shape[0]
    smem = [pl.BlockSpec(memory_space=pltpu.SMEM)]
    tile = jax.ShapeDtypeStruct((half, half), jnp.float32)
    scratch = [pltpu.VMEM((half, half), jnp.float32)] * 2
    params = pltpu.CompilerParams(vmem_limit_bytes=24 << 20)
    first, first_inv = pl.pallas_call(
        first_kernel,
        out_shape=[tile] * 2,
        in_specs=smem + vmem(2) + [pl.BlockSpec(memory_space=pl.ANY)],
        out_specs=vmem(2),
        scratch_shapes=scratch,
        compiler_params=params,
        cost_estimate=pl.CostEstimate(flops=2 * half**3, bytes_accessed=1 << 24, transcendentals=half),
    )(place, own, other, after)
    return pl.pallas_call(
        second_kernel,
        out_shape=[jax.ShapeDtypeStruct((2 * half, 2 * half), jnp.float32)] * 2,
        in_specs=smem + vmem(5),
        out_specs=vmem(2),
        scratch_shapes=scratch,
        compiler_params=params,
    )(place, own, other, cross, first, first_inv)


def basis_kernel(place_ref, inv_ref, own_ref, other_ref, out_ref):
    half, total = out_ref.shape
    place = place_ref[0]
    rows = pl.ds(pl.multiple_of(place * half, half), half)
    away = pl.ds(pl.multiple_of((1 - place) * half, half), half)
    near_high, near_low = split(inv_ref[rows, rows])
    far_high, far_low = split(inv_ref[rows, away])
    both_high = jnp.concatenate([near_high, far_high], axis=1)
    both_low = jnp.concatenate([near_low, far_low], axis=1)
    step = 512 if total % 512 == 0 else total
    for at in range(0, total, step):
        here = slice(at, at + step)
        high, low = split(own_ref[:, here])
        both = jnp.concatenate([high, other_ref[:, here]], axis=0)
        out_ref[:, here] = (
            jnp.dot(both_high, both, preferred_element_type=jnp.float32)
            + jnp.dot(both_low, both, preferred_element_type=jnp.float32)
            + jnp.dot(near_high, low, preferred_element_type=jnp.float32)
        )


def shards(hamiltonian, orbitals, adjacency):
    count = hamiltonian.shape[0]
    owned = orbitals.shape[0]
    blocks = lax.axis_size("space")
    groups = lax.axis_size("orb")
    half = owned * groups // 2
    odd = lax.axis_index("space").astype(jnp.int32).reshape(1) % 2
    loc = adjacency % count
    swapped = jnp.concatenate([loc[:, 1:2], loc[:, 0:1], loc[:, 2:]], axis=1)
    loc = jnp.where(odd[0] == 1, loc, swapped)
    near_pairs = [(i, i ^ 1) for i in range(blocks)]
    far_pairs = [(i, (i + 1 if i % 2 else i - 1) % blocks) for i in range(blocks)]
    smem = [pl.BlockSpec(memory_space=pltpu.SMEM)]

    def halo(vec):
        far = lax.ppermute(vec, "space", far_pairs)
        return lax.ppermute(vec, "space", near_pairs), far

    side = halo(orbitals)
    turned, acc = turn_part(orbitals, hamiltonian, loc, odd)
    (one,) = halo_part(1, *side, acc, orbitals, orbitals, turned, loc)
    side = halo(one)
    (two,) = halo_part(2, *side, own_part(one, turned, loc), one, orbitals, turned, loc)
    side = halo(two)
    filtered, narrow = halo_part(3, *side, own_part(two, turned, loc), two, one, turned, loc)

    steps = [1 << i for i in range((blocks - 1).bit_length())]
    stages = [steps[:1]] + [steps[i : i + 2] for i in range(1, len(steps), 2)]

    def summed(part, chosen):
        def moved(step):
            return lax.ppermute(part, "space", [(i, i ^ step) for i in range(blocks)])

        for stage in chosen:
            if len(stage) == 1:
                part = part + moved(stage[0])
            else:
                one, two = stage
                part = (part + moved(one)) + (moved(two) + moved(one ^ two))
        return part

    place = lax.axis_index("orb").astype(jnp.int32).reshape(1)
    if groups == 2:
        swap = [(0, 1), (1, 0)]
        other = lax.ppermute(narrow, "orb", swap)
        tile = jax.ShapeDtypeStruct((half, half), jnp.float32)
        params = pltpu.CompilerParams(vmem_limit_bytes=24 << 20)
        near = pl.pallas_call(
            own_gram_kernel,
            out_shape=tile,
            in_specs=vmem(2),
            out_specs=pl.BlockSpec(memory_space=pltpu.VMEM),
            compiler_params=params,
        )(filtered, narrow)
        near = summed(near, stages[:-1])
        cross = pl.pallas_call(
            cross_gram_kernel,
            out_shape=tile,
            in_specs=smem + vmem(2) + [pl.BlockSpec(memory_space=pl.ANY)],
            out_specs=pl.BlockSpec(memory_space=pltpu.VMEM),
            compiler_params=params,
        )(place, narrow, other, near)
        near = summed(near, stages[-1:])
        far = lax.ppermute(near, "orb", swap)
        cross = summed(cross, stages[:-1])
        upper, inverse = factorize(place, near, far, summed(cross, stages[-1:]), cross)
    else:
        columns = lax.all_gather(narrow, "orb", axis=0, tiled=True)
        whole = summed(dot_nt(columns, columns), stages)
        upper, inverse = factorize(
            jnp.zeros_like(place), whole[:half, :half], whole[half:, half:], whole[:half, half:], whole
        )
    if groups == 2:
        basis = pl.pallas_call(
            basis_kernel,
            out_shape=jax.ShapeDtypeStruct(orbitals.shape, jnp.float32),
            in_specs=smem + vmem(3),
            out_specs=pl.BlockSpec(memory_space=pltpu.VMEM),
            compiler_params=pltpu.CompilerParams(vmem_limit_bytes=24 << 20),
        )(place, inverse, filtered, other)
    else:
        mine = lax.dynamic_slice_in_dim(inverse, place[0] * owned, owned, 0)
        near = lax.dynamic_slice_in_dim(mine, place[0] * owned, owned, 1)
        rest = filtered - narrow.astype(jnp.float32)
        basis = dot_full(mine, columns.astype(jnp.float32)) + dot_full(near, rest)
    return (basis, upper)


def solution(mesh):
    in_specs = (P("space", None, None, None), P("orb", "space"), P("space", None))
    out_specs = (P("orb", "space"), P())
    return jax.shard_map(shards, mesh=mesh, in_specs=in_specs, out_specs=out_specs, check_vma=False)
```

```python
import functools

import jax
import jax.numpy as jnp
from jax import lax
from jax.experimental import pallas as pl
from jax.experimental.pallas import tpu as pltpu
from jax.sharding import PartitionSpec as P

centre = 0.25
radius = 0.75
SUB = 8


def vmem(count):
    return [pl.BlockSpec(memory_space=pltpu.VMEM)] * count


def dot_nt(a, b):
    return lax.dot_general(a, b, (((1,), (1,)), ((), ())), preferred_element_type=jnp.float32)


def dot_full(a, b, dims=((1,), (0,))):
    return lax.dot_general(
        a, b, (dims, ((), ())), precision=lax.Precision.HIGHEST, preferred_element_type=jnp.float32
    )


def split(a):
    high = a.astype(jnp.bfloat16)
    return high, (a - high.astype(jnp.float32)).astype(jnp.bfloat16)


def turn_kernel(loc_ref, odd_ref, vec_ref, ham_ref, turned_ref, out_ref):
    count, faces, width, _ = ham_ref.shape
    odd = odd_ref[0]
    for e in range(count):
        here = slice(e * width, (e + 1) * width)
        total = None
        for face in range(faces):
            source = 2 - odd if face == 1 else 1 + odd if face == 2 else face
            turned = ham_ref[e, source].T
            turned_ref[e, face] = turned
            if face == 1 or face == 2:
                continue
            at = here if face == 0 else pl.ds(pl.multiple_of(loc_ref[e, face - 1] * width, width), width)
            part = jnp.dot(vec_ref[:, at], turned, preferred_element_type=jnp.float32)
            total = part if total is None else total + part
        out_ref[:, here] = total


def turn_part(vec, hamiltonian, loc, odd):
    count, faces, width, _ = hamiltonian.shape
    owned = vec.shape[0]
    return pl.pallas_call(
        turn_kernel,
        out_shape=[
            jax.ShapeDtypeStruct(hamiltonian.shape, hamiltonian.dtype),
            jax.ShapeDtypeStruct(vec.shape, jnp.float32),
        ],
        in_specs=[pl.BlockSpec(memory_space=pltpu.SMEM)] * 2 + vmem(2),
        out_specs=vmem(2),
        compiler_params=pltpu.CompilerParams(vmem_limit_bytes=32 << 20),
        cost_estimate=pl.CostEstimate(
            flops=2 * owned * count * width * width * 5,
            bytes_accessed=count * faces * width * width * 4,
            transcendentals=0,
        ),
    )(loc, odd, vec, hamiltonian)


def own_kernel(loc_ref, vec_ref, turned_ref, out_ref):
    count, _, width, _ = turned_ref.shape
    for e in range(count):
        here = slice(e * width, (e + 1) * width)
        total = jnp.dot(vec_ref[:, here], turned_ref[e, 0], preferred_element_type=jnp.float32)
        for face in range(2, 6):
            at = pl.ds(pl.multiple_of(loc_ref[e, face] * width, width), width)
            total += jnp.dot(
                vec_ref[:, at], turned_ref[e, face + 1], preferred_element_type=jnp.float32
            )
        out_ref[:, here] = total


def own_part(vec, turned, loc):
    count, _, width, _ = turned.shape
    owned = vec.shape[0]
    return pl.pallas_call(
        own_kernel,
        out_shape=jax.ShapeDtypeStruct(vec.shape, jnp.float32),
        in_specs=[pl.BlockSpec(memory_space=pltpu.SMEM)] + vmem(2),
        out_specs=pl.BlockSpec(memory_space=pltpu.VMEM),
        compiler_params=pltpu.CompilerParams(vmem_limit_bytes=24 << 20),
        cost_estimate=pl.CostEstimate(
            flops=2 * owned * count * width * width * 5,
            bytes_accessed=count * 5 * width * width * 2,
            transcendentals=0,
        ),
    )(loc, vec, turned)


def halo_kernel(level, loc_ref, near_ref, far_ref, acc_ref, vec_ref, prior_ref, turned_ref, *outs):
    count, _, width, _ = turned_ref.shape
    for e in range(count):
        here = slice(e * width, (e + 1) * width)
        total = acc_ref[:, here]
        for face, ref in enumerate((near_ref, far_ref)):
            at = pl.ds(pl.multiple_of(loc_ref[e, face] * width, width), width)
            total += jnp.dot(
                ref[:, at], turned_ref[e, face + 1], preferred_element_type=jnp.float32
            )
        shifted = (total - centre * vec_ref[:, here].astype(jnp.float32)) * (1.0 / radius)
        if level > 1:
            shifted = 2.0 * shifted - prior_ref[:, here].astype(jnp.float32)
        for out in outs:
            out[:, here] = shifted.astype(out.dtype)


def halo_part(level, near, far, acc, vec, prior, turned, loc):
    count, _, width, _ = turned.shape
    owned = vec.shape[0]
    kinds = [jnp.bfloat16] if level < 3 else [jnp.float32, jnp.bfloat16]
    return pl.pallas_call(
        functools.partial(halo_kernel, level),
        out_shape=[jax.ShapeDtypeStruct(vec.shape, kind) for kind in kinds],
        in_specs=[pl.BlockSpec(memory_space=pltpu.SMEM)] + vmem(6),
        out_specs=vmem(len(kinds)),
        compiler_params=pltpu.CompilerParams(vmem_limit_bytes=24 << 20),
        cost_estimate=pl.CostEstimate(
            flops=2 * owned * count * width * width * 2,
            bytes_accessed=count * 2 * width * width * 2,
            transcendentals=0,
        ),
    )(loc, near, far, acc, vec, prior, turned)


def own_gram_kernel(own_ref, high_ref, out_ref):
    high = high_ref[...]
    low = (own_ref[...] - high.astype(jnp.float32)).astype(jnp.bfloat16)
    mixed = dot_nt(high, low)
    out_ref[...] = dot_nt(high, high) + (mixed + mixed.T)


def cross_gram_kernel(place_ref, own_ref, other_ref, after_ref, out_ref):
    del after_ref

    @pl.when(place_ref[0] == 0)
    def _():
        out_ref[...] = dot_nt(other_ref[...], own_ref[...])

    @pl.when(place_ref[0] != 0)
    def _():
        out_ref[...] = dot_nt(own_ref[...], other_ref[...])


def tree(terms):
    while len(terms) > 1:
        terms = [terms[i] + terms[i + 1] if i + 1 < len(terms) else terms[i] for i in range(0, len(terms), 2)]
    return terms[0]


def factor_block(rows, right):
    strips = len(rows)
    shape = rows[0].shape
    sub = lax.broadcasted_iota(jnp.int32, shape, 0)
    upper, inverse = [], []
    for k in range(strips):
        lanes = [
            jnp.broadcast_to(rows[k][:, k * SUB + j : k * SUB + j + 1], shape) for j in range(SUB)
        ]
        entry = [
            [jnp.broadcast_to(lanes[j][i : i + 1, :], shape) if j <= i else None for j in range(SUB)]
            for i in range(SUB)
        ]
        parts = [
            [jnp.broadcast_to(source[i : i + 1, :], shape) for i in range(SUB)]
            for source in (rows[k], right[k])
        ]
        pairs = []
        for p in range(0, SUB, 2):
            q = p + 1
            a, b, c = entry[p][p], entry[q][p], entry[q][q]
            det = a * c - b * b
            root = lax.rsqrt(det)
            over = root * root
            scaled = {}
            for i in range(q + 1, SUB):
                first = c * entry[i][p] - b * entry[i][q]
                second = a * entry[i][q] - b * entry[i][p]
                scaled[i] = (first * over, second * over)
                for t in range(q + 1, i + 1):
                    entry[i][t] = entry[i][t] - (first * entry[t][p] + second * entry[t][q]) * over
                for part in parts:
                    part[i] = part[i] - (scaled[i][0] * part[p] + scaled[i][1] * part[q])
            pairs.append((p, a, b, c, root, over, scaled))
        packed = [None, None]
        backs = []
        for at, part in enumerate(parts):
            back = [None] * SUB
            for p, a, b, c, root, over, scaled in reversed(pairs):
                q = p + 1
                one = (c * part[p] - b * part[q]) * over
                two = (a * part[q] - b * part[p]) * over
                if scaled:
                    one = one - tree([scaled[i][0] * back[i] for i in scaled])
                    two = two - tree([scaled[i][1] * back[i] for i in scaled])
                back[p], back[q] = one, two
            backs.append(back)
            for p, a, b, c, root, over, scaled in pairs:
                first_root = lax.rsqrt(a)
                high = part[p] * first_root
                low = (a * part[p + 1] - b * part[p]) * (first_root * root)
                packed[at] = high if packed[at] is None else jnp.where(sub == p, high, packed[at])
                packed[at] = jnp.where(sub == p + 1, low, packed[at])
        upper.append(packed[0])
        inverse.append(packed[1])
        for r in range(k + 1, strips):
            columns = [
                jnp.broadcast_to(rows[r][:, k * SUB + i : k * SUB + i + 1], shape) for i in range(SUB)
            ]
            rows[r] = rows[r] - tree([backs[0][i] * columns[i] for i in range(SUB)])
            right[r] = right[r] - tree([backs[1][i] * columns[i] for i in range(SUB)])
    return upper, inverse


def factor_into(work, right, upper_ref, inv_ref):
    half = work.shape[0]
    strips = half // SUB
    row = lax.broadcasted_iota(jnp.int32, (half, half), 0)
    col = lax.broadcasted_iota(jnp.int32, (half, half), 1)
    whole = work[...]
    diagonal = jnp.where(row == col, whole, 0.0)
    across = jnp.sum(diagonal, axis=0, keepdims=True)
    scale = lax.rsqrt(across)
    work[...] = whole * lax.rsqrt(jnp.sum(diagonal, axis=1, keepdims=True)) * scale
    rows = [work[SUB * s : SUB * (s + 1), :] for s in range(strips)]
    eye = (row == col).astype(jnp.float32)
    beside = [eye[SUB * s : SUB * (s + 1), :] for s in range(strips)]
    upper, inverse = factor_block(rows, beside)
    for s in range(strips):
        work[SUB * s : SUB * (s + 1), :] = upper[s]
        right[SUB * s : SUB * (s + 1), :] = inverse[s]
    upper_ref[...] = jnp.where(col >= row, work[...] * (across * scale), 0.0)
    inv_ref[...] = jnp.where(col <= row, right[...] * scale, 0.0)


def first_kernel(place_ref, own_ref, other_ref, after_ref, upper_ref, inv_ref, work, right):
    del after_ref

    @pl.when(place_ref[0] == 0)
    def _():
        work[...] = own_ref[...]

    @pl.when(place_ref[0] != 0)
    def _():
        work[...] = other_ref[...]

    factor_into(work, right, upper_ref, inv_ref)


def second_kernel(place_ref, own_ref, other_ref, cross_ref, first_ref, first_inv_ref, upper_ref, inv_ref, work, right):
    half = own_ref.shape[0]
    across = dot_full(first_inv_ref[...], cross_ref[...])
    update = dot_full(across, across, ((0,), (0,)))

    @pl.when(place_ref[0] == 0)
    def _():
        work[...] = other_ref[...] - update

    @pl.when(place_ref[0] != 0)
    def _():
        work[...] = own_ref[...] - update

    zero = jnp.zeros((half, half), jnp.float32)
    upper_ref[0:half, 0:half] = first_ref[...]
    upper_ref[0:half, half:] = across
    upper_ref[half:, 0:half] = zero
    inv_ref[0:half, 0:half] = first_inv_ref[...]
    inv_ref[0:half, half:] = zero
    between = dot_full(across, first_inv_ref[...], ((0,), (0,)))
    factor_into(work, right, upper_ref.at[half:, half:], inv_ref.at[half:, half:])
    inv_ref[half:, 0:half] = -dot_full(inv_ref[half:, half:], between)


def factor_first(place, own, other, after):
    half = own.shape[0]
    return pl.pallas_call(
        first_kernel,
        out_shape=[jax.ShapeDtypeStruct((half, half), jnp.float32)] * 2,
        in_specs=[pl.BlockSpec(memory_space=pltpu.SMEM)]
        + vmem(2)
        + [pl.BlockSpec(memory_space=pl.ANY)],
        out_specs=vmem(2),
        scratch_shapes=[pltpu.VMEM((half, half), jnp.float32)] * 2,
        compiler_params=pltpu.CompilerParams(vmem_limit_bytes=24 << 20),
        cost_estimate=pl.CostEstimate(flops=2 * half**3, bytes_accessed=1 << 24, transcendentals=half),
    )(place, own, other, after)


def factor_second(place, own, other, cross, first, first_inv):
    half = own.shape[0]
    return pl.pallas_call(
        second_kernel,
        out_shape=[jax.ShapeDtypeStruct((2 * half, 2 * half), jnp.float32)] * 2,
        in_specs=[pl.BlockSpec(memory_space=pltpu.SMEM)] + vmem(5),
        out_specs=vmem(2),
        scratch_shapes=[pltpu.VMEM((half, half), jnp.float32)] * 2,
        compiler_params=pltpu.CompilerParams(vmem_limit_bytes=24 << 20),
    )(place, own, other, cross, first, first_inv)


def finish_kernel(
    place_ref, own_ref, other_ref, cross_ref, first_ref, first_inv_ref, wide_ref, high_ref, away_ref,
    upper_ref, basis_ref, work, right, inverse, part, result, sems,
):
    half, total = wide_ref.shape
    pieces = sems.shape[0]
    spans = [slice(i * (total // pieces), (i + 1) * (total // pieces)) for i in range(pieces)]
    leading = place_ref[0] == 0
    trailing = place_ref[0] != 0
    copies = [
        pltpu.make_async_copy(result.at[:, here], basis_ref.at[:, here], sems.at[i])
        for i, here in enumerate(spans)
    ]

    def dot(a, b):
        return jnp.dot(a, b, preferred_element_type=jnp.float32)

    lower = dot_full(cross_ref[...], first_inv_ref[...], ((1,), (1,)))
    update = dot_full(lower, lower, ((1,), (1,)))

    @pl.when(leading)
    def _():
        work[...] = other_ref[...] - update
        high_inv, low_inv = split(first_inv_ref[...])
        for copy, here in zip(copies, spans):
            high = high_ref[:, here]
            low = (wide_ref[:, here] - high.astype(jnp.float32)).astype(jnp.bfloat16)
            result[:, here] = dot(high_inv, high) + (dot(high_inv, low) + dot(low_inv, high))
            copy.start()

    @pl.when(trailing)
    def _():
        work[...] = own_ref[...] - update
        high_mix, low_mix = split(dot_full(lower, first_inv_ref[...]))
        for here in spans:
            away = away_ref[:, here]
            part[:, here] = wide_ref[:, here] - (dot(high_mix, away) + dot(low_mix, away))

    upper_ref[0:half, 0:half] = first_ref[...]
    upper_ref[0:half, half:] = lower.T
    upper_ref[half:, 0:half] = jnp.zeros((half, half), jnp.float32)
    factor_into(work, right, upper_ref.at[half:, half:], inverse)

    @pl.when(trailing)
    def _():
        high_inv, low_inv = split(inverse[...])
        for copy, here in zip(copies, spans):
            high, low = split(part[:, here])
            result[:, here] = dot(high_inv, high) + (dot(high_inv, low) + dot(low_inv, high))
            copy.start()

    for copy in copies:
        copy.wait()


def finish(place, own, other, cross, first, first_inv, wide, high, away):
    half, total = wide.shape
    pieces = 4 if total % 512 == 0 else 1
    tile = pltpu.VMEM((half, half), jnp.float32)
    return pl.pallas_call(
        finish_kernel,
        out_shape=[
            jax.ShapeDtypeStruct((2 * half, 2 * half), jnp.float32),
            jax.ShapeDtypeStruct(wide.shape, jnp.float32),
        ],
        in_specs=[pl.BlockSpec(memory_space=pltpu.SMEM)] + vmem(8),
        out_specs=vmem(1) + [pl.BlockSpec(memory_space=pl.ANY)],
        scratch_shapes=[tile] * 3
        + [pltpu.VMEM((half, total), jnp.float32)] * 2
        + [pltpu.SemaphoreType.DMA((pieces,))],
        compiler_params=pltpu.CompilerParams(vmem_limit_bytes=24 << 20),
    )(place, own, other, cross, first, first_inv, wide, high, away)


def shards(hamiltonian, orbitals, adjacency):
    count = hamiltonian.shape[0]
    owned = orbitals.shape[0]
    blocks = lax.axis_size("space")
    groups = lax.axis_size("orb")
    half = owned * groups // 2
    odd = lax.axis_index("space").astype(jnp.int32).reshape(1) % 2
    loc = adjacency % count
    swapped = jnp.concatenate([loc[:, 1:2], loc[:, 0:1], loc[:, 2:]], axis=1)
    loc = jnp.where(odd[0] == 1, loc, swapped)
    near_pairs = [(i, i ^ 1) for i in range(blocks)]
    far_pairs = [(i, (i + 1 if i % 2 else i - 1) % blocks) for i in range(blocks)]
    smem = [pl.BlockSpec(memory_space=pltpu.SMEM)]

    def halo(vec):
        far = lax.ppermute(vec, "space", far_pairs)
        return lax.ppermute(vec, "space", near_pairs), far

    side = halo(orbitals)
    turned, acc = turn_part(orbitals, hamiltonian, loc, odd)
    (one,) = halo_part(1, *side, acc, orbitals, orbitals, turned, loc)
    side = halo(one)
    (two,) = halo_part(2, *side, own_part(one, turned, loc), one, orbitals, turned, loc)
    side = halo(two)
    filtered, narrow = halo_part(3, *side, own_part(two, turned, loc), two, one, turned, loc)

    steps = [1 << i for i in range((blocks - 1).bit_length())]
    stages = [steps[:1]] + [steps[i : i + 2] for i in range(1, len(steps), 2)]

    def summed(part, chosen):
        def moved(step):
            return lax.ppermute(part, "space", [(i, i ^ step) for i in range(blocks)])

        for stage in chosen:
            if len(stage) == 1:
                part = part + moved(stage[0])
            else:
                one, two = stage
                part = (part + moved(one)) + (moved(two) + moved(one ^ two))
        return part

    place = lax.axis_index("orb").astype(jnp.int32).reshape(1)
    if groups == 2:
        swap = [(0, 1), (1, 0)]
        other = lax.ppermute(narrow, "orb", swap)
        tile = jax.ShapeDtypeStruct((half, half), jnp.float32)
        params = pltpu.CompilerParams(vmem_limit_bytes=24 << 20)
        near = pl.pallas_call(
            own_gram_kernel,
            out_shape=tile,
            in_specs=vmem(2),
            out_specs=pl.BlockSpec(memory_space=pltpu.VMEM),
            compiler_params=params,
        )(filtered, narrow)
        near = summed(near, stages[:-1])
        cross = pl.pallas_call(
            cross_gram_kernel,
            out_shape=tile,
            in_specs=smem + vmem(2) + [pl.BlockSpec(memory_space=pl.ANY)],
            out_specs=pl.BlockSpec(memory_space=pltpu.VMEM),
            compiler_params=params,
        )(place, narrow, other, near)
        near = summed(near, stages[-1:])
        far = lax.ppermute(near, "orb", swap)
        cross = summed(cross, stages[:-1])
        first, first_inv = factor_first(place, near, far, cross)
        cross = summed(cross, stages[-1:])
        upper, basis = finish(place, near, far, cross, first, first_inv, filtered, narrow, other)
    else:
        columns = lax.all_gather(narrow, "orb", axis=0, tiled=True)
        whole = summed(dot_nt(columns, columns), stages)
        blocks_of = (jnp.zeros_like(place), whole[:half, :half], whole[half:, half:])
        first, first_inv = factor_first(*blocks_of, whole)
        upper, inverse = factor_second(*blocks_of, whole[:half, half:], first, first_inv)
        mine = lax.dynamic_slice_in_dim(inverse, place[0] * owned, owned, 0)
        near = lax.dynamic_slice_in_dim(mine, place[0] * owned, owned, 1)
        rest = filtered - narrow.astype(jnp.float32)
        basis = dot_full(mine, columns.astype(jnp.float32)) + dot_full(near, rest)
    return (basis, upper)


def solution(mesh):
    in_specs = (P("space", None, None, None), P("orb", "space"), P("space", None))
    out_specs = (P("orb", "space"), P())
    return jax.shard_map(shards, mesh=mesh, in_specs=in_specs, out_specs=out_specs, check_vma=False)
```

```python
import functools

import jax
import jax.numpy as jnp
from jax import lax
from jax.experimental import pallas as pl
from jax.experimental.pallas import tpu as pltpu
from jax.sharding import PartitionSpec as P

centre = 0.25
radius = 0.75
SUB = 8


def vmem(count):
    return [pl.BlockSpec(memory_space=pltpu.VMEM)] * count


def dot_nt(a, b):
    return lax.dot_general(a, b, (((1,), (1,)), ((), ())), preferred_element_type=jnp.float32)


def dot_full(a, b, dims=((1,), (0,))):
    return lax.dot_general(
        a, b, (dims, ((), ())), precision=lax.Precision.HIGHEST, preferred_element_type=jnp.float32
    )


def split(a):
    high = a.astype(jnp.bfloat16)
    return high, (a - high.astype(jnp.float32)).astype(jnp.bfloat16)


def turn_kernel(loc_ref, odd_ref, vec_ref, ham_ref, turned_ref, out_ref):
    count, faces, width, _ = ham_ref.shape
    odd = odd_ref[0]
    for e in range(count):
        here = slice(e * width, (e + 1) * width)
        total = None
        for face in range(faces):
            source = 2 - odd if face == 1 else 1 + odd if face == 2 else face
            turned = ham_ref[e, source].T
            turned_ref[e, face] = turned
            if face == 1 or face == 2:
                continue
            at = here if face == 0 else pl.ds(pl.multiple_of(loc_ref[e, face - 1] * width, width), width)
            part = jnp.dot(vec_ref[:, at], turned, preferred_element_type=jnp.float32)
            total = part if total is None else total + part
        out_ref[:, here] = total


def turn_part(vec, hamiltonian, loc, odd):
    count, faces, width, _ = hamiltonian.shape
    owned = vec.shape[0]
    return pl.pallas_call(
        turn_kernel,
        out_shape=[
            jax.ShapeDtypeStruct(hamiltonian.shape, hamiltonian.dtype),
            jax.ShapeDtypeStruct(vec.shape, jnp.float32),
        ],
        in_specs=[pl.BlockSpec(memory_space=pltpu.SMEM)] * 2 + vmem(2),
        out_specs=vmem(2),
        compiler_params=pltpu.CompilerParams(vmem_limit_bytes=32 << 20),
        cost_estimate=pl.CostEstimate(
            flops=2 * owned * count * width * width * 5,
            bytes_accessed=count * faces * width * width * 4,
            transcendentals=0,
        ),
    )(loc, odd, vec, hamiltonian)


def own_kernel(loc_ref, vec_ref, turned_ref, out_ref):
    count, _, width, _ = turned_ref.shape
    for e in range(count):
        here = slice(e * width, (e + 1) * width)
        total = jnp.dot(vec_ref[:, here], turned_ref[e, 0], preferred_element_type=jnp.float32)
        for face in range(2, 6):
            at = pl.ds(pl.multiple_of(loc_ref[e, face] * width, width), width)
            total += jnp.dot(
                vec_ref[:, at], turned_ref[e, face + 1], preferred_element_type=jnp.float32
            )
        out_ref[:, here] = total


def own_part(vec, turned, loc):
    count, _, width, _ = turned.shape
    owned = vec.shape[0]
    return pl.pallas_call(
        own_kernel,
        out_shape=jax.ShapeDtypeStruct(vec.shape, jnp.float32),
        in_specs=[pl.BlockSpec(memory_space=pltpu.SMEM)] + vmem(2),
        out_specs=pl.BlockSpec(memory_space=pltpu.VMEM),
        compiler_params=pltpu.CompilerParams(vmem_limit_bytes=24 << 20),
        cost_estimate=pl.CostEstimate(
            flops=2 * owned * count * width * width * 5,
            bytes_accessed=count * 5 * width * width * 2,
            transcendentals=0,
        ),
    )(loc, vec, turned)


def halo_kernel(level, loc_ref, near_ref, far_ref, acc_ref, vec_ref, prior_ref, turned_ref, *outs):
    count, _, width, _ = turned_ref.shape
    for e in range(count):
        here = slice(e * width, (e + 1) * width)
        total = acc_ref[:, here]
        for face, ref in enumerate((near_ref, far_ref)):
            at = pl.ds(pl.multiple_of(loc_ref[e, face] * width, width), width)
            total += jnp.dot(
                ref[:, at], turned_ref[e, face + 1], preferred_element_type=jnp.float32
            )
        shifted = (total - centre * vec_ref[:, here].astype(jnp.float32)) * (1.0 / radius)
        if level > 1:
            shifted = 2.0 * shifted - prior_ref[:, here].astype(jnp.float32)
        for out in outs:
            out[:, here] = shifted.astype(out.dtype)


def halo_part(level, near, far, acc, vec, prior, turned, loc):
    count, _, width, _ = turned.shape
    owned = vec.shape[0]
    kinds = [jnp.bfloat16] if level < 3 else [jnp.float32, jnp.bfloat16]
    return pl.pallas_call(
        functools.partial(halo_kernel, level),
        out_shape=[jax.ShapeDtypeStruct(vec.shape, kind) for kind in kinds],
        in_specs=[pl.BlockSpec(memory_space=pltpu.SMEM)] + vmem(6),
        out_specs=vmem(len(kinds)),
        compiler_params=pltpu.CompilerParams(vmem_limit_bytes=24 << 20),
        cost_estimate=pl.CostEstimate(
            flops=2 * owned * count * width * width * 2,
            bytes_accessed=count * 2 * width * width * 2,
            transcendentals=0,
        ),
    )(loc, near, far, acc, vec, prior, turned)


def own_gram_kernel(own_ref, high_ref, out_ref):
    high = high_ref[...]
    low = (own_ref[...] - high.astype(jnp.float32)).astype(jnp.bfloat16)
    mixed = dot_nt(high, low)
    out_ref[...] = dot_nt(high, high) + (mixed + mixed.T)


def cross_gram_kernel(place_ref, own_ref, other_ref, after_ref, out_ref):
    del after_ref

    @pl.when(place_ref[0] == 0)
    def _():
        out_ref[...] = dot_nt(other_ref[...], own_ref[...])

    @pl.when(place_ref[0] != 0)
    def _():
        out_ref[...] = dot_nt(own_ref[...], other_ref[...])


def tree(terms):
    while len(terms) > 1:
        terms = [terms[i] + terms[i + 1] if i + 1 < len(terms) else terms[i] for i in range(0, len(terms), 2)]
    return terms[0]


def factor_block(rows, right):
    strips = len(rows)
    shape = rows[0].shape
    sub = lax.broadcasted_iota(jnp.int32, shape, 0)
    upper, inverse = [], []
    for k in range(strips):
        lanes = [
            jnp.broadcast_to(rows[k][:, k * SUB + j : k * SUB + j + 1], shape) for j in range(SUB)
        ]
        entry = [
            [jnp.broadcast_to(lanes[j][i : i + 1, :], shape) if j <= i else None for j in range(SUB)]
            for i in range(SUB)
        ]
        parts = [
            [jnp.broadcast_to(source[i : i + 1, :], shape) for i in range(SUB)]
            for source in (rows[k], right[k])
        ]
        pairs = []
        for p in range(0, SUB, 2):
            q = p + 1
            a, b, c = entry[p][p], entry[q][p], entry[q][q]
            det = a * c - b * b
            root = lax.rsqrt(det)
            over = root * root
            scaled = {}
            for i in range(q + 1, SUB):
                first = c * entry[i][p] - b * entry[i][q]
                second = a * entry[i][q] - b * entry[i][p]
                scaled[i] = (first * over, second * over)
                for t in range(q + 1, i + 1):
                    entry[i][t] = entry[i][t] - (first * entry[t][p] + second * entry[t][q]) * over
                for part in parts:
                    part[i] = part[i] - (scaled[i][0] * part[p] + scaled[i][1] * part[q])
            pairs.append((p, a, b, c, root, over, scaled))
        packed = [None, None]
        backs = []
        for at, part in enumerate(parts):
            back = [None] * SUB
            for p, a, b, c, root, over, scaled in reversed(pairs):
                q = p + 1
                one = (c * part[p] - b * part[q]) * over
                two = (a * part[q] - b * part[p]) * over
                if scaled:
                    one = one - tree([scaled[i][0] * back[i] for i in scaled])
                    two = two - tree([scaled[i][1] * back[i] for i in scaled])
                back[p], back[q] = one, two
            backs.append(back)
            for p, a, b, c, root, over, scaled in pairs:
                first_root = lax.rsqrt(a)
                high = part[p] * first_root
                low = (a * part[p + 1] - b * part[p]) * (first_root * root)
                packed[at] = high if packed[at] is None else jnp.where(sub == p, high, packed[at])
                packed[at] = jnp.where(sub == p + 1, low, packed[at])
        upper.append(packed[0])
        inverse.append(packed[1])
        for r in range(k + 1, strips):
            columns = [
                jnp.broadcast_to(rows[r][:, k * SUB + i : k * SUB + i + 1], shape) for i in range(SUB)
            ]
            rows[r] = rows[r] - tree([backs[0][i] * columns[i] for i in range(SUB)])
            right[r] = right[r] - tree([backs[1][i] * columns[i] for i in range(SUB)])
    return upper, inverse


def factor_into(work, right, upper_ref, inv_ref):
    half = work.shape[0]
    strips = half // SUB
    row = lax.broadcasted_iota(jnp.int32, (half, half), 0)
    col = lax.broadcasted_iota(jnp.int32, (half, half), 1)
    whole = work[...]
    diagonal = jnp.where(row == col, whole, 0.0)
    across = jnp.sum(diagonal, axis=0, keepdims=True)
    scale = lax.rsqrt(across)
    work[...] = whole * lax.rsqrt(jnp.sum(diagonal, axis=1, keepdims=True)) * scale
    rows = [work[SUB * s : SUB * (s + 1), :] for s in range(strips)]
    eye = (row == col).astype(jnp.float32)
    beside = [eye[SUB * s : SUB * (s + 1), :] for s in range(strips)]
    upper, inverse = factor_block(rows, beside)
    for s in range(strips):
        work[SUB * s : SUB * (s + 1), :] = upper[s]
        right[SUB * s : SUB * (s + 1), :] = inverse[s]
    upper_ref[...] = jnp.where(col >= row, work[...] * (across * scale), 0.0)
    inv_ref[...] = jnp.where(col <= row, right[...] * scale, 0.0)


def first_kernel(place_ref, own_ref, other_ref, after_ref, upper_ref, inv_ref, work, right):
    del after_ref

    @pl.when(place_ref[0] == 0)
    def _():
        work[...] = own_ref[...]

    @pl.when(place_ref[0] != 0)
    def _():
        work[...] = other_ref[...]

    factor_into(work, right, upper_ref, inv_ref)


def second_kernel(place_ref, own_ref, other_ref, cross_ref, first_ref, first_inv_ref, upper_ref, inv_ref, work, right):
    half = own_ref.shape[0]
    across = dot_full(first_inv_ref[...], cross_ref[...])
    update = dot_full(across, across, ((0,), (0,)))

    @pl.when(place_ref[0] == 0)
    def _():
        work[...] = other_ref[...] - update

    @pl.when(place_ref[0] != 0)
    def _():
        work[...] = own_ref[...] - update

    zero = jnp.zeros((half, half), jnp.float32)
    upper_ref[0:half, 0:half] = first_ref[...]
    upper_ref[0:half, half:] = across
    upper_ref[half:, 0:half] = zero
    inv_ref[0:half, 0:half] = first_inv_ref[...]
    inv_ref[0:half, half:] = zero
    between = dot_full(across, first_inv_ref[...], ((0,), (0,)))
    factor_into(work, right, upper_ref.at[half:, half:], inv_ref.at[half:, half:])
    inv_ref[half:, 0:half] = -dot_full(inv_ref[half:, half:], between)


def factor_first(place, own, other, after):
    half = own.shape[0]
    return pl.pallas_call(
        first_kernel,
        out_shape=[jax.ShapeDtypeStruct((half, half), jnp.float32)] * 2,
        in_specs=[pl.BlockSpec(memory_space=pltpu.SMEM)]
        + vmem(2)
        + [pl.BlockSpec(memory_space=pl.ANY)],
        out_specs=vmem(2),
        scratch_shapes=[pltpu.VMEM((half, half), jnp.float32)] * 2,
        compiler_params=pltpu.CompilerParams(vmem_limit_bytes=24 << 20),
        cost_estimate=pl.CostEstimate(flops=2 * half**3, bytes_accessed=1 << 24, transcendentals=half),
    )(place, own, other, after)


def factor_second(place, own, other, cross, first, first_inv):
    half = own.shape[0]
    return pl.pallas_call(
        second_kernel,
        out_shape=[jax.ShapeDtypeStruct((2 * half, 2 * half), jnp.float32)] * 2,
        in_specs=[pl.BlockSpec(memory_space=pltpu.SMEM)] + vmem(5),
        out_specs=vmem(2),
        scratch_shapes=[pltpu.VMEM((half, half), jnp.float32)] * 2,
        compiler_params=pltpu.CompilerParams(vmem_limit_bytes=24 << 20),
    )(place, own, other, cross, first, first_inv)


def finish_kernel(
    place_ref, own_ref, other_ref, cross_ref, first_ref, first_inv_ref, wide_ref, high_ref, away_ref,
    upper_ref, basis_ref, work, right, inverse, part, result, sems,
):
    half, total = wide_ref.shape
    pieces = sems.shape[0]
    spans = [slice(i * (total // pieces), (i + 1) * (total // pieces)) for i in range(pieces)]
    leading = place_ref[0] == 0
    trailing = place_ref[0] != 0
    copies = [
        pltpu.make_async_copy(result.at[:, here], basis_ref.at[:, here], sems.at[i])
        for i, here in enumerate(spans)
    ]

    def dot(a, b):
        return jnp.dot(a, b, preferred_element_type=jnp.float32)

    def product(inverse, high, low):
        high_inv, low_inv = split(inverse)
        stacked = jnp.concatenate([high_inv, high_inv], axis=1)
        return dot(stacked, jnp.concatenate([high, low], axis=0)) + dot(low_inv, high)

    @pl.when(leading)
    def _():
        for copy, here in zip(copies, spans):
            high = high_ref[:, here]
            low = (wide_ref[:, here] - high.astype(jnp.float32)).astype(jnp.bfloat16)
            result[:, here] = product(first_inv_ref[...], high, low)
            copy.start()

    lower = dot_full(cross_ref[...], first_inv_ref[...], ((1,), (1,)))
    rest = jnp.where(leading, other_ref[...], own_ref[...])
    work[...] = rest - dot_full(lower, lower, ((1,), (1,)))
    high_mix, low_mix = split(dot_full(lower, first_inv_ref[...]))
    mixes = jnp.concatenate([high_mix, low_mix], axis=1)
    for here in spans:
        away = away_ref[:, here]
        part[:, here] = wide_ref[:, here] - dot(mixes, jnp.concatenate([away, away], axis=0))
    upper_ref[0:half, 0:half] = first_ref[...]
    upper_ref[0:half, half:] = lower.T
    upper_ref[half:, 0:half] = jnp.zeros((half, half), jnp.float32)
    factor_into(work, right, upper_ref.at[half:, half:], inverse)

    @pl.when(trailing)
    def _():
        for copy, here in zip(copies, spans):
            result[:, here] = product(inverse[...], *split(part[:, here]))
            copy.start()

    for copy in copies:
        copy.wait()


def finish(place, own, other, cross, first, first_inv, wide, high, away):
    half, total = wide.shape
    pieces = 4 if total % 512 == 0 else 1
    tile = pltpu.VMEM((half, half), jnp.float32)
    return pl.pallas_call(
        finish_kernel,
        out_shape=[
            jax.ShapeDtypeStruct((2 * half, 2 * half), jnp.float32),
            jax.ShapeDtypeStruct(wide.shape, jnp.float32),
        ],
        in_specs=[pl.BlockSpec(memory_space=pltpu.SMEM)] + vmem(8),
        out_specs=vmem(1) + [pl.BlockSpec(memory_space=pl.ANY)],
        scratch_shapes=[tile] * 3
        + [pltpu.VMEM((half, total), jnp.float32)] * 2
        + [pltpu.SemaphoreType.DMA((pieces,))],
        compiler_params=pltpu.CompilerParams(vmem_limit_bytes=24 << 20),
    )(place, own, other, cross, first, first_inv, wide, high, away)


def shards(hamiltonian, orbitals, adjacency):
    count = hamiltonian.shape[0]
    owned = orbitals.shape[0]
    blocks = lax.axis_size("space")
    groups = lax.axis_size("orb")
    half = owned * groups // 2
    odd = lax.axis_index("space").astype(jnp.int32).reshape(1) % 2
    loc = adjacency % count
    swapped = jnp.concatenate([loc[:, 1:2], loc[:, 0:1], loc[:, 2:]], axis=1)
    loc = jnp.where(odd[0] == 1, loc, swapped)
    near_pairs = [(i, i ^ 1) for i in range(blocks)]
    far_pairs = [(i, (i + 1 if i % 2 else i - 1) % blocks) for i in range(blocks)]
    smem = [pl.BlockSpec(memory_space=pltpu.SMEM)]

    def halo(vec):
        far = lax.ppermute(vec, "space", far_pairs)
        return lax.ppermute(vec, "space", near_pairs), far

    side = halo(orbitals)
    turned, acc = turn_part(orbitals, hamiltonian, loc, odd)
    (one,) = halo_part(1, *side, acc, orbitals, orbitals, turned, loc)
    side = halo(one)
    (two,) = halo_part(2, *side, own_part(one, turned, loc), one, orbitals, turned, loc)
    side = halo(two)
    filtered, narrow = halo_part(3, *side, own_part(two, turned, loc), two, one, turned, loc)

    steps = [1 << i for i in range((blocks - 1).bit_length())]
    stages = [steps[:1]] + [steps[i : i + 2] for i in range(1, len(steps), 2)]

    def summed(part, chosen):
        def moved(step):
            return lax.ppermute(part, "space", [(i, i ^ step) for i in range(blocks)])

        for stage in chosen:
            if len(stage) == 1:
                part = part + moved(stage[0])
            else:
                one, two = stage
                part = (part + moved(one)) + (moved(two) + moved(one ^ two))
        return part

    place = lax.axis_index("orb").astype(jnp.int32).reshape(1)
    if groups == 2:
        swap = [(0, 1), (1, 0)]
        other = lax.ppermute(narrow, "orb", swap)
        tile = jax.ShapeDtypeStruct((half, half), jnp.float32)
        params = pltpu.CompilerParams(vmem_limit_bytes=24 << 20)
        near = pl.pallas_call(
            own_gram_kernel,
            out_shape=tile,
            in_specs=vmem(2),
            out_specs=pl.BlockSpec(memory_space=pltpu.VMEM),
            compiler_params=params,
        )(filtered, narrow)
        near = summed(near, stages[:1])
        cross = pl.pallas_call(
            cross_gram_kernel,
            out_shape=tile,
            in_specs=smem + vmem(2) + [pl.BlockSpec(memory_space=pl.ANY)],
            out_specs=pl.BlockSpec(memory_space=pltpu.VMEM),
            compiler_params=params,
        )(place, narrow, other, near)
        near = summed(near, stages[1:])
        far = lax.ppermute(near, "orb", swap)
        cross = summed(cross, stages[:-1])
        first, first_inv = factor_first(place, near, far, cross)
        cross = summed(cross, stages[-1:])
        upper, basis = finish(place, near, far, cross, first, first_inv, filtered, narrow, other)
    else:
        columns = lax.all_gather(narrow, "orb", axis=0, tiled=True)
        whole = summed(dot_nt(columns, columns), stages)
        blocks_of = (jnp.zeros_like(place), whole[:half, :half], whole[half:, half:])
        first, first_inv = factor_first(*blocks_of, whole)
        upper, inverse = factor_second(*blocks_of, whole[:half, half:], first, first_inv)
        mine = lax.dynamic_slice_in_dim(inverse, place[0] * owned, owned, 0)
        near = lax.dynamic_slice_in_dim(mine, place[0] * owned, owned, 1)
        rest = filtered - narrow.astype(jnp.float32)
        basis = dot_full(mine, columns.astype(jnp.float32)) + dot_full(near, rest)
    return (basis, upper)


def solution(mesh):
    in_specs = (P("space", None, None, None), P("orb", "space"), P("space", None))
    out_specs = (P("orb", "space"), P())
    return jax.shard_map(shards, mesh=mesh, in_specs=in_specs, out_specs=out_specs, check_vma=False)
```

```python
import functools

import jax
import jax.numpy as jnp
from jax import lax
from jax.experimental import pallas as pl
from jax.experimental.pallas import tpu as pltpu
from jax.sharding import PartitionSpec as P

centre = 0.25
radius = 0.75
SUB = 8


def vmem(count):
    return [pl.BlockSpec(memory_space=pltpu.VMEM)] * count


def dot_nt(a, b):
    return lax.dot_general(a, b, (((1,), (1,)), ((), ())), preferred_element_type=jnp.float32)


def dot_full(a, b, dims=((1,), (0,))):
    return lax.dot_general(
        a, b, (dims, ((), ())), precision=lax.Precision.HIGHEST, preferred_element_type=jnp.float32
    )


def split(a):
    high = a.astype(jnp.bfloat16)
    return high, (a - high.astype(jnp.float32)).astype(jnp.bfloat16)


def turn_kernel(loc_ref, odd_ref, vec_ref, ham_ref, turned_ref, out_ref):
    count, faces, width, _ = ham_ref.shape
    odd = odd_ref[0]
    for e in range(count):
        here = slice(e * width, (e + 1) * width)
        total = None
        for face in range(faces):
            source = 2 - odd if face == 1 else 1 + odd if face == 2 else face
            turned = ham_ref[e, source].T
            turned_ref[e, face] = turned
            if face == 1 or face == 2:
                continue
            at = here if face == 0 else pl.ds(pl.multiple_of(loc_ref[e, face - 1] * width, width), width)
            part = jnp.dot(vec_ref[:, at], turned, preferred_element_type=jnp.float32)
            total = part if total is None else total + part
        out_ref[:, here] = total


def turn_part(vec, hamiltonian, loc, odd):
    count, faces, width, _ = hamiltonian.shape
    owned = vec.shape[0]
    return pl.pallas_call(
        turn_kernel,
        out_shape=[
            jax.ShapeDtypeStruct(hamiltonian.shape, hamiltonian.dtype),
            jax.ShapeDtypeStruct(vec.shape, jnp.float32),
        ],
        in_specs=[pl.BlockSpec(memory_space=pltpu.SMEM)] * 2 + vmem(2),
        out_specs=vmem(2),
        compiler_params=pltpu.CompilerParams(vmem_limit_bytes=32 << 20),
        cost_estimate=pl.CostEstimate(
            flops=2 * owned * count * width * width * 5,
            bytes_accessed=count * faces * width * width * 4,
            transcendentals=0,
        ),
    )(loc, odd, vec, hamiltonian)


def own_kernel(loc_ref, vec_ref, turned_ref, out_ref):
    count, _, width, _ = turned_ref.shape
    for e in range(count):
        here = slice(e * width, (e + 1) * width)
        total = jnp.dot(vec_ref[:, here], turned_ref[e, 0], preferred_element_type=jnp.float32)
        for face in range(2, 6):
            at = pl.ds(pl.multiple_of(loc_ref[e, face] * width, width), width)
            total += jnp.dot(
                vec_ref[:, at], turned_ref[e, face + 1], preferred_element_type=jnp.float32
            )
        out_ref[:, here] = total


def own_part(vec, turned, loc):
    count, _, width, _ = turned.shape
    owned = vec.shape[0]
    return pl.pallas_call(
        own_kernel,
        out_shape=jax.ShapeDtypeStruct(vec.shape, jnp.float32),
        in_specs=[pl.BlockSpec(memory_space=pltpu.SMEM)] + vmem(2),
        out_specs=pl.BlockSpec(memory_space=pltpu.VMEM),
        compiler_params=pltpu.CompilerParams(vmem_limit_bytes=24 << 20),
        cost_estimate=pl.CostEstimate(
            flops=2 * owned * count * width * width * 5,
            bytes_accessed=count * 5 * width * width * 2,
            transcendentals=0,
        ),
    )(loc, vec, turned)


def halo_kernel(level, loc_ref, near_ref, far_ref, acc_ref, vec_ref, prior_ref, turned_ref, *outs):
    count, _, width, _ = turned_ref.shape
    for e in range(count):
        here = slice(e * width, (e + 1) * width)
        total = acc_ref[:, here]
        for face, ref in enumerate((near_ref, far_ref)):
            at = pl.ds(pl.multiple_of(loc_ref[e, face] * width, width), width)
            total += jnp.dot(
                ref[:, at], turned_ref[e, face + 1], preferred_element_type=jnp.float32
            )
        shifted = (total - centre * vec_ref[:, here].astype(jnp.float32)) * (1.0 / radius)
        if level > 1:
            shifted = 2.0 * shifted - prior_ref[:, here].astype(jnp.float32)
        for out in outs:
            out[:, here] = shifted.astype(out.dtype)


def halo_part(level, near, far, acc, vec, prior, turned, loc):
    count, _, width, _ = turned.shape
    owned = vec.shape[0]
    kinds = [jnp.bfloat16] if level < 3 else [jnp.float32, jnp.bfloat16]
    return pl.pallas_call(
        functools.partial(halo_kernel, level),
        out_shape=[jax.ShapeDtypeStruct(vec.shape, kind) for kind in kinds],
        in_specs=[pl.BlockSpec(memory_space=pltpu.SMEM)] + vmem(6),
        out_specs=vmem(len(kinds)),
        compiler_params=pltpu.CompilerParams(vmem_limit_bytes=24 << 20),
        cost_estimate=pl.CostEstimate(
            flops=2 * owned * count * width * width * 2,
            bytes_accessed=count * 2 * width * width * 2,
            transcendentals=0,
        ),
    )(loc, near, far, acc, vec, prior, turned)


def own_gram_kernel(own_ref, high_ref, out_ref):
    high = high_ref[...]
    low = (own_ref[...] - high.astype(jnp.float32)).astype(jnp.bfloat16)
    mixed = dot_nt(high, low)
    out_ref[...] = dot_nt(high, high) + (mixed + mixed.T)


def cross_gram_kernel(place_ref, own_ref, other_ref, after_ref, out_ref):
    del after_ref

    @pl.when(place_ref[0] == 0)
    def _():
        out_ref[...] = dot_nt(other_ref[...], own_ref[...])

    @pl.when(place_ref[0] != 0)
    def _():
        out_ref[...] = dot_nt(own_ref[...], other_ref[...])


def tree(terms):
    while len(terms) > 1:
        terms = [terms[i] + terms[i + 1] if i + 1 < len(terms) else terms[i] for i in range(0, len(terms), 2)]
    return terms[0]


def factor_block(rows, right):
    strips = len(rows)
    shape = rows[0].shape
    sub = lax.broadcasted_iota(jnp.int32, shape, 0)
    upper, inverse = [], []
    for k in range(strips):
        lanes = [
            jnp.broadcast_to(rows[k][:, k * SUB + j : k * SUB + j + 1], shape) for j in range(SUB)
        ]
        entry = [
            [jnp.broadcast_to(lanes[j][i : i + 1, :], shape) if j <= i else None for j in range(SUB)]
            for i in range(SUB)
        ]
        parts = [
            [jnp.broadcast_to(source[i : i + 1, :], shape) for i in range(SUB)]
            for source in (rows[k], right[k])
        ]
        pairs = []
        for p in range(0, SUB, 2):
            q = p + 1
            a, b, c = entry[p][p], entry[q][p], entry[q][q]
            det = a * c - b * b
            root = lax.rsqrt(det)
            over = root * root
            scaled = {}
            for i in range(q + 1, SUB):
                first = c * entry[i][p] - b * entry[i][q]
                second = a * entry[i][q] - b * entry[i][p]
                scaled[i] = (first * over, second * over)
                for t in range(q + 1, i + 1):
                    entry[i][t] = entry[i][t] - (first * entry[t][p] + second * entry[t][q]) * over
                for part in parts:
                    part[i] = part[i] - (scaled[i][0] * part[p] + scaled[i][1] * part[q])
            pairs.append((p, a, b, c, root, over, scaled))
        packed = [None, None]
        backs = []
        for at, part in enumerate(parts):
            back = [None] * SUB
            for p, a, b, c, root, over, scaled in reversed(pairs):
                q = p + 1
                one = (c * part[p] - b * part[q]) * over
                two = (a * part[q] - b * part[p]) * over
                if scaled:
                    one = one - tree([scaled[i][0] * back[i] for i in scaled])
                    two = two - tree([scaled[i][1] * back[i] for i in scaled])
                back[p], back[q] = one, two
            backs.append(back)
            for p, a, b, c, root, over, scaled in pairs:
                first_root = lax.rsqrt(a)
                high = part[p] * first_root
                low = (a * part[p + 1] - b * part[p]) * (first_root * root)
                packed[at] = high if packed[at] is None else jnp.where(sub == p, high, packed[at])
                packed[at] = jnp.where(sub == p + 1, low, packed[at])
        upper.append(packed[0])
        inverse.append(packed[1])
        for r in range(k + 1, strips):
            columns = [
                jnp.broadcast_to(rows[r][:, k * SUB + i : k * SUB + i + 1], shape) for i in range(SUB)
            ]
            rows[r] = rows[r] - tree([backs[0][i] * columns[i] for i in range(SUB)])
            right[r] = right[r] - tree([backs[1][i] * columns[i] for i in range(SUB)])
    return upper, inverse


def factor_into(work, right, upper_ref, inv_ref):
    half = work.shape[0]
    strips = half // SUB
    row = lax.broadcasted_iota(jnp.int32, (half, half), 0)
    col = lax.broadcasted_iota(jnp.int32, (half, half), 1)
    whole = work[...]
    diagonal = jnp.where(row == col, whole, 0.0)
    across = jnp.sum(diagonal, axis=0, keepdims=True)
    scale = lax.rsqrt(across)
    work[...] = whole * lax.rsqrt(jnp.sum(diagonal, axis=1, keepdims=True)) * scale
    rows = [work[SUB * s : SUB * (s + 1), :] for s in range(strips)]
    eye = (row == col).astype(jnp.float32)
    beside = [eye[SUB * s : SUB * (s + 1), :] for s in range(strips)]
    upper, inverse = factor_block(rows, beside)
    for s in range(strips):
        work[SUB * s : SUB * (s + 1), :] = upper[s]
        right[SUB * s : SUB * (s + 1), :] = inverse[s]
    upper_ref[...] = jnp.where(col >= row, work[...] * (across * scale), 0.0)
    inv_ref[...] = jnp.where(col <= row, right[...] * scale, 0.0)


def first_kernel(place_ref, own_ref, other_ref, after_ref, upper_ref, inv_ref, work, right):
    del after_ref

    @pl.when(place_ref[0] == 0)
    def _():
        work[...] = own_ref[...]

    @pl.when(place_ref[0] != 0)
    def _():
        work[...] = other_ref[...]

    factor_into(work, right, upper_ref, inv_ref)


def second_kernel(place_ref, own_ref, other_ref, cross_ref, first_ref, first_inv_ref, upper_ref, inv_ref, work, right):
    half = own_ref.shape[0]
    across = dot_full(first_inv_ref[...], cross_ref[...])
    update = dot_full(across, across, ((0,), (0,)))

    @pl.when(place_ref[0] == 0)
    def _():
        work[...] = other_ref[...] - update

    @pl.when(place_ref[0] != 0)
    def _():
        work[...] = own_ref[...] - update

    zero = jnp.zeros((half, half), jnp.float32)
    upper_ref[0:half, 0:half] = first_ref[...]
    upper_ref[0:half, half:] = across
    upper_ref[half:, 0:half] = zero
    inv_ref[0:half, 0:half] = first_inv_ref[...]
    inv_ref[0:half, half:] = zero
    between = dot_full(across, first_inv_ref[...], ((0,), (0,)))
    factor_into(work, right, upper_ref.at[half:, half:], inv_ref.at[half:, half:])
    inv_ref[half:, 0:half] = -dot_full(inv_ref[half:, half:], between)


def factor_first(place, own, other, after):
    half = own.shape[0]
    return pl.pallas_call(
        first_kernel,
        out_shape=[jax.ShapeDtypeStruct((half, half), jnp.float32)] * 2,
        in_specs=[pl.BlockSpec(memory_space=pltpu.SMEM)]
        + vmem(2)
        + [pl.BlockSpec(memory_space=pl.ANY)],
        out_specs=vmem(2),
        scratch_shapes=[pltpu.VMEM((half, half), jnp.float32)] * 2,
        compiler_params=pltpu.CompilerParams(vmem_limit_bytes=24 << 20),
        cost_estimate=pl.CostEstimate(flops=2 * half**3, bytes_accessed=1 << 24, transcendentals=half),
    )(place, own, other, after)


def factor_second(place, own, other, cross, first, first_inv):
    half = own.shape[0]
    return pl.pallas_call(
        second_kernel,
        out_shape=[jax.ShapeDtypeStruct((2 * half, 2 * half), jnp.float32)] * 2,
        in_specs=[pl.BlockSpec(memory_space=pltpu.SMEM)] + vmem(5),
        out_specs=vmem(2),
        scratch_shapes=[pltpu.VMEM((half, half), jnp.float32)] * 2,
        compiler_params=pltpu.CompilerParams(vmem_limit_bytes=24 << 20),
    )(place, own, other, cross, first, first_inv)


def finish_kernel(
    place_ref, own_ref, other_ref, cross_ref, first_ref, first_inv_ref, wide_ref, high_ref, away_ref,
    upper_ref, basis_ref, work, right, inverse, part, result, sems,
):
    half, total = wide_ref.shape
    pieces = sems.shape[0]
    spans = [slice(i * (total // pieces), (i + 1) * (total // pieces)) for i in range(pieces)]
    leading = place_ref[0] == 0
    trailing = place_ref[0] != 0
    copies = [
        pltpu.make_async_copy(result.at[:, here], basis_ref.at[:, here], sems.at[i])
        for i, here in enumerate(spans)
    ]

    def dot(a, b):
        return jnp.dot(a, b, preferred_element_type=jnp.float32)

    def product(inverse, high, low):
        high_inv, low_inv = split(inverse)
        stacked = jnp.concatenate([high_inv, high_inv], axis=1)
        return dot(stacked, jnp.concatenate([high, low], axis=0)) + dot(low_inv, high)

    @pl.when(leading)
    def _():
        for copy, here in zip(copies, spans):
            high = high_ref[:, here]
            low = (wide_ref[:, here] - high.astype(jnp.float32)).astype(jnp.bfloat16)
            result[:, here] = product(first_inv_ref[...], high, low)
            copy.start()

    lower = dot_full(cross_ref[...], first_inv_ref[...], ((1,), (1,)))
    rest = jnp.where(leading, other_ref[...], own_ref[...])
    work[...] = rest - dot_full(lower, lower, ((1,), (1,)))
    high_mix, low_mix = split(dot_full(lower, first_inv_ref[...]))
    mixes = jnp.concatenate([high_mix, low_mix], axis=1)
    for here in spans:
        away = away_ref[:, here]
        part[:, here] = wide_ref[:, here] - dot(mixes, jnp.concatenate([away, away], axis=0))
    upper_ref[0:half, 0:half] = first_ref[...]
    upper_ref[0:half, half:] = lower.T
    upper_ref[half:, 0:half] = jnp.zeros((half, half), jnp.float32)
    factor_into(work, right, upper_ref.at[half:, half:], inverse)

    @pl.when(trailing)
    def _():
        for copy, here in zip(copies, spans):
            result[:, here] = product(inverse[...], *split(part[:, here]))
            copy.start()

    for copy in copies:
        copy.wait()


def finish(place, own, other, cross, first, first_inv, wide, high, away):
    half, total = wide.shape
    pieces = 4 if total % 512 == 0 else 1
    tile = pltpu.VMEM((half, half), jnp.float32)
    return pl.pallas_call(
        finish_kernel,
        out_shape=[
            jax.ShapeDtypeStruct((2 * half, 2 * half), jnp.float32),
            jax.ShapeDtypeStruct(wide.shape, jnp.float32),
        ],
        in_specs=[pl.BlockSpec(memory_space=pltpu.SMEM)] + vmem(8),
        out_specs=vmem(1) + [pl.BlockSpec(memory_space=pl.ANY)],
        scratch_shapes=[tile] * 3
        + [pltpu.VMEM((half, total), jnp.float32)] * 2
        + [pltpu.SemaphoreType.DMA((pieces,))],
        compiler_params=pltpu.CompilerParams(vmem_limit_bytes=24 << 20),
    )(place, own, other, cross, first, first_inv, wide, high, away)


def shards(hamiltonian, orbitals, adjacency):
    count = hamiltonian.shape[0]
    owned = orbitals.shape[0]
    blocks = lax.axis_size("space")
    groups = lax.axis_size("orb")
    half = owned * groups // 2
    odd = lax.axis_index("space").astype(jnp.int32).reshape(1) % 2
    loc = adjacency % count
    swapped = jnp.concatenate([loc[:, 1:2], loc[:, 0:1], loc[:, 2:]], axis=1)
    loc = jnp.where(odd[0] == 1, loc, swapped)
    near_pairs = [(i, i ^ 1) for i in range(blocks)]
    far_pairs = [(i, (i + 1 if i % 2 else i - 1) % blocks) for i in range(blocks)]
    smem = [pl.BlockSpec(memory_space=pltpu.SMEM)]

    def halo(vec):
        far = lax.ppermute(vec, "space", far_pairs)
        return lax.ppermute(vec, "space", near_pairs), far

    side = halo(orbitals)
    turned, acc = turn_part(orbitals, hamiltonian, loc, odd)
    (one,) = halo_part(1, *side, acc, orbitals, orbitals, turned, loc)
    side = halo(one)
    (two,) = halo_part(2, *side, own_part(one, turned, loc), one, orbitals, turned, loc)
    side = halo(two)
    filtered, narrow = halo_part(3, *side, own_part(two, turned, loc), two, one, turned, loc)

    steps = [1 << i for i in range((blocks - 1).bit_length())]
    stages = [steps[:1]] + [steps[i : i + 2] for i in range(1, len(steps), 2)]

    def summed(part, chosen):
        def moved(step):
            return lax.ppermute(part, "space", [(i, i ^ step) for i in range(blocks)])

        for stage in chosen:
            if len(stage) == 1:
                part = part + moved(stage[0])
            else:
                one, two = stage
                part = (part + moved(one)) + (moved(two) + moved(one ^ two))
        return part

    place = lax.axis_index("orb").astype(jnp.int32).reshape(1)
    if groups == 2:
        swap = [(0, 1), (1, 0)]
        other = lax.ppermute(narrow, "orb", swap)
        tile = jax.ShapeDtypeStruct((half, half), jnp.float32)
        params = pltpu.CompilerParams(vmem_limit_bytes=24 << 20)
        near = pl.pallas_call(
            own_gram_kernel,
            out_shape=tile,
            in_specs=vmem(2),
            out_specs=pl.BlockSpec(memory_space=pltpu.VMEM),
            compiler_params=params,
        )(filtered, narrow)
        near = summed(near, stages[:-1])
        cross = pl.pallas_call(
            cross_gram_kernel,
            out_shape=tile,
            in_specs=smem + vmem(2) + [pl.BlockSpec(memory_space=pl.ANY)],
            out_specs=pl.BlockSpec(memory_space=pltpu.VMEM),
            compiler_params=params,
        )(place, narrow, other, near)
        last = stages[-1]

        def away(step):
            pairs = [(2 * i + j, 2 * (i ^ step) + 1 - j) for i in range(blocks) for j in range(2)]
            return lax.ppermute(near, ("space", "orb"), pairs)

        if len(last) == 1:
            far = away(0) + away(last[0])
            near = summed(near, [last])
        else:
            near = summed(near, [last])
            far = away(0)
        cross = summed(cross, stages[:-1])
        first, first_inv = factor_first(place, near, far, cross)
        cross = summed(cross, stages[-1:])
        upper, basis = finish(place, near, far, cross, first, first_inv, filtered, narrow, other)
    else:
        columns = lax.all_gather(narrow, "orb", axis=0, tiled=True)
        whole = summed(dot_nt(columns, columns), stages)
        blocks_of = (jnp.zeros_like(place), whole[:half, :half], whole[half:, half:])
        first, first_inv = factor_first(*blocks_of, whole)
        upper, inverse = factor_second(*blocks_of, whole[:half, half:], first, first_inv)
        mine = lax.dynamic_slice_in_dim(inverse, place[0] * owned, owned, 0)
        near = lax.dynamic_slice_in_dim(mine, place[0] * owned, owned, 1)
        rest = filtered - narrow.astype(jnp.float32)
        basis = dot_full(mine, columns.astype(jnp.float32)) + dot_full(near, rest)
    return (basis, upper)


def solution(mesh):
    in_specs = (P("space", None, None, None), P("orb", "space"), P("space", None))
    out_specs = (P("orb", "space"), P())
    return jax.shard_map(shards, mesh=mesh, in_specs=in_specs, out_specs=out_specs, check_vma=False)
```

```python
import functools

import jax
import jax.numpy as jnp
from jax import lax
from jax.experimental import pallas as pl
from jax.experimental.pallas import tpu as pltpu
from jax.sharding import PartitionSpec as P

centre = 0.25
radius = 0.75
SUB = 8


def vmem(count):
    return [pl.BlockSpec(memory_space=pltpu.VMEM)] * count


def dot_nt(a, b):
    return lax.dot_general(a, b, (((1,), (1,)), ((), ())), preferred_element_type=jnp.float32)


def dot_full(a, b, dims=((1,), (0,))):
    return lax.dot_general(
        a, b, (dims, ((), ())), precision=lax.Precision.HIGHEST, preferred_element_type=jnp.float32
    )


def split(a):
    high = a.astype(jnp.bfloat16)
    return high, (a - high.astype(jnp.float32)).astype(jnp.bfloat16)


def stacked(refs, here=slice(None)):
    return jnp.concatenate([ref[:, here] for ref in refs], axis=0)


def turn_kernel(chunks, loc_ref, odd_ref, *refs):
    vec_refs, ham_ref, turned_ref, outs = refs[:chunks], refs[chunks], refs[chunks + 1], refs[chunks + 2 : -2]
    buf, sems = refs[-2:]
    count, faces, width, _ = ham_ref.shape
    share = outs[0].shape[0]
    odd = odd_ref[0]
    copies = [pltpu.make_async_copy(ham_ref.at[e], buf.at[e], sems.at[e]) for e in range(count)]
    for copy in copies:
        copy.start()
    for e in range(count):
        copies[e].wait()
        here = slice(e * width, (e + 1) * width)
        total = None
        for face in range(faces):
            source = 2 - odd if face == 1 else 1 + odd if face == 2 else face
            turned = buf[e, source].T
            turned_ref[e, face] = turned
            if face == 1 or face == 2:
                continue
            at = here if face == 0 else pl.ds(pl.multiple_of(loc_ref[e, face - 1] * width, width), width)
            part = jnp.dot(stacked(vec_refs, at), turned, preferred_element_type=jnp.float32)
            total = part if total is None else total + part
        for piece, out in enumerate(outs):
            out[:, here] = total[piece * share : (piece + 1) * share]


def turn_part(vecs, hamiltonian, loc, odd):
    count, faces, width, _ = hamiltonian.shape
    chunks = len(vecs)
    return pl.pallas_call(
        functools.partial(turn_kernel, chunks),
        out_shape=[jax.ShapeDtypeStruct(hamiltonian.shape, hamiltonian.dtype)]
        + [jax.ShapeDtypeStruct(vec.shape, jnp.float32) for vec in vecs],
        in_specs=[pl.BlockSpec(memory_space=pltpu.SMEM)] * 2
        + vmem(chunks)
        + [pl.BlockSpec(memory_space=pl.ANY)],
        out_specs=vmem(1 + chunks),
        scratch_shapes=[
            pltpu.VMEM(hamiltonian.shape, hamiltonian.dtype),
            pltpu.SemaphoreType.DMA((count,)),
        ],
        compiler_params=pltpu.CompilerParams(vmem_limit_bytes=43 << 20),
        cost_estimate=pl.CostEstimate(
            flops=10 * chunks * vecs[0].shape[0] * count * width * width,
            bytes_accessed=count * faces * width * width * 4,
            transcendentals=0,
        ),
    )(loc, odd, *vecs, hamiltonian)


def own_kernel(loc_ref, vec_ref, turned_ref, out_ref):
    count, _, width, _ = turned_ref.shape
    for e in range(count):
        here = slice(e * width, (e + 1) * width)
        total = jnp.dot(vec_ref[:, here], turned_ref[e, 0], preferred_element_type=jnp.float32)
        for face in range(2, 6):
            at = pl.ds(pl.multiple_of(loc_ref[e, face] * width, width), width)
            total += jnp.dot(
                vec_ref[:, at], turned_ref[e, face + 1], preferred_element_type=jnp.float32
            )
        out_ref[:, here] = total


def own_part(vec, turned, loc):
    count, _, width, _ = turned.shape
    owned = vec.shape[0]
    return pl.pallas_call(
        own_kernel,
        out_shape=jax.ShapeDtypeStruct(vec.shape, jnp.float32),
        in_specs=[pl.BlockSpec(memory_space=pltpu.SMEM)] + vmem(2),
        out_specs=pl.BlockSpec(memory_space=pltpu.VMEM),
        compiler_params=pltpu.CompilerParams(vmem_limit_bytes=24 << 20),
        cost_estimate=pl.CostEstimate(
            flops=2 * owned * count * width * width * 5,
            bytes_accessed=count * 5 * width * width * 2,
            transcendentals=0,
        ),
    )(loc, vec, turned)


def halo_kernel(level, loc_ref, near_ref, far_ref, acc_ref, vec_ref, prior_ref, turned_ref, *outs):
    count, _, width, _ = turned_ref.shape
    for e in range(count):
        here = slice(e * width, (e + 1) * width)
        total = acc_ref[:, here]
        for face, ref in enumerate((near_ref, far_ref)):
            at = pl.ds(pl.multiple_of(loc_ref[e, face] * width, width), width)
            total += jnp.dot(
                ref[:, at], turned_ref[e, face + 1], preferred_element_type=jnp.float32
            )
        shifted = (total - centre * vec_ref[:, here].astype(jnp.float32)) * (1.0 / radius)
        if level > 1:
            shifted = 2.0 * shifted - prior_ref[:, here].astype(jnp.float32)
        for out in outs:
            out[:, here] = shifted.astype(out.dtype)


def halo_part(level, near, far, acc, vec, prior, turned, loc):
    count, _, width, _ = turned.shape
    owned = vec.shape[0]
    kinds = [jnp.bfloat16] if level < 3 else [jnp.float32, jnp.bfloat16]
    return pl.pallas_call(
        functools.partial(halo_kernel, level),
        out_shape=[jax.ShapeDtypeStruct(vec.shape, kind) for kind in kinds],
        in_specs=[pl.BlockSpec(memory_space=pltpu.SMEM)] + vmem(6),
        out_specs=vmem(len(kinds)),
        compiler_params=pltpu.CompilerParams(vmem_limit_bytes=24 << 20),
        cost_estimate=pl.CostEstimate(
            flops=2 * owned * count * width * width * 2,
            bytes_accessed=count * 2 * width * width * 2,
            transcendentals=0,
        ),
    )(loc, near, far, acc, vec, prior, turned)


def own_gram_kernel(chunks, *refs):
    own_refs, high_refs, out_ref = refs[:chunks], refs[chunks:-1], refs[-1]
    high = stacked(high_refs)
    low = (stacked(own_refs) - high.astype(jnp.float32)).astype(jnp.bfloat16)
    mixed = dot_nt(high, low)
    out_ref[...] = dot_nt(high, high) + (mixed + mixed.T)


def cross_gram_kernel(chunks, place_ref, *refs):
    own_refs, other_refs, out_ref = refs[:chunks], refs[chunks:-2], refs[-1]

    @pl.when(place_ref[0] == 0)
    def _():
        out_ref[...] = dot_nt(stacked(other_refs), stacked(own_refs))

    @pl.when(place_ref[0] != 0)
    def _():
        out_ref[...] = dot_nt(stacked(own_refs), stacked(other_refs))


def tree(terms):
    while len(terms) > 1:
        terms = [terms[i] + terms[i + 1] if i + 1 < len(terms) else terms[i] for i in range(0, len(terms), 2)]
    return terms[0]


def factor_block(rows, right):
    strips = len(rows)
    shape = rows[0].shape
    sub = lax.broadcasted_iota(jnp.int32, shape, 0)
    upper, inverse = [], []
    for k in range(strips):
        lanes = [
            jnp.broadcast_to(rows[k][:, k * SUB + j : k * SUB + j + 1], shape) for j in range(SUB)
        ]
        entry = [
            [jnp.broadcast_to(lanes[j][i : i + 1, :], shape) if j <= i else None for j in range(SUB)]
            for i in range(SUB)
        ]
        parts = [
            [jnp.broadcast_to(source[i : i + 1, :], shape) for i in range(SUB)]
            for source in (rows[k], right[k])
        ]
        pairs = []
        for p in range(0, SUB, 2):
            q = p + 1
            a, b, c = entry[p][p], entry[q][p], entry[q][q]
            det = a * c - b * b
            root = lax.rsqrt(det)
            over = root * root
            scaled = {}
            for i in range(q + 1, SUB):
                first = c * entry[i][p] - b * entry[i][q]
                second = a * entry[i][q] - b * entry[i][p]
                scaled[i] = (first * over, second * over)
                for t in range(q + 1, i + 1):
                    entry[i][t] = entry[i][t] - (first * entry[t][p] + second * entry[t][q]) * over
                for part in parts:
                    part[i] = part[i] - (scaled[i][0] * part[p] + scaled[i][1] * part[q])
            pairs.append((p, a, b, c, root, over, scaled))
        packed = [None, None]
        backs = []
        for at, part in enumerate(parts):
            back = [None] * SUB
            for p, a, b, c, root, over, scaled in reversed(pairs):
                q = p + 1
                one = (c * part[p] - b * part[q]) * over
                two = (a * part[q] - b * part[p]) * over
                if scaled:
                    one = one - tree([scaled[i][0] * back[i] for i in scaled])
                    two = two - tree([scaled[i][1] * back[i] for i in scaled])
                back[p], back[q] = one, two
            backs.append(back)
            for p, a, b, c, root, over, scaled in pairs:
                first_root = lax.rsqrt(a)
                high = part[p] * first_root
                low = (a * part[p + 1] - b * part[p]) * (first_root * root)
                packed[at] = high if packed[at] is None else jnp.where(sub == p, high, packed[at])
                packed[at] = jnp.where(sub == p + 1, low, packed[at])
        upper.append(packed[0])
        inverse.append(packed[1])
        for r in range(k + 1, strips):
            columns = [
                jnp.broadcast_to(rows[r][:, k * SUB + i : k * SUB + i + 1], shape) for i in range(SUB)
            ]
            rows[r] = rows[r] - tree([backs[0][i] * columns[i] for i in range(SUB)])
            right[r] = right[r] - tree([backs[1][i] * columns[i] for i in range(SUB)])
    return upper, inverse


def factor_into(work, right, upper_ref, inv_ref):
    half = work.shape[0]
    strips = half // SUB
    row = lax.broadcasted_iota(jnp.int32, (half, half), 0)
    col = lax.broadcasted_iota(jnp.int32, (half, half), 1)
    whole = work[...]
    diagonal = jnp.where(row == col, whole, 0.0)
    across = jnp.sum(diagonal, axis=0, keepdims=True)
    scale = lax.rsqrt(across)
    work[...] = whole * lax.rsqrt(jnp.sum(diagonal, axis=1, keepdims=True)) * scale
    rows = [work[SUB * s : SUB * (s + 1), :] for s in range(strips)]
    eye = (row == col).astype(jnp.float32)
    beside = [eye[SUB * s : SUB * (s + 1), :] for s in range(strips)]
    upper, inverse = factor_block(rows, beside)
    for s in range(strips):
        work[SUB * s : SUB * (s + 1), :] = upper[s]
        right[SUB * s : SUB * (s + 1), :] = inverse[s]
    upper_ref[...] = jnp.where(col >= row, work[...] * (across * scale), 0.0)
    inv_ref[...] = jnp.where(col <= row, right[...] * scale, 0.0)


def first_kernel(place_ref, own_ref, other_ref, after_ref, upper_ref, inv_ref, work, right):
    del after_ref

    @pl.when(place_ref[0] == 0)
    def _():
        work[...] = own_ref[...]

    @pl.when(place_ref[0] != 0)
    def _():
        work[...] = other_ref[...]

    factor_into(work, right, upper_ref, inv_ref)


def second_kernel(place_ref, own_ref, other_ref, cross_ref, first_ref, first_inv_ref, upper_ref, inv_ref, work, right):
    half = own_ref.shape[0]
    across = dot_full(first_inv_ref[...], cross_ref[...])
    update = dot_full(across, across, ((0,), (0,)))

    @pl.when(place_ref[0] == 0)
    def _():
        work[...] = other_ref[...] - update

    @pl.when(place_ref[0] != 0)
    def _():
        work[...] = own_ref[...] - update

    zero = jnp.zeros((half, half), jnp.float32)
    upper_ref[0:half, 0:half] = first_ref[...]
    upper_ref[0:half, half:] = across
    upper_ref[half:, 0:half] = zero
    inv_ref[0:half, 0:half] = first_inv_ref[...]
    inv_ref[0:half, half:] = zero
    between = dot_full(across, first_inv_ref[...], ((0,), (0,)))
    factor_into(work, right, upper_ref.at[half:, half:], inv_ref.at[half:, half:])
    inv_ref[half:, 0:half] = -dot_full(inv_ref[half:, half:], between)


def factor_first(place, own, other, after):
    half = own.shape[0]
    return pl.pallas_call(
        first_kernel,
        out_shape=[jax.ShapeDtypeStruct((half, half), jnp.float32)] * 2,
        in_specs=[pl.BlockSpec(memory_space=pltpu.SMEM)]
        + vmem(2)
        + [pl.BlockSpec(memory_space=pl.ANY)],
        out_specs=vmem(2),
        scratch_shapes=[pltpu.VMEM((half, half), jnp.float32)] * 2,
        compiler_params=pltpu.CompilerParams(vmem_limit_bytes=24 << 20),
        cost_estimate=pl.CostEstimate(flops=2 * half**3, bytes_accessed=1 << 24, transcendentals=half),
    )(place, own, other, after)


def factor_second(place, own, other, cross, first, first_inv):
    half = own.shape[0]
    return pl.pallas_call(
        second_kernel,
        out_shape=[jax.ShapeDtypeStruct((2 * half, 2 * half), jnp.float32)] * 2,
        in_specs=[pl.BlockSpec(memory_space=pltpu.SMEM)] + vmem(5),
        out_specs=vmem(2),
        scratch_shapes=[pltpu.VMEM((half, half), jnp.float32)] * 2,
        compiler_params=pltpu.CompilerParams(vmem_limit_bytes=24 << 20),
    )(place, own, other, cross, first, first_inv)


def finish_kernel(chunks, place_ref, own_ref, other_ref, cross_ref, first_ref, first_inv_ref, *refs):
    wides, highs, aways = refs[:chunks], refs[chunks : 2 * chunks], refs[2 * chunks : 3 * chunks]
    upper_ref, basis_ref, work, right, inverse, part, result, sems = refs[3 * chunks :]
    half, total = result.shape
    pieces = sems.shape[0]
    spans = [slice(i * (total // pieces), (i + 1) * (total // pieces)) for i in range(pieces)]
    leading = place_ref[0] == 0
    trailing = place_ref[0] != 0
    copies = [
        pltpu.make_async_copy(result.at[:, here], basis_ref.at[:, here], sems.at[i])
        for i, here in enumerate(spans)
    ]

    def dot(a, b):
        return jnp.dot(a, b, preferred_element_type=jnp.float32)

    def product(inverse, high, low):
        high_inv, low_inv = split(inverse)
        stacked = jnp.concatenate([high_inv, high_inv], axis=1)
        return dot(stacked, jnp.concatenate([high, low], axis=0)) + dot(low_inv, high)

    @pl.when(leading)
    def _():
        for copy, here in zip(copies, spans):
            high = stacked(highs, here)
            low = (stacked(wides, here) - high.astype(jnp.float32)).astype(jnp.bfloat16)
            result[:, here] = product(first_inv_ref[...], high, low)
            copy.start()

    lower = dot_full(cross_ref[...], first_inv_ref[...], ((1,), (1,)))
    rest = jnp.where(leading, other_ref[...], own_ref[...])
    work[...] = rest - dot_full(lower, lower, ((1,), (1,)))
    high_mix, low_mix = split(dot_full(lower, first_inv_ref[...]))
    mixes = jnp.concatenate([high_mix, low_mix], axis=1)
    for here in spans:
        away = stacked(aways, here)
        part[:, here] = stacked(wides, here) - dot(mixes, jnp.concatenate([away, away], axis=0))
    upper_ref[0:half, 0:half] = first_ref[...]
    upper_ref[0:half, half:] = lower.T
    upper_ref[half:, 0:half] = jnp.zeros((half, half), jnp.float32)
    factor_into(work, right, upper_ref.at[half:, half:], inverse)

    @pl.when(trailing)
    def _():
        for copy, here in zip(copies, spans):
            result[:, here] = product(inverse[...], *split(part[:, here]))
            copy.start()

    for copy in copies:
        copy.wait()


def finish(place, own, other, cross, first, first_inv, wide, high, away):
    half, total = own.shape[0], wide[0].shape[1]
    pieces = 4 if total % 512 == 0 else 1
    tile = pltpu.VMEM((half, half), jnp.float32)
    return pl.pallas_call(
        functools.partial(finish_kernel, len(wide)),
        out_shape=[
            jax.ShapeDtypeStruct((2 * half, 2 * half), jnp.float32),
            jax.ShapeDtypeStruct((half, total), jnp.float32),
        ],
        in_specs=[pl.BlockSpec(memory_space=pltpu.SMEM)] + vmem(5 + 3 * len(wide)),
        out_specs=vmem(1) + [pl.BlockSpec(memory_space=pl.ANY)],
        scratch_shapes=[tile] * 3
        + [pltpu.VMEM((half, total), jnp.float32)] * 2
        + [pltpu.SemaphoreType.DMA((pieces,))],
        compiler_params=pltpu.CompilerParams(vmem_limit_bytes=24 << 20),
    )(place, own, other, cross, first, first_inv, *wide, *high, *away)


def shards(hamiltonian, orbitals, adjacency):
    count = hamiltonian.shape[0]
    owned = orbitals.shape[0]
    blocks = lax.axis_size("space")
    groups = lax.axis_size("orb")
    half = owned * groups // 2
    chunks = 2
    share = owned // chunks
    odd = lax.axis_index("space").astype(jnp.int32).reshape(1) % 2
    loc = adjacency % count
    swapped = jnp.concatenate([loc[:, 1:2], loc[:, 0:1], loc[:, 2:]], axis=1)
    loc = jnp.where(odd[0] == 1, loc, swapped)
    near_pairs = [(i, i ^ 1) for i in range(blocks)]
    far_pairs = [(i, (i + 1 if i % 2 else i - 1) % blocks) for i in range(blocks)]
    smem = [pl.BlockSpec(memory_space=pltpu.SMEM)]

    def level(number, vec, prior, turned):
        far = lax.ppermute(vec, "space", far_pairs)
        near = lax.ppermute(vec, "space", near_pairs)
        acc = own_part(vec, turned, loc)
        return halo_part(number, near, far, acc, vec, prior, turned, loc)

    zero = [orbitals[piece * share : (piece + 1) * share] for piece in range(chunks)]
    fars = [lax.ppermute(vec, "space", far_pairs) for vec in zero]
    nears = [lax.ppermute(vec, "space", near_pairs) for vec in zero]
    turned, *accs = turn_part(zero, hamiltonian, loc, odd)
    one, two, filtered, narrow = [], [], [], []
    for base, near, far, acc in zip(zero, nears, fars, accs):
        one += halo_part(1, near, far, acc, base, base, turned, loc)
    for vec, prior in zip(one, zero):
        two += level(2, vec, prior, turned)
    for vec, prior in zip(two, one):
        wide, short = level(3, vec, prior, turned)
        filtered.append(wide)
        narrow.append(short)

    steps = [1 << i for i in range((blocks - 1).bit_length())]
    stages = [steps[:1]] + [steps[i : i + 2] for i in range(1, len(steps), 2)]

    def summed(part, chosen):
        def moved(step):
            return lax.ppermute(part, "space", [(i, i ^ step) for i in range(blocks)])

        for stage in chosen:
            if len(stage) == 1:
                part = part + moved(stage[0])
            else:
                one, two = stage
                part = (part + moved(one)) + (moved(two) + moved(one ^ two))
        return part

    place = lax.axis_index("orb").astype(jnp.int32).reshape(1)
    if groups == 2:
        swap = [(0, 1), (1, 0)]
        other = [lax.ppermute(piece, "orb", swap) for piece in narrow]
        tile = jax.ShapeDtypeStruct((half, half), jnp.float32)
        params = pltpu.CompilerParams(vmem_limit_bytes=24 << 20)
        near = pl.pallas_call(
            functools.partial(own_gram_kernel, chunks),
            out_shape=tile,
            in_specs=vmem(2 * chunks),
            out_specs=pl.BlockSpec(memory_space=pltpu.VMEM),
            compiler_params=params,
        )(*filtered, *narrow)
        near = summed(near, stages[:1])
        cross = pl.pallas_call(
            functools.partial(cross_gram_kernel, chunks),
            out_shape=tile,
            in_specs=smem + vmem(2 * chunks) + [pl.BlockSpec(memory_space=pl.ANY)],
            out_specs=pl.BlockSpec(memory_space=pltpu.VMEM),
            compiler_params=params,
        )(place, *narrow, *other, near)
        near = summed(near, stages[1:])
        far = lax.ppermute(near, "orb", swap)
        cross = summed(cross, stages[:-1])
        first, first_inv = factor_first(place, near, far, cross)
        cross = summed(cross, stages[-1:])
        upper, basis = finish(place, near, far, cross, first, first_inv, filtered, narrow, other)
    else:
        columns = lax.all_gather(jnp.concatenate(narrow), "orb", axis=0, tiled=True)
        whole = summed(dot_nt(columns, columns), stages)
        blocks_of = (jnp.zeros_like(place), whole[:half, :half], whole[half:, half:])
        first, first_inv = factor_first(*blocks_of, whole)
        upper, inverse = factor_second(*blocks_of, whole[:half, half:], first, first_inv)
        mine = lax.dynamic_slice_in_dim(inverse, place[0] * owned, owned, 0)
        near = lax.dynamic_slice_in_dim(mine, place[0] * owned, owned, 1)
        rest = jnp.concatenate(filtered) - jnp.concatenate(narrow).astype(jnp.float32)
        basis = dot_full(mine, columns.astype(jnp.float32)) + dot_full(near, rest)
    return (basis, upper)


def solution(mesh):
    in_specs = (P("space", None, None, None), P("orb", "space"), P("space", None))
    out_specs = (P("orb", "space"), P())
    return jax.shard_map(shards, mesh=mesh, in_specs=in_specs, out_specs=out_specs, check_vma=False)
```

```python
import functools

import jax
import jax.numpy as jnp
from jax import lax
from jax.experimental import pallas as pl
from jax.experimental.pallas import tpu as pltpu
from jax.sharding import PartitionSpec as P

centre = 0.25
radius = 0.75
SUB = 8


def vmem(count):
    return [pl.BlockSpec(memory_space=pltpu.VMEM)] * count


def dot_nt(a, b):
    return lax.dot_general(a, b, (((1,), (1,)), ((), ())), preferred_element_type=jnp.float32)


def dot_full(a, b, dims=((1,), (0,))):
    return lax.dot_general(
        a, b, (dims, ((), ())), precision=lax.Precision.HIGHEST, preferred_element_type=jnp.float32
    )


def split(a):
    high = a.astype(jnp.bfloat16)
    return high, (a - high.astype(jnp.float32)).astype(jnp.bfloat16)


def stacked(refs, here=slice(None)):
    return jnp.concatenate([ref[:, here] for ref in refs], axis=0)


def turn_kernel(chunks, loc_ref, odd_ref, *refs):
    vec_refs, ham_ref, turned_ref, outs = refs[:chunks], refs[chunks], refs[chunks + 1], refs[chunks + 2 : -2]
    buf, sems = refs[-2:]
    count, faces, width, _ = ham_ref.shape
    share = outs[0].shape[0]
    odd = odd_ref[0]
    copies = [pltpu.make_async_copy(ham_ref.at[e], buf.at[e], sems.at[e]) for e in range(count)]
    for copy in copies:
        copy.start()
    for e in range(count):
        copies[e].wait()
        here = slice(e * width, (e + 1) * width)
        total = None
        for face in range(faces):
            source = 2 - odd if face == 1 else 1 + odd if face == 2 else face
            turned = buf[e, source].T
            turned_ref[e, face] = turned
            if face == 1 or face == 2:
                continue
            at = here if face == 0 else pl.ds(pl.multiple_of(loc_ref[e, face - 1] * width, width), width)
            part = jnp.dot(stacked(vec_refs, at), turned, preferred_element_type=jnp.float32)
            total = part if total is None else total + part
        for piece, out in enumerate(outs):
            out[:, here] = total[piece * share : (piece + 1) * share]


def turn_part(vecs, hamiltonian, loc, odd):
    count, faces, width, _ = hamiltonian.shape
    chunks = len(vecs)
    return pl.pallas_call(
        functools.partial(turn_kernel, chunks),
        out_shape=[jax.ShapeDtypeStruct(hamiltonian.shape, hamiltonian.dtype)]
        + [jax.ShapeDtypeStruct(vec.shape, jnp.float32) for vec in vecs],
        in_specs=[pl.BlockSpec(memory_space=pltpu.SMEM)] * 2
        + vmem(chunks)
        + [pl.BlockSpec(memory_space=pl.ANY)],
        out_specs=vmem(1 + chunks),
        scratch_shapes=[
            pltpu.VMEM(hamiltonian.shape, hamiltonian.dtype),
            pltpu.SemaphoreType.DMA((count,)),
        ],
        compiler_params=pltpu.CompilerParams(vmem_limit_bytes=43 << 20),
        cost_estimate=pl.CostEstimate(
            flops=10 * chunks * vecs[0].shape[0] * count * width * width,
            bytes_accessed=count * faces * width * width * 4,
            transcendentals=0,
        ),
    )(loc, odd, *vecs, hamiltonian)


def own_kernel(loc_ref, vec_ref, turned_ref, out_ref):
    count, _, width, _ = turned_ref.shape
    for e in range(count):
        here = slice(e * width, (e + 1) * width)
        total = jnp.dot(vec_ref[:, here], turned_ref[e, 0], preferred_element_type=jnp.float32)
        for face in range(2, 6):
            at = pl.ds(pl.multiple_of(loc_ref[e, face] * width, width), width)
            total += jnp.dot(
                vec_ref[:, at], turned_ref[e, face + 1], preferred_element_type=jnp.float32
            )
        out_ref[:, here] = total


def own_part(vec, turned, loc):
    count, _, width, _ = turned.shape
    owned = vec.shape[0]
    return pl.pallas_call(
        own_kernel,
        out_shape=jax.ShapeDtypeStruct(vec.shape, jnp.float32),
        in_specs=[pl.BlockSpec(memory_space=pltpu.SMEM)] + vmem(2),
        out_specs=pl.BlockSpec(memory_space=pltpu.VMEM),
        compiler_params=pltpu.CompilerParams(vmem_limit_bytes=24 << 20),
        cost_estimate=pl.CostEstimate(
            flops=2 * owned * count * width * width * 5,
            bytes_accessed=count * 5 * width * width * 2,
            transcendentals=0,
        ),
    )(loc, vec, turned)


def halo_kernel(level, loc_ref, near_ref, far_ref, acc_ref, vec_ref, prior_ref, turned_ref, *outs):
    count, _, width, _ = turned_ref.shape
    for e in range(count):
        here = slice(e * width, (e + 1) * width)
        total = acc_ref[:, here]
        for face, ref in enumerate((near_ref, far_ref)):
            at = pl.ds(pl.multiple_of(loc_ref[e, face] * width, width), width)
            total += jnp.dot(
                ref[:, at], turned_ref[e, face + 1], preferred_element_type=jnp.float32
            )
        shifted = (total - centre * vec_ref[:, here].astype(jnp.float32)) * (1.0 / radius)
        if level > 1:
            shifted = 2.0 * shifted - prior_ref[:, here].astype(jnp.float32)
        for out in outs:
            out[:, here] = shifted.astype(out.dtype)


def halo_part(level, near, far, acc, vec, prior, turned, loc):
    count, _, width, _ = turned.shape
    owned = vec.shape[0]
    kinds = [jnp.bfloat16] if level < 3 else [jnp.float32, jnp.bfloat16]
    return pl.pallas_call(
        functools.partial(halo_kernel, level),
        out_shape=[jax.ShapeDtypeStruct(vec.shape, kind) for kind in kinds],
        in_specs=[pl.BlockSpec(memory_space=pltpu.SMEM)] + vmem(6),
        out_specs=vmem(len(kinds)),
        compiler_params=pltpu.CompilerParams(vmem_limit_bytes=24 << 20),
        cost_estimate=pl.CostEstimate(
            flops=2 * owned * count * width * width * 2,
            bytes_accessed=count * 2 * width * width * 2,
            transcendentals=0,
        ),
    )(loc, near, far, acc, vec, prior, turned)


def own_gram_kernel(chunks, *refs):
    own_refs, high_refs, out_ref = refs[:chunks], refs[chunks:-1], refs[-1]
    high = stacked(high_refs)
    low = (stacked(own_refs) - high.astype(jnp.float32)).astype(jnp.bfloat16)
    mixed = dot_nt(high, low)
    out_ref[...] = dot_nt(high, high) + (mixed + mixed.T)


def cross_gram_kernel(chunks, place_ref, *refs):
    own_refs, other_refs, out_ref = refs[:chunks], refs[chunks:-2], refs[-1]

    @pl.when(place_ref[0] == 0)
    def _():
        out_ref[...] = dot_nt(stacked(other_refs), stacked(own_refs))

    @pl.when(place_ref[0] != 0)
    def _():
        out_ref[...] = dot_nt(stacked(own_refs), stacked(other_refs))


def tree(terms):
    while len(terms) > 1:
        terms = [terms[i] + terms[i + 1] if i + 1 < len(terms) else terms[i] for i in range(0, len(terms), 2)]
    return terms[0]


def factor_block(rows, right):
    strips = len(rows)
    shape = rows[0].shape
    sub = lax.broadcasted_iota(jnp.int32, shape, 0)
    upper, inverse = [], []
    for k in range(strips):
        lanes = [
            jnp.broadcast_to(rows[k][:, k * SUB + j : k * SUB + j + 1], shape) for j in range(SUB)
        ]
        entry = [
            [jnp.broadcast_to(lanes[j][i : i + 1, :], shape) if j <= i else None for j in range(SUB)]
            for i in range(SUB)
        ]
        parts = [
            [jnp.broadcast_to(source[i : i + 1, :], shape) for i in range(SUB)]
            for source in (rows[k], right[k])
        ]
        pairs = []
        for p in range(0, SUB, 2):
            q = p + 1
            a, b, c = entry[p][p], entry[q][p], entry[q][q]
            det = a * c - b * b
            root = lax.rsqrt(det)
            over = root * root
            scaled = {}
            for i in range(q + 1, SUB):
                first = c * entry[i][p] - b * entry[i][q]
                second = a * entry[i][q] - b * entry[i][p]
                scaled[i] = (first * over, second * over)
                for t in range(q + 1, i + 1):
                    entry[i][t] = entry[i][t] - (first * entry[t][p] + second * entry[t][q]) * over
                for part in parts:
                    part[i] = part[i] - (scaled[i][0] * part[p] + scaled[i][1] * part[q])
            pairs.append((p, a, b, c, root, over, scaled))
        packed = [None, None]
        backs = []
        for at, part in enumerate(parts):
            back = [None] * SUB
            for p, a, b, c, root, over, scaled in reversed(pairs):
                q = p + 1
                one = (c * part[p] - b * part[q]) * over
                two = (a * part[q] - b * part[p]) * over
                if scaled:
                    one = one - tree([scaled[i][0] * back[i] for i in scaled])
                    two = two - tree([scaled[i][1] * back[i] for i in scaled])
                back[p], back[q] = one, two
            backs.append(back)
            for p, a, b, c, root, over, scaled in pairs:
                first_root = lax.rsqrt(a)
                high = part[p] * first_root
                low = (a * part[p + 1] - b * part[p]) * (first_root * root)
                packed[at] = high if packed[at] is None else jnp.where(sub == p, high, packed[at])
                packed[at] = jnp.where(sub == p + 1, low, packed[at])
        upper.append(packed[0])
        inverse.append(packed[1])
        for r in range(k + 1, strips):
            columns = [
                jnp.broadcast_to(rows[r][:, k * SUB + i : k * SUB + i + 1], shape) for i in range(SUB)
            ]
            rows[r] = rows[r] - tree([backs[0][i] * columns[i] for i in range(SUB)])
            right[r] = right[r] - tree([backs[1][i] * columns[i] for i in range(SUB)])
    return upper, inverse


def factor_into(work, right, upper_ref, inv_ref):
    half = work.shape[0]
    strips = half // SUB
    row = lax.broadcasted_iota(jnp.int32, (half, half), 0)
    col = lax.broadcasted_iota(jnp.int32, (half, half), 1)
    whole = work[...]
    diagonal = jnp.where(row == col, whole, 0.0)
    across = jnp.sum(diagonal, axis=0, keepdims=True)
    scale = lax.rsqrt(across)
    work[...] = whole * lax.rsqrt(jnp.sum(diagonal, axis=1, keepdims=True)) * scale
    rows = [work[SUB * s : SUB * (s + 1), :] for s in range(strips)]
    eye = (row == col).astype(jnp.float32)
    beside = [eye[SUB * s : SUB * (s + 1), :] for s in range(strips)]
    upper, inverse = factor_block(rows, beside)
    for s in range(strips):
        work[SUB * s : SUB * (s + 1), :] = upper[s]
        right[SUB * s : SUB * (s + 1), :] = inverse[s]
    upper_ref[...] = jnp.where(col >= row, work[...] * (across * scale), 0.0)
    inv_ref[...] = jnp.where(col <= row, right[...] * scale, 0.0)


def first_kernel(place_ref, own_ref, other_ref, after_ref, upper_ref, inv_ref, work, right):
    del after_ref

    @pl.when(place_ref[0] == 0)
    def _():
        work[...] = own_ref[...]

    @pl.when(place_ref[0] != 0)
    def _():
        work[...] = other_ref[...]

    factor_into(work, right, upper_ref, inv_ref)


def second_kernel(place_ref, own_ref, other_ref, cross_ref, first_ref, first_inv_ref, upper_ref, inv_ref, work, right):
    half = own_ref.shape[0]
    across = dot_full(first_inv_ref[...], cross_ref[...])
    update = dot_full(across, across, ((0,), (0,)))

    @pl.when(place_ref[0] == 0)
    def _():
        work[...] = other_ref[...] - update

    @pl.when(place_ref[0] != 0)
    def _():
        work[...] = own_ref[...] - update

    zero = jnp.zeros((half, half), jnp.float32)
    upper_ref[0:half, 0:half] = first_ref[...]
    upper_ref[0:half, half:] = across
    upper_ref[half:, 0:half] = zero
    inv_ref[0:half, 0:half] = first_inv_ref[...]
    inv_ref[0:half, half:] = zero
    between = dot_full(across, first_inv_ref[...], ((0,), (0,)))
    factor_into(work, right, upper_ref.at[half:, half:], inv_ref.at[half:, half:])
    inv_ref[half:, 0:half] = -dot_full(inv_ref[half:, half:], between)


def factor_first(place, own, other, after):
    half = own.shape[0]
    return pl.pallas_call(
        first_kernel,
        out_shape=[jax.ShapeDtypeStruct((half, half), jnp.float32)] * 2,
        in_specs=[pl.BlockSpec(memory_space=pltpu.SMEM)]
        + vmem(2)
        + [pl.BlockSpec(memory_space=pl.ANY)],
        out_specs=vmem(2),
        scratch_shapes=[pltpu.VMEM((half, half), jnp.float32)] * 2,
        compiler_params=pltpu.CompilerParams(vmem_limit_bytes=24 << 20),
        cost_estimate=pl.CostEstimate(flops=2 * half**3, bytes_accessed=1 << 24, transcendentals=half),
    )(place, own, other, after)


def factor_second(place, own, other, cross, first, first_inv):
    half = own.shape[0]
    return pl.pallas_call(
        second_kernel,
        out_shape=[jax.ShapeDtypeStruct((2 * half, 2 * half), jnp.float32)] * 2,
        in_specs=[pl.BlockSpec(memory_space=pltpu.SMEM)] + vmem(5),
        out_specs=vmem(2),
        scratch_shapes=[pltpu.VMEM((half, half), jnp.float32)] * 2,
        compiler_params=pltpu.CompilerParams(vmem_limit_bytes=24 << 20),
    )(place, own, other, cross, first, first_inv)


def finish_kernel(chunks, place_ref, own_ref, other_ref, cross_ref, first_ref, first_inv_ref, *refs):
    wides, highs, aways = refs[:chunks], refs[chunks : 2 * chunks], refs[2 * chunks : 3 * chunks]
    upper_ref, basis_ref, work, right, inverse, part, result, sems = refs[3 * chunks :]
    half, total = result.shape
    pieces = sems.shape[0]
    spans = [slice(i * (total // pieces), (i + 1) * (total // pieces)) for i in range(pieces)]
    leading = place_ref[0] == 0
    trailing = place_ref[0] != 0
    copies = [
        pltpu.make_async_copy(result.at[:, here], basis_ref.at[:, here], sems.at[i])
        for i, here in enumerate(spans)
    ]

    def dot(a, b):
        return jnp.dot(a, b, preferred_element_type=jnp.float32)

    def product(inverse, high, low):
        high_inv, low_inv = split(inverse)
        stacked = jnp.concatenate([high_inv, high_inv], axis=1)
        return dot(stacked, jnp.concatenate([high, low], axis=0)) + dot(low_inv, high)

    lower = dot_full(cross_ref[...], first_inv_ref[...], ((1,), (1,)))
    rest = jnp.where(leading, other_ref[...], own_ref[...])
    work[...] = rest - dot_full(lower, lower, ((1,), (1,)))
    high_mix, low_mix = split(dot_full(lower, first_inv_ref[...]))
    mixes = jnp.concatenate([high_mix, low_mix], axis=1)
    for here in spans:
        high = stacked(highs, here)
        low = (stacked(wides, here) - high.astype(jnp.float32)).astype(jnp.bfloat16)
        result[:, here] = product(first_inv_ref[...], high, low)
        away = stacked(aways, here)
        part[:, here] = stacked(wides, here) - dot(mixes, jnp.concatenate([away, away], axis=0))
    upper_ref[0:half, 0:half] = first_ref[...]
    upper_ref[0:half, half:] = lower.T
    upper_ref[half:, 0:half] = jnp.zeros((half, half), jnp.float32)
    factor_into(work, right, upper_ref.at[half:, half:], inverse)

    @pl.when(leading)
    def _():
        for copy in copies:
            copy.start()

    @pl.when(trailing)
    def _():
        for copy, here in zip(copies, spans):
            result[:, here] = product(inverse[...], *split(part[:, here]))
            copy.start()

    for copy in copies:
        copy.wait()


def finish(place, own, other, cross, first, first_inv, wide, high, away):
    half, total = own.shape[0], wide[0].shape[1]
    pieces = 4 if total % 512 == 0 else 1
    tile = pltpu.VMEM((half, half), jnp.float32)
    return pl.pallas_call(
        functools.partial(finish_kernel, len(wide)),
        out_shape=[
            jax.ShapeDtypeStruct((2 * half, 2 * half), jnp.float32),
            jax.ShapeDtypeStruct((half, total), jnp.float32),
        ],
        in_specs=[pl.BlockSpec(memory_space=pltpu.SMEM)] + vmem(5 + 3 * len(wide)),
        out_specs=vmem(1) + [pl.BlockSpec(memory_space=pl.ANY)],
        scratch_shapes=[tile] * 3
        + [pltpu.VMEM((half, total), jnp.float32)] * 2
        + [pltpu.SemaphoreType.DMA((pieces,))],
        compiler_params=pltpu.CompilerParams(vmem_limit_bytes=24 << 20),
    )(place, own, other, cross, first, first_inv, *wide, *high, *away)


def shards(hamiltonian, orbitals, adjacency):
    count = hamiltonian.shape[0]
    owned = orbitals.shape[0]
    blocks = lax.axis_size("space")
    groups = lax.axis_size("orb")
    half = owned * groups // 2
    chunks = 2
    share = owned // chunks
    odd = lax.axis_index("space").astype(jnp.int32).reshape(1) % 2
    loc = adjacency % count
    swapped = jnp.concatenate([loc[:, 1:2], loc[:, 0:1], loc[:, 2:]], axis=1)
    loc = jnp.where(odd[0] == 1, loc, swapped)
    near_pairs = [(i, i ^ 1) for i in range(blocks)]
    far_pairs = [(i, (i + 1 if i % 2 else i - 1) % blocks) for i in range(blocks)]
    smem = [pl.BlockSpec(memory_space=pltpu.SMEM)]

    def level(number, vec, prior, turned):
        far = lax.ppermute(vec, "space", far_pairs)
        near = lax.ppermute(vec, "space", near_pairs)
        acc = own_part(vec, turned, loc)
        return halo_part(number, near, far, acc, vec, prior, turned, loc)

    zero = [orbitals[piece * share : (piece + 1) * share] for piece in range(chunks)]
    fars = [lax.ppermute(vec, "space", far_pairs) for vec in zero]
    nears = [lax.ppermute(vec, "space", near_pairs) for vec in zero]
    turned, *accs = turn_part(zero, hamiltonian, loc, odd)
    one, two, filtered, narrow = [], [], [], []
    for base, near, far, acc in zip(zero, nears, fars, accs):
        one += halo_part(1, near, far, acc, base, base, turned, loc)
    for vec, prior in zip(one, zero):
        two += level(2, vec, prior, turned)
    for vec, prior in zip(two, one):
        wide, short = level(3, vec, prior, turned)
        filtered.append(wide)
        narrow.append(short)

    steps = [1 << i for i in range((blocks - 1).bit_length())]
    stages = [steps[:1]] + [steps[i : i + 2] for i in range(1, len(steps), 2)]

    def summed(part, chosen):
        def moved(step):
            return lax.ppermute(part, "space", [(i, i ^ step) for i in range(blocks)])

        for stage in chosen:
            if len(stage) == 1:
                part = part + moved(stage[0])
            else:
                one, two = stage
                part = (part + moved(one)) + (moved(two) + moved(one ^ two))
        return part

    place = lax.axis_index("orb").astype(jnp.int32).reshape(1)
    if groups == 2:
        swap = [(0, 1), (1, 0)]
        other = [lax.ppermute(piece, "orb", swap) for piece in narrow]
        tile = jax.ShapeDtypeStruct((half, half), jnp.float32)
        params = pltpu.CompilerParams(vmem_limit_bytes=24 << 20)
        near = pl.pallas_call(
            functools.partial(own_gram_kernel, chunks),
            out_shape=tile,
            in_specs=vmem(2 * chunks),
            out_specs=pl.BlockSpec(memory_space=pltpu.VMEM),
            compiler_params=params,
        )(*filtered, *narrow)
        near = summed(near, stages[:1])
        cross = pl.pallas_call(
            functools.partial(cross_gram_kernel, chunks),
            out_shape=tile,
            in_specs=smem + vmem(2 * chunks) + [pl.BlockSpec(memory_space=pl.ANY)],
            out_specs=pl.BlockSpec(memory_space=pltpu.VMEM),
            compiler_params=params,
        )(place, *narrow, *other, near)
        near = summed(near, stages[1:])
        far = lax.ppermute(near, "orb", swap)
        cross = summed(cross, stages[:-1])
        first, first_inv = factor_first(place, near, far, cross)
        cross = summed(cross, stages[-1:])
        upper, basis = finish(place, near, far, cross, first, first_inv, filtered, narrow, other)
    else:
        columns = lax.all_gather(jnp.concatenate(narrow), "orb", axis=0, tiled=True)
        whole = summed(dot_nt(columns, columns), stages)
        blocks_of = (jnp.zeros_like(place), whole[:half, :half], whole[half:, half:])
        first, first_inv = factor_first(*blocks_of, whole)
        upper, inverse = factor_second(*blocks_of, whole[:half, half:], first, first_inv)
        mine = lax.dynamic_slice_in_dim(inverse, place[0] * owned, owned, 0)
        near = lax.dynamic_slice_in_dim(mine, place[0] * owned, owned, 1)
        rest = jnp.concatenate(filtered) - jnp.concatenate(narrow).astype(jnp.float32)
        basis = dot_full(mine, columns.astype(jnp.float32)) + dot_full(near, rest)
    return (basis, upper)


def solution(mesh):
    in_specs = (P("space", None, None, None), P("orb", "space"), P("space", None))
    out_specs = (P("orb", "space"), P())
    return jax.shard_map(shards, mesh=mesh, in_specs=in_specs, out_specs=out_specs, check_vma=False)
```

```python
import functools

import jax
import jax.numpy as jnp
from jax import lax
from jax.experimental import pallas as pl
from jax.experimental.pallas import tpu as pltpu
from jax.sharding import PartitionSpec as P

centre = 0.25
radius = 0.75
SUB = 8


def vmem(count):
    return [pl.BlockSpec(memory_space=pltpu.VMEM)] * count


def dot_nt(a, b):
    return lax.dot_general(a, b, (((1,), (1,)), ((), ())), preferred_element_type=jnp.float32)


def dot_full(a, b, dims=((1,), (0,))):
    return lax.dot_general(
        a, b, (dims, ((), ())), precision=lax.Precision.HIGHEST, preferred_element_type=jnp.float32
    )


def split(a):
    high = a.astype(jnp.bfloat16)
    return high, (a - high.astype(jnp.float32)).astype(jnp.bfloat16)


def stacked(refs, here=slice(None)):
    return jnp.concatenate([ref[:, here] for ref in refs], axis=0)


def turn_kernel(chunks, loc_ref, odd_ref, *refs):
    vec_refs, ham_ref, turned_ref, outs = refs[:chunks], refs[chunks], refs[chunks + 1], refs[chunks + 2 : -2]
    buf, sems = refs[-2:]
    count, faces, width, _ = ham_ref.shape
    share = outs[0].shape[0]
    odd = odd_ref[0]
    copies = [pltpu.make_async_copy(ham_ref.at[e], buf.at[e], sems.at[e]) for e in range(count)]
    for copy in copies:
        copy.start()
    for e in range(count):
        copies[e].wait()
        here = slice(e * width, (e + 1) * width)
        total = None
        for face in range(faces):
            source = 2 - odd if face == 1 else 1 + odd if face == 2 else face
            turned = buf[e, source].T
            turned_ref[e, face] = turned
            if face == 1 or face == 2:
                continue
            at = here if face == 0 else pl.ds(pl.multiple_of(loc_ref[e, face - 1] * width, width), width)
            part = jnp.dot(stacked(vec_refs, at), turned, preferred_element_type=jnp.float32)
            total = part if total is None else total + part
        for piece, out in enumerate(outs):
            out[:, here] = total[piece * share : (piece + 1) * share]


def turn_part(vecs, hamiltonian, loc, odd):
    count, faces, width, _ = hamiltonian.shape
    chunks = len(vecs)
    return pl.pallas_call(
        functools.partial(turn_kernel, chunks),
        out_shape=[jax.ShapeDtypeStruct(hamiltonian.shape, hamiltonian.dtype)]
        + [jax.ShapeDtypeStruct(vec.shape, jnp.float32) for vec in vecs],
        in_specs=[pl.BlockSpec(memory_space=pltpu.SMEM)] * 2
        + vmem(chunks)
        + [pl.BlockSpec(memory_space=pl.ANY)],
        out_specs=vmem(1 + chunks),
        scratch_shapes=[
            pltpu.VMEM(hamiltonian.shape, hamiltonian.dtype),
            pltpu.SemaphoreType.DMA((count,)),
        ],
        compiler_params=pltpu.CompilerParams(vmem_limit_bytes=43 << 20),
        cost_estimate=pl.CostEstimate(
            flops=10 * chunks * vecs[0].shape[0] * count * width * width,
            bytes_accessed=count * faces * width * width * 4,
            transcendentals=0,
        ),
    )(loc, odd, *vecs, hamiltonian)


def own_kernel(loc_ref, vec_ref, turned_ref, out_ref):
    count, _, width, _ = turned_ref.shape
    for e in range(count):
        here = slice(e * width, (e + 1) * width)
        total = jnp.dot(vec_ref[:, here], turned_ref[e, 0], preferred_element_type=jnp.float32)
        for face in range(2, 6):
            at = pl.ds(pl.multiple_of(loc_ref[e, face] * width, width), width)
            total += jnp.dot(
                vec_ref[:, at], turned_ref[e, face + 1], preferred_element_type=jnp.float32
            )
        out_ref[:, here] = total


def own_part(vec, turned, loc):
    count, _, width, _ = turned.shape
    owned = vec.shape[0]
    return pl.pallas_call(
        own_kernel,
        out_shape=jax.ShapeDtypeStruct(vec.shape, jnp.float32),
        in_specs=[pl.BlockSpec(memory_space=pltpu.SMEM)] + vmem(2),
        out_specs=pl.BlockSpec(memory_space=pltpu.VMEM),
        compiler_params=pltpu.CompilerParams(vmem_limit_bytes=24 << 20),
        cost_estimate=pl.CostEstimate(
            flops=2 * owned * count * width * width * 5,
            bytes_accessed=count * 5 * width * width * 2,
            transcendentals=0,
        ),
    )(loc, vec, turned)


def halo_kernel(level, loc_ref, near_ref, far_ref, acc_ref, vec_ref, prior_ref, turned_ref, *outs):
    count, _, width, _ = turned_ref.shape
    for e in range(count):
        here = slice(e * width, (e + 1) * width)
        total = acc_ref[:, here]
        for face, ref in enumerate((near_ref, far_ref)):
            at = pl.ds(pl.multiple_of(loc_ref[e, face] * width, width), width)
            total += jnp.dot(
                ref[:, at], turned_ref[e, face + 1], preferred_element_type=jnp.float32
            )
        shifted = (total - centre * vec_ref[:, here].astype(jnp.float32)) * (1.0 / radius)
        if level > 1:
            shifted = 2.0 * shifted - prior_ref[:, here].astype(jnp.float32)
        for out in outs:
            out[:, here] = shifted.astype(out.dtype)


def halo_part(level, near, far, acc, vec, prior, turned, loc):
    count, _, width, _ = turned.shape
    owned = vec.shape[0]
    kinds = [jnp.bfloat16] if level < 3 else [jnp.float32, jnp.bfloat16]
    return pl.pallas_call(
        functools.partial(halo_kernel, level),
        out_shape=[jax.ShapeDtypeStruct(vec.shape, kind) for kind in kinds],
        in_specs=[pl.BlockSpec(memory_space=pltpu.SMEM)] + vmem(6),
        out_specs=vmem(len(kinds)),
        compiler_params=pltpu.CompilerParams(vmem_limit_bytes=24 << 20),
        cost_estimate=pl.CostEstimate(
            flops=2 * owned * count * width * width * 2,
            bytes_accessed=count * 2 * width * width * 2,
            transcendentals=0,
        ),
    )(loc, near, far, acc, vec, prior, turned)


def own_gram_kernel(chunks, *refs):
    own_refs, high_refs, out_ref = refs[:chunks], refs[chunks:-1], refs[-1]
    high = stacked(high_refs)
    low = (stacked(own_refs) - high.astype(jnp.float32)).astype(jnp.bfloat16)
    mixed = dot_nt(high, low)
    out_ref[...] = dot_nt(high, high) + (mixed + mixed.T)


def cross_gram_kernel(chunks, place_ref, *refs):
    own_refs, other_refs, out_ref = refs[:chunks], refs[chunks:-2], refs[-1]

    @pl.when(place_ref[0] == 0)
    def _():
        out_ref[...] = dot_nt(stacked(other_refs), stacked(own_refs))

    @pl.when(place_ref[0] != 0)
    def _():
        out_ref[...] = dot_nt(stacked(own_refs), stacked(other_refs))


def tree(terms):
    while len(terms) > 1:
        terms = [terms[i] + terms[i + 1] if i + 1 < len(terms) else terms[i] for i in range(0, len(terms), 2)]
    return terms[0]


def factor_block(rows, right):
    strips = len(rows)
    shape = rows[0].shape
    sub = lax.broadcasted_iota(jnp.int32, shape, 0)
    upper, inverse = [], []
    for k in range(strips):
        lanes = [
            jnp.broadcast_to(rows[k][:, k * SUB + j : k * SUB + j + 1], shape) for j in range(SUB)
        ]
        entry = [
            [jnp.broadcast_to(lanes[j][i : i + 1, :], shape) if j <= i else None for j in range(SUB)]
            for i in range(SUB)
        ]
        parts = [
            [jnp.broadcast_to(source[i : i + 1, :], shape) for i in range(SUB)]
            for source in (rows[k], right[k])
        ]
        pairs = []
        for p in range(0, SUB, 2):
            q = p + 1
            a, b, c = entry[p][p], entry[q][p], entry[q][q]
            det = a * c - b * b
            root = lax.rsqrt(det)
            over = root * root
            scaled = {}
            for i in range(q + 1, SUB):
                first = c * entry[i][p] - b * entry[i][q]
                second = a * entry[i][q] - b * entry[i][p]
                scaled[i] = (first * over, second * over)
                for t in range(q + 1, i + 1):
                    entry[i][t] = entry[i][t] - (first * entry[t][p] + second * entry[t][q]) * over
                for part in parts:
                    part[i] = part[i] - (scaled[i][0] * part[p] + scaled[i][1] * part[q])
            pairs.append((p, a, b, c, root, over, scaled))
        packed = [None, None]
        backs = []
        for at, part in enumerate(parts):
            back = [None] * SUB
            for p, a, b, c, root, over, scaled in reversed(pairs):
                q = p + 1
                one = (c * part[p] - b * part[q]) * over
                two = (a * part[q] - b * part[p]) * over
                if scaled:
                    one = one - tree([scaled[i][0] * back[i] for i in scaled])
                    two = two - tree([scaled[i][1] * back[i] for i in scaled])
                back[p], back[q] = one, two
            backs.append(back)
            for p, a, b, c, root, over, scaled in pairs:
                first_root = lax.rsqrt(a)
                high = part[p] * first_root
                low = (a * part[p + 1] - b * part[p]) * (first_root * root)
                packed[at] = high if packed[at] is None else jnp.where(sub == p, high, packed[at])
                packed[at] = jnp.where(sub == p + 1, low, packed[at])
        upper.append(packed[0])
        inverse.append(packed[1])
        for r in range(k + 1, strips):
            columns = [
                jnp.broadcast_to(rows[r][:, k * SUB + i : k * SUB + i + 1], shape) for i in range(SUB)
            ]
            rows[r] = rows[r] - tree([backs[0][i] * columns[i] for i in range(SUB)])
            right[r] = right[r] - tree([backs[1][i] * columns[i] for i in range(SUB)])
    return upper, inverse


def factor_into(work, right, upper_ref, inv_ref):
    half = work.shape[0]
    strips = half // SUB
    row = lax.broadcasted_iota(jnp.int32, (half, half), 0)
    col = lax.broadcasted_iota(jnp.int32, (half, half), 1)
    whole = work[...]
    diagonal = jnp.where(row == col, whole, 0.0)
    across = jnp.sum(diagonal, axis=0, keepdims=True)
    scale = lax.rsqrt(across)
    work[...] = whole * lax.rsqrt(jnp.sum(diagonal, axis=1, keepdims=True)) * scale
    rows = [work[SUB * s : SUB * (s + 1), :] for s in range(strips)]
    eye = (row == col).astype(jnp.float32)
    beside = [eye[SUB * s : SUB * (s + 1), :] for s in range(strips)]
    upper, inverse = factor_block(rows, beside)
    for s in range(strips):
        work[SUB * s : SUB * (s + 1), :] = upper[s]
        right[SUB * s : SUB * (s + 1), :] = inverse[s]
    upper_ref[...] = jnp.where(col >= row, work[...] * (across * scale), 0.0)
    inv_ref[...] = jnp.where(col <= row, right[...] * scale, 0.0)


def first_kernel(place_ref, own_ref, other_ref, after_ref, upper_ref, inv_ref, work, right):
    del after_ref

    @pl.when(place_ref[0] == 0)
    def _():
        work[...] = own_ref[...]

    @pl.when(place_ref[0] != 0)
    def _():
        work[...] = other_ref[...]

    factor_into(work, right, upper_ref, inv_ref)


def second_kernel(place_ref, own_ref, other_ref, cross_ref, first_ref, first_inv_ref, upper_ref, inv_ref, work, right):
    half = own_ref.shape[0]
    across = dot_full(first_inv_ref[...], cross_ref[...])
    update = dot_full(across, across, ((0,), (0,)))

    @pl.when(place_ref[0] == 0)
    def _():
        work[...] = other_ref[...] - update

    @pl.when(place_ref[0] != 0)
    def _():
        work[...] = own_ref[...] - update

    zero = jnp.zeros((half, half), jnp.float32)
    upper_ref[0:half, 0:half] = first_ref[...]
    upper_ref[0:half, half:] = across
    upper_ref[half:, 0:half] = zero
    inv_ref[0:half, 0:half] = first_inv_ref[...]
    inv_ref[0:half, half:] = zero
    between = dot_full(across, first_inv_ref[...], ((0,), (0,)))
    factor_into(work, right, upper_ref.at[half:, half:], inv_ref.at[half:, half:])
    inv_ref[half:, 0:half] = -dot_full(inv_ref[half:, half:], between)


def factor_first(place, own, other, after):
    half = own.shape[0]
    return pl.pallas_call(
        first_kernel,
        out_shape=[jax.ShapeDtypeStruct((half, half), jnp.float32)] * 2,
        in_specs=[pl.BlockSpec(memory_space=pltpu.SMEM)]
        + vmem(2)
        + [pl.BlockSpec(memory_space=pl.ANY)],
        out_specs=vmem(2),
        scratch_shapes=[pltpu.VMEM((half, half), jnp.float32)] * 2,
        compiler_params=pltpu.CompilerParams(vmem_limit_bytes=24 << 20),
        cost_estimate=pl.CostEstimate(flops=2 * half**3, bytes_accessed=1 << 24, transcendentals=half),
    )(place, own, other, after)


def factor_second(place, own, other, cross, first, first_inv):
    half = own.shape[0]
    return pl.pallas_call(
        second_kernel,
        out_shape=[jax.ShapeDtypeStruct((2 * half, 2 * half), jnp.float32)] * 2,
        in_specs=[pl.BlockSpec(memory_space=pltpu.SMEM)] + vmem(5),
        out_specs=vmem(2),
        scratch_shapes=[pltpu.VMEM((half, half), jnp.float32)] * 2,
        compiler_params=pltpu.CompilerParams(vmem_limit_bytes=24 << 20),
    )(place, own, other, cross, first, first_inv)


def finish_kernel(chunks, place_ref, own_ref, other_ref, cross_ref, first_ref, first_inv_ref, *refs):
    wides, highs, aways = refs[:chunks], refs[chunks : 2 * chunks], refs[2 * chunks : 3 * chunks]
    upper_ref, basis_ref, work, right, inverse, part, result, sems = refs[3 * chunks :]
    half, total = result.shape
    pieces = sems.shape[0]
    spans = [slice(i * (total // pieces), (i + 1) * (total // pieces)) for i in range(pieces)]
    leading = place_ref[0] == 0
    trailing = place_ref[0] != 0
    copies = [
        pltpu.make_async_copy(result.at[:, here], basis_ref.at[:, here], sems.at[i])
        for i, here in enumerate(spans)
    ]

    def dot(a, b):
        return jnp.dot(a, b, preferred_element_type=jnp.float32)

    def product(inverse, high, low):
        high_inv, low_inv = split(inverse)
        stacked = jnp.concatenate([high_inv, high_inv], axis=1)
        return dot(stacked, jnp.concatenate([high, low], axis=0)) + dot(low_inv, high)

    @pl.when(leading)
    def _():
        for copy, here in zip(copies, spans):
            high = stacked(highs, here)
            low = (stacked(wides, here) - high.astype(jnp.float32)).astype(jnp.bfloat16)
            result[:, here] = product(first_inv_ref[...], high, low)
            copy.start()

    lower = dot_full(cross_ref[...], first_inv_ref[...], ((1,), (1,)))
    rest = jnp.where(leading, other_ref[...], own_ref[...])
    work[...] = rest - dot_full(lower, lower, ((1,), (1,)))
    high_mix, low_mix = split(dot_full(lower, first_inv_ref[...]))
    mixes = jnp.concatenate([high_mix, low_mix], axis=1)
    for here in spans:
        away = stacked(aways, here)
        part[:, here] = stacked(wides, here) - dot(mixes, jnp.concatenate([away, away], axis=0))
    upper_ref[0:half, 0:half] = first_ref[...]
    upper_ref[0:half, half:] = lower.T
    upper_ref[half:, 0:half] = jnp.zeros((half, half), jnp.float32)
    factor_into(work, right, upper_ref.at[half:, half:], inverse)

    @pl.when(trailing)
    def _():
        for copy, here in zip(copies, spans):
            result[:, here] = product(inverse[...], *split(part[:, here]))
            copy.start()

    for copy in copies:
        copy.wait()


def finish(place, own, other, cross, first, first_inv, wide, high, away):
    half, total = own.shape[0], wide[0].shape[1]
    pieces = 4 if total % 512 == 0 else 1
    tile = pltpu.VMEM((half, half), jnp.float32)
    return pl.pallas_call(
        functools.partial(finish_kernel, len(wide)),
        out_shape=[
            jax.ShapeDtypeStruct((2 * half, 2 * half), jnp.float32),
            jax.ShapeDtypeStruct((half, total), jnp.float32),
        ],
        in_specs=[pl.BlockSpec(memory_space=pltpu.SMEM)] + vmem(5 + 3 * len(wide)),
        out_specs=vmem(1) + [pl.BlockSpec(memory_space=pl.ANY)],
        scratch_shapes=[tile] * 3
        + [pltpu.VMEM((half, total), jnp.float32)] * 2
        + [pltpu.SemaphoreType.DMA((pieces,))],
        compiler_params=pltpu.CompilerParams(vmem_limit_bytes=24 << 20),
    )(place, own, other, cross, first, first_inv, *wide, *high, *away)


def shards(hamiltonian, orbitals, adjacency):
    count = hamiltonian.shape[0]
    owned = orbitals.shape[0]
    blocks = lax.axis_size("space")
    groups = lax.axis_size("orb")
    half = owned * groups // 2
    chunks = 2
    share = owned // chunks
    odd = lax.axis_index("space").astype(jnp.int32).reshape(1) % 2
    loc = adjacency % count
    swapped = jnp.concatenate([loc[:, 1:2], loc[:, 0:1], loc[:, 2:]], axis=1)
    loc = jnp.where(odd[0] == 1, loc, swapped)
    near_pairs = [(i, i ^ 1) for i in range(blocks)]
    far_pairs = [(i, (i + 1 if i % 2 else i - 1) % blocks) for i in range(blocks)]
    smem = [pl.BlockSpec(memory_space=pltpu.SMEM)]

    def level(number, vec, prior, turned):
        far = lax.ppermute(vec, "space", far_pairs)
        near = lax.ppermute(vec, "space", near_pairs)
        acc = own_part(vec, turned, loc)
        return halo_part(number, near, far, acc, vec, prior, turned, loc)

    zero = [orbitals[piece * share : (piece + 1) * share] for piece in range(chunks)]
    fars = [lax.ppermute(vec, "space", far_pairs) for vec in zero]
    nears = [lax.ppermute(vec, "space", near_pairs) for vec in zero]
    turned, *accs = turn_part(zero, hamiltonian, loc, odd)
    one, two, filtered, narrow = [], [], [], []
    for base, near, far, acc in zip(zero, nears, fars, accs):
        one += halo_part(1, near, far, acc, base, base, turned, loc)
    for vec, prior in zip(one, zero):
        two += level(2, vec, prior, turned)
    for vec, prior in zip(two, one):
        wide, short = level(3, vec, prior, turned)
        filtered.append(wide)
        narrow.append(short)

    steps = [1 << i for i in range((blocks - 1).bit_length())]
    stages = [steps[:1]] + [steps[i : i + 2] for i in range(1, len(steps), 2)]

    def summed(part, chosen):
        def moved(step):
            return lax.ppermute(part, "space", [(i, i ^ step) for i in range(blocks)])

        for stage in chosen:
            if len(stage) == 1:
                part = part + moved(stage[0])
            else:
                one, two = stage
                part = (part + moved(one)) + (moved(two) + moved(one ^ two))
        return part

    place = lax.axis_index("orb").astype(jnp.int32).reshape(1)
    if groups == 2:
        swap = [(0, 1), (1, 0)]
        other = [lax.ppermute(piece, "orb", swap) for piece in narrow]
        tile = jax.ShapeDtypeStruct((half, half), jnp.float32)
        params = pltpu.CompilerParams(vmem_limit_bytes=24 << 20)
        near = pl.pallas_call(
            functools.partial(own_gram_kernel, chunks),
            out_shape=tile,
            in_specs=vmem(2 * chunks),
            out_specs=pl.BlockSpec(memory_space=pltpu.VMEM),
            compiler_params=params,
        )(*filtered, *narrow)
        near = summed(near, stages[:1])
        cross = pl.pallas_call(
            functools.partial(cross_gram_kernel, chunks),
            out_shape=tile,
            in_specs=smem + vmem(2 * chunks) + [pl.BlockSpec(memory_space=pl.ANY)],
            out_specs=pl.BlockSpec(memory_space=pltpu.VMEM),
            compiler_params=params,
        )(place, *narrow, *other, narrow[0])
        near = summed(near, stages[1:])
        far = lax.ppermute(near, "orb", swap)
        cross = summed(cross, stages[:-1])
        first, first_inv = factor_first(place, near, far, cross)
        cross = summed(cross, stages[-1:])
        upper, basis = finish(place, near, far, cross, first, first_inv, filtered, narrow, other)
    else:
        columns = lax.all_gather(jnp.concatenate(narrow), "orb", axis=0, tiled=True)
        whole = summed(dot_nt(columns, columns), stages)
        blocks_of = (jnp.zeros_like(place), whole[:half, :half], whole[half:, half:])
        first, first_inv = factor_first(*blocks_of, whole)
        upper, inverse = factor_second(*blocks_of, whole[:half, half:], first, first_inv)
        mine = lax.dynamic_slice_in_dim(inverse, place[0] * owned, owned, 0)
        near = lax.dynamic_slice_in_dim(mine, place[0] * owned, owned, 1)
        rest = jnp.concatenate(filtered) - jnp.concatenate(narrow).astype(jnp.float32)
        basis = dot_full(mine, columns.astype(jnp.float32)) + dot_full(near, rest)
    return (basis, upper)


def solution(mesh):
    in_specs = (P("space", None, None, None), P("orb", "space"), P("space", None))
    out_specs = (P("orb", "space"), P())
    return jax.shard_map(shards, mesh=mesh, in_specs=in_specs, out_specs=out_specs, check_vma=False)
```
